32 devices in a mesh: wide: 8 (over z, x), narrow: 4 (over y, core).
Axes of the slice: x: 2, y: 2, z: 4, core: 2. Of those that a mesh axis runs over, the one named last changes fastest.
Arguments:
- images: bfloat16 [16, 32, 32, 1024], P('wide', 'narrow'), may hold values from -6 to 6
- first_reduce: bfloat16 [1024, 512], replicated, may hold values from -0.1875 to 0.1875
- first_spatial: bfloat16 [3, 3, 512, 512], replicated, may hold values from -0.09375 to 0.09375
- first_expand: bfloat16 [512, 2048], replicated, may hold values from -0.25 to 0.25
- first_squeeze: bfloat16 [2048, 128], replicated, may hold values from -3 to 3
- first_excite: bfloat16 [128, 2048], replicated, may hold values from -2 to 2
- first_project: bfloat16 [1024, 2048], replicated, may hold values from -0.1875 to 0.1875
- second_reduce: bfloat16 [2048, 512], replicated, may hold values from -0.125 to 0.125
- second_spatial: bfloat16 [3, 3, 512, 512], replicated, may hold values from -0.09375 to 0.09375
- second_expand: bfloat16 [512, 2048], replicated, may hold values from -0.25 to 0.25
- second_squeeze: bfloat16 [2048, 128], replicated, may hold values from -3 to 3
- second_excite: bfloat16 [128, 2048], replicated, may hold values from -2 to 2
- norm_gains: float32 [8192], replicated, may hold values from 0.25 to 1.75
- norm_shifts: float32 [8192], replicated, may hold values from -3 to 3
- image_counts: int32 [8], P('wide'), may hold values from 1 to 2, as said below
- out_grad: bfloat16 [16, 16, 16, 2048], P('wide', 'narrow'), may hold values from -6 to 6
Outputs:
- mixed: bfloat16 [16, 16, 16, 2048], P('wide', 'narrow')
- image_grad: bfloat16 [16, 32, 32, 1024], P('wide', 'narrow')
- first_block_grads: float32 [6553600], P(('wide', 'narrow'))
- second_block_grads: float32 [4980736], P(('wide', 'narrow'))
- gain_grad: float32 [8192], replicated
- shift_grad: float32 [8192], replicated
The draws below stay inside these ranges and needn't reach their ends.
Inputs may be any that keep to these rules, and one draw needn't show every extreme that they name: Slot i of the 2 slots of wide index d holds an image when i < image_counts[d]; other slots hold data that no output reads. Some index holds 2 images in every draw.
All inputs are finite; a program needn't handle non-finite values.
Results may differ from the reference program's by a relative error of at most 0.018.
The reference program's roundings to bfloat16 on the way count: a program that leaves them out, or rounds other values in their place, can miss the bound.
Values may be sent and summed in bfloat16 or wider, within the bound.
No kernel may reach another device: no remote copies, remote signals or barrier semaphores. Data moves between devices by JAX's collectives and lax.ppermute only.
A program may use at most 256 MiB of HBM per device.

```python
import jax
import jax.numpy as jnp
from jax import lax

CIN = 1024
MID = 512
COUT = 2048
SQZ = 128
HT = 32
WD = 32
IMG_DEV = 2
IMAGES = 16
NORM = 8192
FIRST_SLICE = 204800
SECOND_SLICE = 155648
N_WIDE = 8
N_NARROW = 4


def draw_image_counts(key, part):
    key = jax.random.fold_in(key, 5)
    first_key, second_key = jax.random.split(key)
    counts = jax.random.randint(first_key, (N_WIDE,), 1, IMG_DEV + 1)
    fullest = jax.random.randint(second_key, (), 0, N_WIDE)
    return jnp.where(jnp.arange(N_WIDE) == fullest, IMG_DEV, counts).astype(jnp.int32)


def level_of(key, dims, cuts, least, largest):
    factor_of = 1.0
    for axis_at, blocks in cuts:
        steps = jax.random.uniform(jax.random.fold_in(jax.random.fold_in(key, 6), axis_at), (blocks,), jnp.float32, least / len(cuts), largest / len(cuts))
        factor_of = factor_of * jnp.repeat(jnp.exp(steps), dims[axis_at] // blocks).reshape((-1,) + (1,) * (len(dims) - 1 - axis_at))
    return factor_of


def gaussian(rng, extent, width, reach, cuts=(), held_as=jnp.bfloat16):
    factor_of = level_of(rng, extent, cuts, -0.22, 0.18) if cuts else 1.0
    values = jax.random.normal(rng, extent, jnp.float32) * width * factor_of
    return jnp.minimum(jnp.maximum(values, -reach), reach).astype(held_as)


def setup_inputs(seed: int = 0) -> dict:
    key_of = jax.random.split(jax.random.key(seed), 17)
    images = gaussian(key_of[0], (IMAGES, HT, WD, CIN), 1.0, 6.0, ((0, 8), (1, 4)))
    first_reduce = gaussian(key_of[1], (CIN, MID), CIN ** -0.5, 0.1875)
    first_spatial = gaussian(key_of[2], (3, 3, MID, MID), (9 * MID) ** -0.5, 0.09375)
    first_expand = gaussian(key_of[3], (MID, COUT), MID ** -0.5, 0.25)
    first_squeeze = gaussian(key_of[4], (COUT, SQZ), (max(COUT // 512, 1)) ** -0.5, 3.0)
    first_excite = gaussian(key_of[5], (SQZ, COUT), (max(SQZ // 16, 1)) ** -0.5, 2.0)
    first_project = gaussian(key_of[6], (CIN, COUT), CIN ** -0.5, 0.1875)
    second_reduce = gaussian(key_of[7], (COUT, MID), COUT ** -0.5, 0.125)
    second_spatial = gaussian(key_of[8], (3, 3, MID, MID), (9 * MID) ** -0.5, 0.09375)
    second_expand = gaussian(key_of[9], (MID, COUT), MID ** -0.5, 0.25)
    second_squeeze = gaussian(key_of[10], (COUT, SQZ), (max(COUT // 512, 1)) ** -0.5, 3.0)
    second_excite = gaussian(key_of[11], (SQZ, COUT), (max(SQZ // 16, 1)) ** -0.5, 2.0)
    norm_gains = jnp.clip(1.0 + 0.15 * jax.random.normal(key_of[12], (NORM,), jnp.float32), 0.25, 1.75)
    norm_shifts = gaussian(key_of[13], (NORM,), 0.3, 3.0, (), jnp.float32)
    image_counts = draw_image_counts(jax.random.fold_in(key_of[16], 71), 0)
    out_grad = gaussian(key_of[15], (IMAGES, HT // 2, WD // 2, COUT), 1.0, 6.0, ((0, 8), (1, 4)))
    return {"images": images, "first_reduce": first_reduce, "first_spatial": first_spatial, "first_expand": first_expand, "first_squeeze": first_squeeze, "first_excite": first_excite, "first_project": first_project, "second_reduce": second_reduce, "second_spatial": second_spatial, "second_expand": second_expand, "second_squeeze": second_squeeze, "second_excite": second_excite, "norm_gains": norm_gains, "norm_shifts": norm_shifts, "image_counts": image_counts, "out_grad": out_grad}


@jax.custom_vjp
def low(v):
    return lax.optimization_barrier(v.astype(jnp.bfloat16)).astype(jnp.float32)

@jax.custom_vjp
def low_back(v):
    return v

def low_keep(v):
    return (low(v), None)

def low_pass(kept, grad):
    return (grad,)

def back_keep(v):
    return (v, None)

def back_low(kept, grad):
    return (low(grad),)
low.defvjp(low_keep, low_pass)
low_back.defvjp(back_keep, back_low)
epsilon = 1e-05
highest = lax.Precision.HIGHEST
layout_spec = ('NHWC', 'HWIO', 'NHWC')

def spatial(values, kernel, stride):
    return lax.conv_general_dilated(values, kernel, (stride, stride), ((1, 1), (1, 1)), dimension_numbers=layout_spec, precision=highest)

def project(values, weight):
    return jnp.einsum('nhwi,io->nhwo', values, weight, precision=highest)

def normalize(hidden, gain, shift, valid_map):
    pixel_total = jnp.sum(valid_map) * (hidden.shape[1] * hidden.shape[2])
    average = lax.optimization_barrier(jnp.sum(hidden * valid_map, axis=(0, 1, 2))) / pixel_total
    centred = hidden - average
    spread = lax.optimization_barrier(jnp.sum(centred * centred * valid_map, axis=(0, 1, 2))) / pixel_total
    return centred * lax.rsqrt(spread + epsilon) * gain + shift

def excite(normed, squeeze_weight, excite_weight):
    pooled = lax.optimization_barrier(jnp.mean(normed, axis=(1, 2)))
    squeezed = jax.nn.silu(jnp.dot(pooled, squeeze_weight, precision=highest))
    return jax.nn.sigmoid(jnp.dot(squeezed, excite_weight, precision=highest))[:, None, None, :]

def forward(images, first_reduce, first_spatial, first_expand, first_squeeze, first_excite, first_project, second_reduce, second_spatial, second_expand, second_squeeze, second_excite, norm_gains, norm_shifts, valid_map):
    mid_width = first_reduce.shape[1]
    out_width = first_expand.shape[1]
    bounds = [0, mid_width, 2 * mid_width, 2 * mid_width + out_width, 2 * mid_width + 2 * out_width, 3 * mid_width + 2 * out_width, 4 * mid_width + 2 * out_width, 4 * mid_width + 3 * out_width]

    def batch_norm(hidden, number):
        return normalize(hidden, norm_gains[bounds[number]:bounds[number + 1]], norm_shifts[bounds[number]:bounds[number + 1]], valid_map)
    reduced_one = low_back(project(images, first_reduce))
    active_a = low(jax.nn.silu(batch_norm(reduced_one, 0)))
    spatial_one = low_back(spatial(active_a, first_spatial, 2))
    active_b = low(jax.nn.silu(batch_norm(spatial_one, 1)))
    expanded_one = low_back(project(active_b, first_expand))
    branch_one = batch_norm(expanded_one, 2)
    shortcut = low_back(project(images[:, ::2, ::2], first_project))
    block_out = low(jax.nn.silu(branch_one * excite(branch_one, first_squeeze, first_excite) + batch_norm(shortcut, 3)))
    reduced_two = low_back(project(block_out, second_reduce))
    active_d = low(jax.nn.silu(batch_norm(reduced_two, 4)))
    spatial_two = low_back(spatial(active_d, second_spatial, 1))
    active_e = low(jax.nn.silu(batch_norm(spatial_two, 5)))
    expanded_two = low_back(project(active_e, second_expand))
    branch_two = batch_norm(expanded_two, 6)
    summed_two = branch_two * excite(branch_two, second_squeeze, second_excite) + block_out
    return jax.nn.silu(summed_two) * valid_map

def flat_padded(grad_list, total_length):
    flattened = jnp.concatenate([element.reshape(-1) for element in grad_list])
    return jnp.pad(flattened, (0, total_length - flattened.shape[0]))

def reference(images, first_reduce, first_spatial, first_expand, first_squeeze, first_excite, first_project, second_reduce, second_spatial, second_expand, second_squeeze, second_excite, norm_gains, norm_shifts, image_counts, out_grad):
    slot_index = jnp.arange(IMAGES, dtype=jnp.int32)
    owners = jnp.repeat(image_counts, IMG_DEV)
    valid_map = (slot_index % IMG_DEV < owners).astype(jnp.float32)[:, None, None, None]
    inputs = [item_value.astype(jnp.float32) for item_value in (images, first_reduce, first_spatial, first_expand, first_squeeze, first_excite, first_project, second_reduce, second_spatial, second_expand, second_squeeze, second_excite, norm_gains, norm_shifts)]

    def network(*values):
        return forward(*values, valid_map)
    result, pullback = jax.vjp(network, *inputs)
    grads = pullback(out_grad.astype(jnp.float32))
    device_total = N_WIDE * N_NARROW
    first_flat = flat_padded(list(grads[1:7]), device_total * FIRST_SLICE)
    second_flat = flat_padded(list(grads[7:12]), device_total * SECOND_SLICE)
    return (result.astype(jnp.bfloat16), grads[0].astype(jnp.bfloat16), first_flat, second_flat, grads[12], grads[13])
```

```python
import jax
import jax.numpy as jnp
from jax import lax
from jax.sharding import PartitionSpec as P

epsilon = 1e-05
highest = lax.Precision.HIGHEST
layout_spec = ("NHWC", "HWIO", "NHWC")


def passed_along(shard, axis, by):
    peers = lax.axis_size(axis)
    pairs = [(i, i + by) for i in range(peers) if 0 <= i + by < peers]
    return lax.ppermute(shard, axis, pairs)


def with_halo(block, sides, width):
    for axis, dim in sides:
        count = lax.axis_size(axis)
        forward = [(i, i + 1) for i in range(count - 1)]
        backward = [(target, source) for source, target in forward]
        low = lax.ppermute(
            lax.slice_in_dim(block, block.shape[dim] - width, None, axis=dim), axis, forward
        )
        high = lax.ppermute(lax.slice_in_dim(block, 0, width, axis=dim), axis, backward)
        block = jnp.concatenate([low, block, high], axis=dim)
    return block


def silu_slope(values):
    logistic = jax.nn.sigmoid(values)
    return logistic * (1.0 + values * (1.0 - logistic))


def channel_sum(values):
    return jnp.sum(values, axis=(0, 1, 2))


def gathered(vector):
    peers = lax.axis_size("wide") * lax.axis_size("narrow")
    copies = jnp.broadcast_to(vector[None], (peers,) + vector.shape)
    return lax.all_to_all(copies, ("wide", "narrow"), 0, 0, tiled=True)


def swapped(shard, axis, bits):
    peers = lax.axis_size(axis)
    return lax.ppermute(shard, axis, [(i, i ^ bits) for i in range(peers)])


def stages(axis):
    peers = lax.axis_size(axis)
    assert peers & (peers - 1) == 0
    steps, bit = [], 1
    if (peers.bit_length() - 1) % 2:
        steps.append((1,))
        bit = 2
    while bit < peers:
        steps.append((bit, 2 * bit, 3 * bit))
        bit *= 4
    return steps


def narrow_sum(values):
    bit = 1
    while bit < lax.axis_size("narrow"):
        values = values + swapped(values, "narrow", bit)
        bit *= 2
    return values


def wide_sum(values):
    for step in stages("wide"):
        parts = [swapped(values, "wide", bits) for bits in step]
        for part in parts:
            values = values + part
    return values


def merged(groups):
    total = sum(group[0] for group in groups)
    summed = sum(group[1] for group in groups)
    average = summed / total
    spread = sum(
        group[2] + group[0] * jnp.square(group[1] / group[0] - average) for group in groups
    )
    return (total, summed, spread)


def local_moments(hidden, valid_map):
    pixels = jnp.sum(valid_map) * (hidden.shape[1] * hidden.shape[2])
    summed = channel_sum(hidden * valid_map)
    centred = hidden - summed / pixels
    return (pixels, summed, channel_sum(centred * centred * valid_map))


def finished(hidden, total, average, spread):
    inverse = lax.rsqrt(spread / total + epsilon)
    return ((hidden - average) * inverse, inverse, total, average)


def moments(hidden, valid_map):
    pixels, summed, spread = local_moments(hidden, valid_map)
    width = summed.shape[0]
    payload = jnp.concatenate([summed, spread, jnp.full((128,), pixels)])
    everyone = gathered(payload)
    counts = everyone[:, 2 * width :][:, :1]
    sums = everyone[:, :width]
    total = jnp.sum(counts)
    average = jnp.sum(sums, axis=0) / total
    between = jnp.sum(counts * jnp.square(sums / counts - average), axis=0)
    return finished(hidden, total, average, jnp.sum(everyone[:, width : 2 * width], axis=0) + between)


def split_group(payload, width):
    return (payload[2 * width], payload[:width], payload[width : 2 * width])


def joined_group(group):
    return jnp.concatenate([group[1], group[2], jnp.full((128,), group[0])])


def wide_merged(group):
    width = group[1].shape[0]
    for step in stages("wide"):
        payload = joined_group(group)
        group = merged(
            [group] + [split_group(swapped(payload, "wide", bits), width) for bits in step]
        )
    return group


def wide_moments(hidden, valid_map, others=()):
    images, width = hidden.shape[0], hidden.shape[-1]
    mask = valid_map[:, 0, 0, :]
    image_sums = jnp.sum(hidden, axis=(1, 2))
    group = local_moments(hidden, valid_map)
    other_groups = [local_moments(other, valid_map) for other in others]
    bit = 1
    while bit < lax.axis_size("narrow"):
        payload = jnp.concatenate(
            [image_sums.reshape(-1), group[2]]
            + [part for other in other_groups for part in other[1:]]
        )
        received = swapped(payload, "narrow", bit)
        theirs_images = received[: images * width].reshape(images, width)
        at = images * width
        theirs = (group[0], jnp.sum(theirs_images * mask, axis=0), received[at : at + width])
        at += width
        group = merged([group, theirs])
        image_sums = image_sums + theirs_images
        next_groups = []
        for other in other_groups:
            size = other[1].shape[0]
            theirs = (other[0], received[at : at + size], received[at + size : at + 2 * size])
            at += 2 * size
            next_groups.append(merged([other, theirs]))
        other_groups = next_groups
        bit *= 2
    whole = [group] + other_groups
    stacked = wide_merged(
        (
            group[0],
            jnp.concatenate([one[1] for one in whole]),
            jnp.concatenate([one[2] for one in whole]),
        )
    )
    total, summed, spread = stacked
    average = summed / total
    results, at = [], 0
    for one in (hidden,) + tuple(others):
        size = one.shape[-1]
        results.append(finished(one, total, average[at : at + size], spread[at : at + size]))
        at += size
    return results, image_sums


def norm_result(upstream, normed, inverse, gain, pixel_total, valid_map, shift_part, gain_part):
    result = gain * inverse * (upstream - (shift_part + normed * gain_part) / pixel_total)
    return (result * valid_map, gain_part, shift_part)


def norm_back(upstream, normed, inverse, gain, pixel_total, valid_map):
    masked = upstream * valid_map
    width = gain.shape[0]
    parts = jnp.concatenate([channel_sum(masked), channel_sum(masked * normed)])
    summed = jnp.sum(gathered(parts), axis=0)
    return norm_result(
        upstream, normed, inverse, gain, pixel_total, valid_map, summed[:width], summed[width:]
    )


def excite(image_sums, inverse, average, gain, shift, area, squeeze_weight, excite_weight):
    image_means = (image_sums / area - average) * inverse
    pooled = image_means * gain + shift
    reduced = jnp.dot(pooled, squeeze_weight.astype(jnp.float32), precision=highest)
    squeezed = jax.nn.silu(reduced)
    gate_value = jax.nn.sigmoid(
        jnp.dot(squeezed, excite_weight.astype(jnp.float32), precision=highest)
    )
    return (image_means, pooled, reduced, squeezed, gate_value)


def excite_back(
    upstream, normed, gain, shift, saved, squeeze_weight, excite_weight, valid_map, area, others=()
):
    image_means, pooled, reduced, squeezed, gate_value = saved
    images, width = gate_value.shape
    share = 1.0 / lax.axis_size("narrow")
    mask = valid_map[:, 0, 0, :]
    payload = jnp.concatenate(
        [
            jnp.sum(upstream, axis=(1, 2)).reshape(-1),
            jnp.sum(upstream * normed, axis=(1, 2)).reshape(-1),
        ]
        + [channel_sum(upstream * valid_map * other) for other in others]
    )
    payload = narrow_sum(payload)
    plain = payload[: images * width].reshape(images, width)
    crossed = payload[images * width : 2 * images * width].reshape(images, width)
    gate_grad = gain * crossed + shift * plain
    before_gate = gate_grad * gate_value * (1.0 - gate_value)
    excite_grad = jnp.dot(squeezed.T, before_gate, precision=highest) * share
    squeezed_grad = jnp.dot(before_gate, excite_weight.astype(jnp.float32).T, precision=highest)
    reduced_grad = squeezed_grad * silu_slope(reduced)
    squeeze_grad = jnp.dot(pooled.T, reduced_grad, precision=highest) * share
    pooled_grad = jnp.dot(reduced_grad, squeeze_weight.astype(jnp.float32).T, precision=highest)
    shift_part = jnp.sum(mask * (plain * gate_value + pooled_grad), axis=0)
    gain_part = jnp.sum(mask * (crossed * gate_value + pooled_grad * image_means), axis=0)
    sums = [shift_part, gain_part]
    if others:
        sums.append(jnp.sum(mask * plain, axis=0))
        sums.append(payload[2 * images * width :])
    summed = wide_sum(jnp.concatenate(sums))
    normed_grad = upstream * gate_value[:, None, None, :] + pooled_grad[:, None, None, :] / area
    return normed_grad, squeeze_grad, excite_grad, summed.reshape(len(sums), width)


def project(values, weight):
    return jnp.einsum("nhwi,io->nhwo", values, weight, preferred_element_type=jnp.float32)


def project_back(values, weight, upstream_low):
    input_grad = jnp.einsum(
        "nhwo,io->nhwi", upstream_low, weight, preferred_element_type=jnp.float32
    )
    weight_grad = jnp.einsum(
        "nhwi,nhwo->io", values, upstream_low, preferred_element_type=jnp.float32
    )
    return (input_grad, weight_grad)


def spatial_forward(padded, kernel, stride):
    return lax.conv_general_dilated(
        padded,
        kernel,
        (stride, stride),
        "VALID",
        dimension_numbers=layout_spec,
        preferred_element_type=jnp.float32,
    )


def spatial_back(upstream_low, padded, kernel, stride):
    rows_out = upstream_low.shape[1]
    cols_out = upstream_low.shape[2]
    tap_count = kernel.shape[0]
    flipped = jnp.flip(kernel, (0, 1)).transpose(0, 1, 3, 2)
    row_spare = padded.shape[1] - (rows_out - 1) * stride - tap_count
    col_spare = padded.shape[2] - (cols_out - 1) * stride - tap_count
    padded_grad = lax.conv_general_dilated(
        upstream_low,
        flipped,
        (1, 1),
        ((tap_count - 1, tap_count - 1 + row_spare), (tap_count - 1, tap_count - 1 + col_spare)),
        lhs_dilation=(stride, stride),
        dimension_numbers=layout_spec,
        preferred_element_type=jnp.float32,
    )
    row_list = []
    for tap_row in range(tap_count):
        col_list = []
        for tap_col in range(tap_count):
            window = padded[
                :,
                tap_row : tap_row + (rows_out - 1) * stride + 1 : stride,
                tap_col : tap_col + (cols_out - 1) * stride + 1 : stride,
            ]
            col_list.append(
                jnp.einsum(
                    "nhwi,nhwo->io", window, upstream_low, preferred_element_type=jnp.float32
                )
            )
        row_list.append(jnp.stack(col_list))
    return (padded_grad, jnp.stack(row_list))


def flatten(grad_list):
    rows = [element.astype(jnp.bfloat16).reshape(-1, 512) for element in grad_list]
    flattened = jnp.concatenate(rows, axis=0)
    devices = lax.axis_size("wide") * lax.axis_size("narrow")
    flattened = jnp.pad(flattened, ((0, -flattened.shape[0] % devices), (0, 0)))
    return lax.psum_scatter(
        flattened, ("wide", "narrow"), scatter_dimension=0, tiled=True
    ).astype(jnp.float32).reshape(-1)


def on_device(
    images,
    first_reduce,
    first_spatial,
    first_expand,
    first_squeeze,
    first_excite,
    first_project,
    second_reduce,
    second_spatial,
    second_expand,
    second_squeeze,
    second_excite,
    norm_gains,
    norm_shifts,
    image_counts,
    out_grad,
):
    slot_index = lax.iota(jnp.int32, images.shape[0])
    valid_map = (slot_index < image_counts[0]).astype(jnp.float32)[:, None, None, None]
    mid_width = first_reduce.shape[1]
    out_width = first_expand.shape[1]
    bounds = [
        0,
        mid_width,
        2 * mid_width,
        2 * mid_width + out_width,
        2 * mid_width + 2 * out_width,
        3 * mid_width + 2 * out_width,
        4 * mid_width + 2 * out_width,
        4 * mid_width + 3 * out_width,
    ]
    gains = [norm_gains[bounds[number] : bounds[number + 1]] for number in range(7)]
    shifts = [norm_shifts[bounds[number] : bounds[number + 1]] for number in range(7)]
    column_pad = ((0, 0), (0, 0), (1, 1), (0, 0))
    reduced_one = project(images, first_reduce)
    normed_a, inverse_a, pixels_a, _ = moments(reduced_one, valid_map)
    before_a = normed_a * gains[0] + shifts[0]
    active_a = jax.nn.silu(before_a).astype(jnp.bfloat16)
    above_row = passed_along(active_a[:, -1:], "narrow", 1)
    padded_a = jnp.pad(jnp.concatenate([above_row, active_a], axis=1), column_pad)
    spatial_one = spatial_forward(padded_a, first_spatial, 2)
    normed_b, inverse_b, pixels_b, _ = moments(spatial_one, valid_map)
    before_b = normed_b * gains[1] + shifts[1]
    active_b = jax.nn.silu(before_b).astype(jnp.bfloat16)
    expanded_one = project(active_b, first_expand)
    strided = images[:, ::2, ::2]
    shortcut = project(strided, first_project)
    results, image_sums_one = wide_moments(expanded_one, valid_map, (shortcut,))
    (normed_c, inverse_c, pixels_c, average_c), (normed_p, inverse_p, pixels_p, _) = results
    branch_one = normed_c * gains[2] + shifts[2]
    area = expanded_one.shape[1] * lax.axis_size("narrow") * expanded_one.shape[2]
    saved_one = excite(
        image_sums_one, inverse_c, average_c, gains[2], shifts[2], area, first_squeeze, first_excite
    )
    summed_one = branch_one * saved_one[4][:, None, None, :] + normed_p * gains[3] + shifts[3]
    block_out = jax.nn.silu(summed_one).astype(jnp.bfloat16)
    reduced_two = project(block_out, second_reduce)
    normed_d, inverse_d, pixels_d, _ = moments(reduced_two, valid_map)
    before_d = normed_d * gains[4] + shifts[4]
    active_d = jax.nn.silu(before_d).astype(jnp.bfloat16)
    beside_all = with_halo(active_d, (("narrow", 1),), 1)
    padded_d = jnp.pad(beside_all, column_pad)
    spatial_two = spatial_forward(padded_d, second_spatial, 1)
    normed_e, inverse_e, pixels_e, _ = moments(spatial_two, valid_map)
    before_e = normed_e * gains[5] + shifts[5]
    active_e = jax.nn.silu(before_e).astype(jnp.bfloat16)
    expanded_two = project(active_e, second_expand)
    results, image_sums_two = wide_moments(expanded_two, valid_map)
    normed_f, inverse_f, pixels_f, average_f = results[0]
    branch_two = normed_f * gains[6] + shifts[6]
    saved_two = excite(
        image_sums_two, inverse_f, average_f, gains[6], shifts[6], area, second_squeeze, second_excite
    )
    summed_two = branch_two * saved_two[4][:, None, None, :] + block_out.astype(jnp.float32)
    mixed = (jax.nn.silu(summed_two) * valid_map).astype(jnp.bfloat16)
    summed_grad_two = out_grad.astype(jnp.float32) * valid_map * silu_slope(summed_two)
    branch_grad_two, squeeze_grad_two, excite_grad_two, sums_two = excite_back(
        summed_grad_two,
        normed_f,
        gains[6],
        shifts[6],
        saved_two,
        second_squeeze,
        second_excite,
        valid_map,
        area,
    )
    expanded_grad_two, gain_f, shift_f = norm_result(
        branch_grad_two, normed_f, inverse_f, gains[6], pixels_f, valid_map, sums_two[0], sums_two[1]
    )
    active_grad_e, expand_grad_two = project_back(
        active_e, second_expand, expanded_grad_two.astype(jnp.bfloat16)
    )
    spatial_grad_two, gain_e, shift_e = norm_back(
        active_grad_e * silu_slope(before_e), normed_e, inverse_e, gains[5], pixels_e, valid_map
    )
    padded_grad_d, spatial_weight_two = spatial_back(
        spatial_grad_two.astype(jnp.bfloat16), padded_d, second_spatial, 1
    )
    inner_d = padded_grad_d[:, 1:-1, 1:-1]
    rim_grads = jnp.concatenate([padded_grad_d[:, :1, 1:-1], padded_grad_d[:, -1:, 1:-1]], axis=1)
    returned = with_halo(rim_grads, (("narrow", 1),), 1)
    active_grad_d = inner_d.at[:, 0].add(returned[:, 0]).at[:, -1].add(returned[:, -1])
    reduced_grad_two, gain_d, shift_d = norm_back(
        active_grad_d * silu_slope(before_d), normed_d, inverse_d, gains[4], pixels_d, valid_map
    )
    block_grad_part, reduce_grad_two = project_back(
        block_out, second_reduce, reduced_grad_two.astype(jnp.bfloat16)
    )
    block_grad = summed_grad_two + block_grad_part
    second_done = flatten(
        [reduce_grad_two, spatial_weight_two, expand_grad_two, squeeze_grad_two, excite_grad_two]
    )
    summed_grad_one = block_grad * silu_slope(summed_one)
    branch_grad_one, squeeze_grad_one, excite_grad_one, sums_one = excite_back(
        summed_grad_one,
        normed_c,
        gains[2],
        shifts[2],
        saved_one,
        first_squeeze,
        first_excite,
        valid_map,
        area,
        (normed_p,),
    )
    shortcut_grad, gain_p, shift_p = norm_result(
        summed_grad_one, normed_p, inverse_p, gains[3], pixels_p, valid_map, sums_one[2], sums_one[3]
    )
    strided_grad, project_grad = project_back(
        strided, first_project, shortcut_grad.astype(jnp.bfloat16)
    )
    expanded_grad_one, gain_c, shift_c = norm_result(
        branch_grad_one, normed_c, inverse_c, gains[2], pixels_c, valid_map, sums_one[0], sums_one[1]
    )
    active_grad_b, expand_grad_one = project_back(
        active_b, first_expand, expanded_grad_one.astype(jnp.bfloat16)
    )
    spatial_grad_one, gain_b, shift_b = norm_back(
        active_grad_b * silu_slope(before_b), normed_b, inverse_b, gains[1], pixels_b, valid_map
    )
    padded_grad_a, spatial_weight_one = spatial_back(
        spatial_grad_one.astype(jnp.bfloat16), padded_a, first_spatial, 2
    )
    below_grad = passed_along(padded_grad_a[:, :1, 1:-1], "narrow", -1)
    active_grad_a = padded_grad_a[:, 1:, 1:-1].at[:, -1:].add(below_grad)
    reduced_grad_one, gain_a, shift_a = norm_back(
        active_grad_a * silu_slope(before_a), normed_a, inverse_a, gains[0], pixels_a, valid_map
    )
    image_grad_part, reduce_grad_one = project_back(
        images, first_reduce, reduced_grad_one.astype(jnp.bfloat16)
    )
    count_here, rows_in, cols_in, channels_in = images.shape
    spread_grad = (
        image_grad_part.reshape(count_here, rows_in // 2, 2, cols_in // 2, 2, channels_in)
        .at[:, :, 0, :, 0]
        .add(strided_grad)
    )
    image_grad = spread_grad.reshape(images.shape).astype(jnp.bfloat16)
    first_done = flatten(
        [
            reduce_grad_one,
            spatial_weight_one,
            expand_grad_one,
            squeeze_grad_one,
            excite_grad_one,
            project_grad,
        ]
    )
    gain_grad = jnp.concatenate([gain_a, gain_b, gain_c, gain_p, gain_d, gain_e, gain_f])
    shift_grad = jnp.concatenate([shift_a, shift_b, shift_c, shift_p, shift_d, shift_e, shift_f])
    return (mixed, image_grad, first_done, second_done, gain_grad, shift_grad)


def solution(mesh):
    in_specs = (
        P("wide", "narrow", None, None),
        P(),
        P(),
        P(),
        P(),
        P(),
        P(),
        P(),
        P(),
        P(),
        P(),
        P(),
        P(),
        P(),
        P("wide"),
        P("wide", "narrow", None, None),
    )
    out_specs = (
        P("wide", "narrow", None, None),
        P("wide", "narrow", None, None),
        P(("wide", "narrow")),
        P(("wide", "narrow")),
        P(),
        P(),
    )
    return jax.shard_map(
        on_device, mesh=mesh, in_specs=in_specs, out_specs=out_specs, check_vma=False
    )
```

```python
import functools

import jax
import jax.numpy as jnp
from jax import lax
from jax.experimental import pallas as pl
from jax.experimental.pallas import tpu as pltpu
from jax.sharding import PartitionSpec as P

epsilon = 1e-05
highest = lax.Precision.HIGHEST
f32 = jnp.float32
bf16 = jnp.bfloat16
everywhere = ("wide", "narrow")


def iota_rows(rows, columns=1):
    return lax.broadcasted_iota(jnp.int32, (rows, columns), 0)


def dot(left, right, left_dim=1, right_dim=0):
    return lax.dot_general(
        left, right, (((left_dim,), (right_dim,)), ((), ())), preferred_element_type=f32
    )


def exact_dot(values, weight, weight_dim=0):
    first = values.astype(bf16)
    rest = values - first.astype(f32)
    second = rest.astype(bf16)
    third = (rest - second.astype(f32)).astype(bf16)
    rows = values.shape[0]
    product = dot(
        jnp.concatenate([first.astype(f32), second.astype(f32), third.astype(f32)], 0).astype(bf16),
        weight,
        1,
        weight_dim,
    )
    return product[:rows] + product[rows : 2 * rows] + product[2 * rows : 3 * rows]


def slope(values):
    logistic = jax.nn.sigmoid(values)
    return logistic * (1.0 + values * (1.0 - logistic))


def silu(values):
    return values * jax.nn.sigmoid(values)


def total_of(values):
    return jnp.sum(values, axis=0, keepdims=True)


def mask_of(info, rows, plane, images):
    per_image = plane // images
    index = iota_rows(rows)
    if rows > plane:
        index = jnp.bitwise_and(index, plane - 1)
    return (index < info[0] * per_image).astype(f32)


def images_of(info, images):
    return jnp.minimum(info[0], images).astype(f32)


def local_moments(hidden, mask, pixels):
    summed = total_of(hidden * mask)
    centred = (hidden - summed / pixels) * mask
    return summed, total_of(centred * centred)


def put_pair(out, first, second):
    peers = out.shape[0]
    chunks = first.shape[1] // 128
    for number, row in enumerate((first, second)):
        for chunk in range(chunks):
            part = row[:, chunk * 128 : chunk * 128 + 128]
            out[:, number * chunks + chunk, :] = jnp.broadcast_to(part, (peers, 128))


def gathered_moments(pairs, counts, chunks):
    total = total_of(counts)
    averages, inverses = [], []
    for chunk in range(chunks):
        sums = pairs[:, chunk, :]
        spread = total_of(pairs[:, chunks + chunk, :])
        average = total_of(sums) / total
        spread = spread + total_of(counts * jnp.square(sums / counts - average))
        averages.append(average)
        inverses.append(lax.rsqrt(spread / total + epsilon))
    return jnp.concatenate(averages, 1), jnp.concatenate(inverses, 1), total[:, :1]


def gathered_sums(pairs, chunks):
    rows = [total_of(pairs[:, chunk, :]) for chunk in range(2 * chunks)]
    return jnp.concatenate(rows[:chunks], 1), jnp.concatenate(rows[chunks:], 1)


def merge(groups):
    total = sum(group[0] for group in groups)
    summed = sum(group[1] for group in groups)
    average = summed / total
    spread = sum(group[2] + group[0] * jnp.square(group[1] / group[0] - average) for group in groups)
    return total, summed, spread


def norm_back(upstream, normed, inverse, gain, total, shift_part, gain_part, mask):
    return mask * (gain * inverse) * (upstream - (shift_part + normed * gain_part) / total)


def shifted(values, by, columns):
    rows = values.shape[0]
    column = jnp.bitwise_and(iota_rows(rows), columns - 1)
    edge = 0 if by == 1 else columns - 1
    return jnp.where(column == edge, 0.0, pltpu.roll(values, by % rows, 0))


def put_halves(mine_out, theirs_out, values, width, info):
    first, second = [], []
    for start in range(0, values.shape[1], width):
        first.append(values[:, start : start + width // 2])
        second.append(values[:, start + width // 2 : start + width])
    first, second = jnp.concatenate(first, 1), jnp.concatenate(second, 1)
    low = jnp.right_shift(info[1], 1) == 0
    mine_out[...] = jnp.where(low, first, second).astype(bf16)
    theirs_out[...] = jnp.where(low, second, first).astype(bf16)


def stack_rows(parts):
    return jnp.concatenate(parts, axis=0)


def plane_order(pixels, images, rows, columns):
    plane = images * rows * columns
    index = iota_rows(4 * plane, 4 * plane)
    other = lax.broadcasted_iota(jnp.int32, (4 * plane, 4 * plane), 1)
    parity = index // plane
    within = index - parity * plane
    line = within // columns
    column = within - line * columns
    natural = (line * 2 + parity // 2) * (2 * columns) + 2 * column + (parity & 1)
    return (other == natural).astype(bf16)


def reduce_first(geometry, info, x, weight, planes_out, hidden_out, pair_out, edge_out):
    images, rows, columns = geometry
    plane = images * rows * columns
    order = plane_order(4 * plane, images, rows, columns)
    planes = dot(order, x[...]).astype(bf16)
    planes_out[...] = planes
    hidden = dot(planes, weight[...])
    hidden_out[...] = hidden
    mask = mask_of(info, 4 * plane, plane, images)
    pixels = images_of(info, images) * (4 * rows * columns)
    summed, spread = local_moments(hidden, mask, pixels)
    put_pair(pair_out, summed, spread)
    chunks = hidden.shape[1] // 128
    pair_out[:, 2 * chunks, :] = jnp.full((pair_out.shape[0], 128), pixels, f32)
    per_image = rows * columns
    edges = []
    for parity in range(2):
        for image in range(images):
            end = (2 + parity) * plane + (image + 1) * per_image
            edges.append(hidden[end - columns : end])
    edge_out[...] = stack_rows(edges)


def project_first(geometry, info, planes, weight, hidden_out, moments_out):
    images, rows, columns = geometry
    plane = images * rows * columns
    hidden = dot(planes[:plane], weight[...])
    hidden_out[...] = hidden
    mask = mask_of(info, plane, plane, images)
    pixels = images_of(info, images) * (rows * columns)
    summed, spread = local_moments(hidden, mask, pixels)
    moments_out[0:1] = summed
    moments_out[1:2] = spread
    moments_out[2:8] = jnp.zeros((6, hidden.shape[1]), f32)


def spatial_first(
    geometry,
    info,
    hidden,
    halo,
    pairs,
    gain,
    shift,
    weight,
    windows_out,
    moved_out,
    moments_out,
    counts_out,
    pair_out,
    edge_out,
):
    images, rows, columns = geometry
    plane = images * rows * columns
    per_image = rows * columns
    width = hidden.shape[1]
    chunks = width // 128
    counts = pairs[:, 2 * chunks, :]
    counts_out[...] = counts
    average, inverse, total = gathered_moments(pairs, counts, chunks)
    moments_out[0:1] = average
    moments_out[1:2] = inverse
    moments_out[2:3] = jnp.broadcast_to(total, (1, width))
    moments_out[3:8] = jnp.zeros((5, width), f32)

    def active(values):
        return silu((values - average) * inverse * gain[...] + shift[...])

    inside = jnp.where(info[1] > 0, 1.0, 0.0)
    above = active(halo[...]) * inside
    planes = [active(hidden[number * plane : (number + 1) * plane]) for number in range(4)]

    def lifted(parity):
        parts = []
        for image in range(images):
            at = (parity * images + image) * columns
            parts.append(above[at : at + columns])
            start = image * per_image
            parts.append(planes[2 + parity][start : start + per_image - columns])
        return stack_rows(parts)

    by_row = [(lifted(0), lifted(1)), (planes[0], planes[1]), (planes[2], planes[3])]
    moved = jnp.zeros((plane, width), f32)
    for tap_row in range(3):
        even, odd = by_row[tap_row]
        for tap_column, window in enumerate((shifted(odd, 1, columns), even, odd)):
            tap = 3 * tap_row + tap_column
            window = window.astype(bf16)
            windows_out[tap] = window
            moved = moved + dot(window, weight[tap])
    moved_out[...] = moved
    mask = mask_of(info, plane, plane, images)
    pixels = images_of(info, images) * per_image
    put_pair(pair_out, *local_moments(moved, mask, pixels))
    edge_out[...] = stack_rows(
        [moved[image * per_image : image * per_image + columns] for image in range(images)]
    )


def expand(geometry, info, hidden, pairs, counts, gain, shift, weight, others, active_out, hidden_out, moments_out, state_out):
    images, rows, columns = geometry
    plane = images * rows * columns
    per_image = rows * columns
    width = hidden.shape[1]
    average, inverse, total = gathered_moments(pairs, counts[...] * (per_image / (4 * per_image)), width // 128)
    moments_out[0:1] = average
    moments_out[1:2] = inverse
    moments_out[2:3] = jnp.broadcast_to(total, (1, width))
    moments_out[3:8] = jnp.zeros((5, width), f32)
    active = silu((hidden[...] - average) * inverse * gain[...] + shift[...]).astype(bf16)
    active_out[...] = active
    wide = dot(active, weight[...])
    hidden_out[...] = wide
    mask = mask_of(info, plane, plane, images)
    pixels = images_of(info, images) * per_image
    summed, spread = local_moments(wide, mask, pixels)
    for image in range(images):
        state_out[image : image + 1] = total_of(wide[image * per_image : (image + 1) * per_image])
    state_out[images : images + 1] = summed
    state_out[images + 1 : images + 2] = spread
    if others is None:
        state_out[images + 2 : images + 4] = jnp.zeros((2, wide.shape[1]), f32)
    else:
        state_out[images + 2 : images + 4] = others[0:2]
    state_out[images + 4 : images + 5] = jnp.full((1, wide.shape[1]), pixels, f32)
    if state_out.shape[0] > images + 5:
        state_out[images + 5 :] = jnp.zeros((state_out.shape[0] - images - 5, wide.shape[1]), f32)


def expand_packing(geometry, info, *refs):
    *refs, pack_out = refs
    block, middle, *refs = refs
    expand(geometry, info, *refs[:6], None, *refs[6:])
    at = 0
    for one in (block, middle, refs[6].held):
        part = one[...]
        pack_out[:, at : at + part.shape[1]] = part
        at += part.shape[1]


def groups_of(states, images, at):
    return [
        (state[images + 4 : images + 5], state[at : at + 1], state[at + 1 : at + 2]) for state in states
    ]


def merge_states(images, adders, *refs):
    *states, out = refs
    image_sums = states[0][0:images]
    for adder in adders:
        image_sums = image_sums + states[adder][0:images]
    out[0:images] = image_sums
    total, summed, spread = merge(groups_of(states, images, images))
    out[images : images + 1] = summed
    out[images + 1 : images + 2] = spread
    _, summed, spread = merge(groups_of(states, images, images + 2))
    out[images + 2 : images + 3] = summed
    out[images + 3 : images + 4] = spread
    out[images + 4 : images + 5] = total
    if out.shape[0] > images + 5:
        out[images + 5 :] = states[0][images + 5 :]


def excited(image_sums, area, average, inverse, gain, shift, squeeze, excite):
    image_means = (image_sums / area - average) * inverse
    pooled = image_means * gain + shift
    reduced = exact_dot(pooled, squeeze)
    squeezed = silu(reduced)
    gate = jax.nn.sigmoid(exact_dot(squeezed, excite))
    return image_means, pooled, reduced, squeezed, gate


def wide_spread(values, per_image):
    return stack_rows(
        [
            jnp.broadcast_to(values[image : image + 1], (per_image, values.shape[1]))
            for image in range(values.shape[0])
        ]
    )


def finish_state(states, images, at):
    total, summed, spread = merge(groups_of(states, images, at))
    average = summed / total
    return average, lax.rsqrt(spread / total + epsilon), total


def put_gates(gates_out, reduced_out, image_means, pooled, gate, reduced, squeezed):
    images = gate.shape[0]
    gates_out[0:images] = image_means
    gates_out[images : 2 * images] = pooled
    gates_out[2 * images : 3 * images] = gate
    reduced_out[0:images] = reduced
    reduced_out[images : 2 * images] = squeezed


def reduce_second(
    geometry,
    peers,
    area,
    info,
    hidden,
    shortcut,
    gain,
    shift,
    gain_p,
    shift_p,
    squeeze,
    excite,
    weight,
    *rest,
):
    images, rows, columns = geometry
    plane = images * rows * columns
    per_image = rows * columns
    states = rest[:peers]
    moments_out, gates_out, reduced_out, summed_out, block_out, moved_out, pair_out, first_out, last_out = rest[peers:]
    average, inverse, total = finish_state(states, images, images)
    average_p, inverse_p, _ = finish_state(states, images, images + 2)
    for row, value in enumerate((average, inverse, total, average_p, inverse_p)):
        moments_out[row : row + 1] = value
    moments_out[5:8] = jnp.zeros((3, average.shape[1]), f32)
    image_means, pooled, reduced, squeezed, gate = excited(
        states[0][0:images], area, average, inverse, gain[...], shift[...], squeeze[...], excite[...]
    )
    put_gates(gates_out, reduced_out, image_means, pooled, gate, reduced, squeezed)
    branch = (hidden[...] - average) * inverse * gain[...] + shift[...]
    summed = (
        branch * wide_spread(gate, per_image)
        + (shortcut[...] - average_p) * inverse_p * gain_p[...]
        + shift_p[...]
    )
    summed_out[...] = summed
    block = silu(summed).astype(bf16)
    block_out[...] = block
    moved = dot(block, weight[...])
    moved_out[...] = moved
    mask = mask_of(info, plane, plane, images)
    pixels = images_of(info, images) * per_image
    put_pair(pair_out, *local_moments(moved, mask, pixels))
    put_edges(first_out, last_out, moved, images, per_image, columns)


def put_edges(first_out, last_out, values, images, per_image, columns):
    first_out[...] = stack_rows(
        [values[image * per_image : image * per_image + columns] for image in range(images)]
    )
    last_out[...] = stack_rows(
        [values[(image + 1) * per_image - columns : (image + 1) * per_image] for image in range(images)]
    )


def extended(values, above, below, images, per_image, columns):
    parts = []
    for image in range(images):
        parts.append(above[image * columns : (image + 1) * columns])
        parts.append(values[image * per_image : (image + 1) * per_image])
        parts.append(below[image * columns : (image + 1) * columns])
    return stack_rows(parts)


def window_of(values, lift, images, per_image, columns):
    span = per_image + 2 * columns
    return stack_rows(
        [
            values[image * span + lift * columns : image * span + lift * columns + per_image]
            for image in range(images)
        ]
    )


def spatial_second(
    geometry,
    last,
    info,
    hidden,
    above,
    below,
    pairs,
    counts,
    gain,
    shift,
    weight,
    active_out,
    moved_out,
    moments_out,
    pair_out,
    first_out,
    last_out,
):
    images, rows, columns = geometry
    plane = images * rows * columns
    per_image = rows * columns
    width = hidden.shape[1]
    average, inverse, total = gathered_moments(pairs, counts[...] * 0.25, width // 128)
    moments_out[0:1] = average
    moments_out[1:2] = inverse
    moments_out[2:3] = jnp.broadcast_to(total, (1, width))
    moments_out[3:8] = jnp.zeros((5, width), f32)

    def active(values):
        return silu((values - average) * inverse * gain[...] + shift[...])

    top = active(above[...]) * jnp.where(info[1] > 0, 1.0, 0.0)
    bottom = active(below[...]) * jnp.where(info[1] < last, 1.0, 0.0)
    middle = active(hidden[...])
    active_out[...] = middle.astype(bf16)
    middle = extended(middle, top, bottom, images, per_image, columns)
    by_column = (shifted(middle, 1, columns), middle, shifted(middle, -1, columns))
    moved = jnp.zeros((plane, width), f32)
    for tap_column in range(3):
        for tap_row in range(3):
            tap = 3 * tap_row + tap_column
            window = window_of(by_column[tap_column], tap_row, images, per_image, columns).astype(bf16)
            moved = moved + dot(window, weight[tap])
    moved_out[...] = moved
    mask = mask_of(info, plane, plane, images)
    pixels = images_of(info, images) * per_image
    put_pair(pair_out, *local_moments(moved, mask, pixels))
    put_edges(first_out, last_out, moved, images, per_image, columns)


def finish_second(
    geometry,
    peers,
    area,
    info,
    hidden,
    block,
    out_grad,
    gain,
    shift,
    squeeze,
    excite,
    *rest,
):
    images, rows, columns = geometry
    plane = images * rows * columns
    per_image = rows * columns
    states = rest[:peers]
    moments_out, gates_out, reduced_out, mixed_out, grad_out, state_out = rest[peers:]
    average, inverse, total = finish_state(states, images, images)
    for row, value in enumerate((average, inverse, total)):
        moments_out[row : row + 1] = value
    moments_out[3:8] = jnp.zeros((5, average.shape[1]), f32)
    image_means, pooled, reduced, squeezed, gate = excited(
        states[0][0:images], area, average, inverse, gain[...], shift[...], squeeze[...], excite[...]
    )
    put_gates(gates_out, reduced_out, image_means, pooled, gate, reduced, squeezed)
    normed = (hidden[...] - average) * inverse
    summed = (normed * gain[...] + shift[...]) * wide_spread(gate, per_image) + block[...].astype(f32)
    mask = mask_of(info, plane, plane, images)
    logistic = jax.nn.sigmoid(summed)
    mixed_out[...] = (summed * logistic * mask).astype(bf16)
    grad = out_grad[...].astype(f32) * mask * (logistic * (1.0 + summed * (1.0 - logistic)))
    grad_out[...] = grad
    put_image_sums(state_out, grad, normed, images, per_image)
    state_out[2 * images :] = jnp.zeros((state_out.shape[0] - 2 * images, grad.shape[1]), f32)


def put_image_sums(state_out, grad, normed, images, per_image):
    crossed = grad * normed
    for image in range(images):
        part = slice(image * per_image, (image + 1) * per_image)
        state_out[image : image + 1] = total_of(grad[part])
        state_out[images + image : images + image + 1] = total_of(crossed[part])


def excite_back(images, area, has_others, info, gain, shift, gates, reduced, squeeze, excite, mine, theirs, sums_out, pooled_grad_out, gate_grad_out, reduced_grad_out):
    state = mine[...] + theirs[...]
    plain = state[0:images]
    crossed = state[images : 2 * images]
    image_means = gates[0:images]
    gate = gates[2 * images : 3 * images]
    gate_grad = gain[...] * crossed + shift[...] * plain
    before_gate = gate_grad * gate * (1.0 - gate)
    squeezed_grad = exact_dot(before_gate, excite[...], 1)
    reduced_grad = squeezed_grad * slope(reduced[0:images])
    pooled_grad = exact_dot(reduced_grad, squeeze[...], 1)
    pooled_grad_out[...] = pooled_grad / area
    gate_grad_out[...] = before_gate
    reduced_grad_out[...] = reduced_grad
    mask = (iota_rows(images) < info[0]).astype(f32)
    sums_out[0:1] = total_of(mask * (plain * gate + pooled_grad))
    sums_out[1:2] = total_of(mask * (crossed * gate + pooled_grad * image_means))
    if has_others:
        sums_out[2:3] = total_of(mask * plain)
        sums_out[3:4] = state[2 * images : 2 * images + 1]
    else:
        sums_out[2:4] = jnp.zeros((2, plain.shape[1]), f32)


def expand_back(
    geometry,
    peers,
    cut,
    info,
    grad,
    hidden,
    moments,
    gates,
    pooled_grad,
    gain,
    weight,
    middle,
    middle_moments,
    middle_gain,
    middle_shift,
    *rest,
):
    images, rows, columns = geometry
    plane = images * rows * columns
    per_image = rows * columns
    sums = rest[0][...]
    for other in rest[1:peers]:
        sums = sums + other[...]
    sums_out, mine_out, *rest = rest[peers:]
    theirs_out = rest.pop(0) if cut else None
    middle_grad_out, pair_out, first_out, last_out = rest
    sums_out[...] = sums
    mask = mask_of(info, plane, plane, images)
    average, inverse, total = moments[0:1], moments[1:2], moments[2:3]
    normed = (hidden[...] - average) * inverse
    upstream = grad[...] * wide_spread(gates[2 * images : 3 * images], per_image) + wide_spread(
        pooled_grad[...], per_image
    )
    low = norm_back(upstream, normed, inverse, gain[...], total, sums[0:1], sums[1:2], mask)
    if cut:
        put_halves(mine_out, theirs_out, low, cut, info)
    low = low.astype(bf16)
    if not cut:
        mine_out[...] = low
    average, inverse = middle_moments[0:1], middle_moments[1:2]
    normed = (middle[...] - average) * inverse
    middle_grad = dot(low, weight[...], 1, 1) * slope(normed * middle_gain[...] + middle_shift[...])
    middle_grad_out[...] = middle_grad
    masked = middle_grad * mask
    put_pair(pair_out, total_of(masked), total_of(masked * normed))
    put_edges(first_out, last_out, middle_grad, images, per_image, columns)


def spatial_second_back(
    geometry,
    last,
    info,
    grad,
    grad_above,
    grad_below,
    hidden,
    above,
    below,
    moments,
    gain,
    pairs,
    weight,
    earlier,
    earlier_moments,
    earlier_gain,
    earlier_shift,
    sums_out,
    mine_out,
    theirs_out,
    earlier_grad_out,
    pair_out,
):
    images, rows, columns = geometry
    plane = images * rows * columns
    per_image = rows * columns
    width = hidden.shape[1]
    shift_part, gain_part = gathered_sums(pairs, width // 128)
    sums_out[0:1] = shift_part
    sums_out[1:2] = gain_part
    sums_out[2:8] = jnp.zeros((6, width), f32)
    mask = mask_of(info, plane, plane, images)
    edge_mask = mask_of(info, images * columns, images * columns, images)
    average, inverse, total = moments[0:1], moments[1:2], moments[2:3]

    def lowered(upstream, values, rows_mask):
        normed = (values - average) * inverse
        return norm_back(upstream, normed, inverse, gain[...], total, shift_part, gain_part, rows_mask)

    middle = lowered(grad[...], hidden[...], mask)
    put_halves(mine_out, theirs_out, middle, width, info)
    top = lowered(grad_above[...], above[...], edge_mask * jnp.where(info[1] > 0, 1.0, 0.0))
    bottom = lowered(grad_below[...], below[...], edge_mask * jnp.where(info[1] < last, 1.0, 0.0))
    middle = extended(middle, top, bottom, images, per_image, columns)
    by_column = (shifted(middle, -1, columns), middle, shifted(middle, 1, columns))
    moved = jnp.zeros((plane, width), f32)
    for tap_column in range(3):
        for tap_row in range(3):
            window = window_of(by_column[tap_column], 2 - tap_row, images, per_image, columns)
            moved = moved + dot(window.astype(bf16), weight[3 * tap_row + tap_column], 1, 1)
    normed = (earlier[...] - earlier_moments[0:1]) * earlier_moments[1:2]
    earlier_grad = moved * slope(normed * earlier_gain[...] + earlier_shift[...])
    earlier_grad_out[...] = earlier_grad
    masked = earlier_grad * mask
    put_pair(pair_out, total_of(masked), total_of(masked * normed))


def reduce_second_back(
    geometry,
    info,
    grad,
    hidden,
    moments,
    gain,
    pairs,
    weight,
    carried,
    summed,
    wide_hidden,
    shortcut,
    wide_moments,
    sums_out,
    mine_out,
    theirs_out,
    summed_grad_out,
    state_out,
):
    images, rows, columns = geometry
    plane = images * rows * columns
    per_image = rows * columns
    width = hidden.shape[1]
    shift_part, gain_part = gathered_sums(pairs, width // 128)
    sums_out[0:1] = shift_part
    sums_out[1:2] = gain_part
    sums_out[2:8] = jnp.zeros((6, width), f32)
    mask = mask_of(info, plane, plane, images)
    normed = (hidden[...] - moments[0:1]) * moments[1:2]
    low = norm_back(
        grad[...], normed, moments[1:2], gain[...], moments[2:3], shift_part, gain_part, mask
    )
    put_halves(mine_out, theirs_out, low, width, info)
    low = low.astype(bf16)
    summed_grad = (carried[...] + dot(low, weight[...], 1, 1)) * slope(summed[...])
    summed_grad_out[...] = summed_grad
    normed = (wide_hidden[...] - wide_moments[0:1]) * wide_moments[1:2]
    put_image_sums(state_out, summed_grad, normed, images, per_image)
    other = (shortcut[...] - wide_moments[3:4]) * wide_moments[4:5]
    state_out[2 * images : 2 * images + 1] = total_of(summed_grad * mask * other)
    rest = state_out.shape[0] - 2 * images - 1
    state_out[2 * images + 1 :] = jnp.zeros((rest, summed_grad.shape[1]), f32)


def shortcut_back(geometry, peers, info, grad, shortcut, moments, gain, weight, *rest):
    images, rows, columns = geometry
    plane = images * rows * columns
    sums = rest[0][...]
    for other in rest[1:peers]:
        sums = sums + other[...]
    low_out, image_out = rest[peers:]
    mask = mask_of(info, plane, plane, images)
    normed = (shortcut[...] - moments[3:4]) * moments[4:5]
    low = norm_back(
        grad[...], normed, moments[4:5], gain[...], moments[2:3], sums[2:3], sums[3:4], mask
    )
    low = low.astype(bf16)
    low_out[...] = low
    image_out[...] = dot(low, weight[...], 1, 1)


def spatial_first_back(
    geometry,
    last,
    info,
    grad,
    grad_below,
    hidden,
    below,
    moments,
    gain,
    pairs,
    weight,
    earlier,
    earlier_moments,
    earlier_gain,
    earlier_shift,
    sums_out,
    low_out,
    earlier_grad_out,
    pair_out,
):
    images, rows, columns = geometry
    plane = images * rows * columns
    per_image = rows * columns
    width = hidden.shape[1]
    shift_part, gain_part = gathered_sums(pairs, width // 128)
    sums_out[0:1] = shift_part
    sums_out[1:2] = gain_part
    sums_out[2:8] = jnp.zeros((6, width), f32)
    mask = mask_of(info, plane, plane, images)
    edge_mask = mask_of(info, images * columns, images * columns, images)
    average, inverse, total = moments[0:1], moments[1:2], moments[2:3]

    def lowered(upstream, values, rows_mask):
        normed = (values - average) * inverse
        return norm_back(upstream, normed, inverse, gain[...], total, shift_part, gain_part, rows_mask)

    middle = lowered(grad[...], hidden[...], mask)
    bottom = lowered(grad_below[...], below[...], edge_mask * jnp.where(info[1] < last, 1.0, 0.0))
    parts = []
    for image in range(images):
        parts.append(middle[image * per_image + columns : (image + 1) * per_image])
        parts.append(bottom[image * columns : (image + 1) * columns])
    lower = stack_rows(parts)
    here = middle.astype(bf16)
    low_out[...] = here
    here_right = shifted(middle, -1, columns).astype(bf16)
    next_right = shifted(lower, -1, columns).astype(bf16)
    lower = lower.astype(bf16)

    def back(window, tap_row, tap_column):
        return dot(window, weight[3 * tap_row + tap_column], 1, 1)

    planes = [
        back(here, 1, 1),
        back(here, 1, 2) + back(here_right, 1, 0),
        back(here, 2, 1) + back(lower, 0, 1),
        back(here, 2, 2) + back(here_right, 2, 0) + back(lower, 0, 2) + back(next_right, 0, 0),
    ]
    shift_sum = jnp.zeros((1, width), f32)
    gain_sum = jnp.zeros((1, width), f32)
    for number in range(4):
        at = slice(number * plane, (number + 1) * plane)
        normed = (earlier[at] - earlier_moments[0:1]) * earlier_moments[1:2]
        earlier_grad = planes[number] * slope(normed * earlier_gain[...] + earlier_shift[...])
        earlier_grad_out[at] = earlier_grad
        masked = earlier_grad * mask
        shift_sum = shift_sum + total_of(masked)
        gain_sum = gain_sum + total_of(masked * normed)
    put_pair(pair_out, shift_sum, gain_sum)


def reduce_first_back(
    geometry,
    info,
    grad,
    hidden,
    moments,
    gain,
    pairs,
    weight,
    image_part,
    sums_2,
    sums_3,
    sums_4,
    sums_5,
    sums_6,
    gain_grad_out,
    shift_grad_out,
    low_out,
    image_out,
):
    images, rows, columns = geometry
    plane = images * rows * columns
    width = hidden.shape[1]
    shift_part, gain_part = gathered_sums(pairs, width // 128)
    at = 0
    for shift_row, gain_row in (
        (shift_part, gain_part),
        (sums_2[0:1], sums_2[1:2]),
        (sums_3[0:1], sums_3[1:2]),
        (sums_3[2:3], sums_3[3:4]),
        (sums_4[0:1], sums_4[1:2]),
        (sums_5[0:1], sums_5[1:2]),
        (sums_6[0:1], sums_6[1:2]),
    ):
        shift_grad_out[:, at : at + shift_row.shape[1]] = shift_row
        gain_grad_out[:, at : at + shift_row.shape[1]] = gain_row
        at += shift_row.shape[1]
    mask = mask_of(info, 4 * plane, plane, images)
    normed = (hidden[...] - moments[0:1]) * moments[1:2]
    low = norm_back(
        grad[...], normed, moments[1:2], gain[...], moments[2:3], shift_part, gain_part, mask
    ).astype(bf16)
    low_out[...] = low
    image_grad = dot(low, weight[...], 1, 1)
    image_grad = stack_rows([image_grad[:plane] + image_part[...], image_grad[plane:]]).astype(bf16)
    order = plane_order(4 * plane, images, rows, columns)
    image_out[...] = dot(order, image_grad, 0, 0).astype(bf16)


def unit(size):
    rows = lax.broadcasted_iota(jnp.int32, (size, size), 0)
    columns = lax.broadcasted_iota(jnp.int32, (size, size), 1)
    return (rows == columns).astype(bf16)


def turned(values, one):
    return dot(one, values, 1, 1).astype(bf16)


def outer_rows(inner, outer, out, base=0):
    width = out.shape[1]
    pieces = outer.shape[1] // width
    count = inner.shape[1]
    if pieces == 1:
        step = min(512, count)
        one = unit(step)
        for start in range(0, count, step):
            part = turned(inner[:, start : start + step], one)
            out[base + start : base + start + step] = dot(part, outer).astype(bf16)
        return
    step = 512 // pieces
    row = lax.broadcasted_iota(jnp.int32, (step * pieces, step), 0)
    column = lax.broadcasted_iota(jnp.int32, (step * pieces, step), 1)
    spreads = [(row == column * pieces + piece).astype(bf16) for piece in range(pieces)]
    stacked = stack_rows([outer[:, piece * width : (piece + 1) * width] for piece in range(pieces)])
    for start in range(0, count, step):
        part = inner[:, start : start + step]
        widened = [dot(spread, part, 1, 1).astype(bf16) for spread in spreads]
        result = dot(jnp.concatenate(widened, 1), stacked)
        out[base + start * pieces : base + (start + step) * pieces] = result.astype(bf16)


def weight_rows(inner, outer, out):
    outer_rows(inner[...], outer[...], out)


def two_parts(values):
    first = values.astype(bf16).astype(f32)
    return first, values - first


def left_parts(values):
    first, second = two_parts(values)
    return stack_rows([first, second, first]).astype(bf16)


def right_parts(values):
    first, second = two_parts(values)
    return stack_rows([first, first, second]).astype(bf16)


def gate_rows(images, share, gates, reduced, gate_grad, reduced_grad, out, base=0):
    width = out.shape[1]
    pooled = gates[images : 2 * images]
    squeezed = reduced[images : 2 * images]
    right = right_parts(reduced_grad[...] * share)
    units = reduced_grad.shape[1]
    pieces = width // units
    index = lax.broadcasted_iota(jnp.int32, (width, units), 0)
    column = lax.broadcasted_iota(jnp.int32, (width, units), 1)
    picks = [(index == column * pieces + piece).astype(bf16) for piece in range(pieces)]
    count = pooled.shape[1]
    for start in range(0, count, width):
        rows = []
        for piece in range(pieces):
            picked = exact_dot(pooled[:, start : start + width], picks[piece])
            rows.append(dot(left_parts(picked), right, 0, 0))
        at = base + start // pieces
        out[at : at + units] = jnp.concatenate(rows, 1).astype(bf16)
    wide_pieces = gate_grad.shape[1] // width
    row = lax.broadcasted_iota(jnp.int32, (units, units * wide_pieces), 0)
    column = lax.broadcasted_iota(jnp.int32, (units, units * wide_pieces), 1)
    left = left_parts(squeezed)
    right = right_parts(gate_grad[...] * share)
    result = jnp.zeros((units * wide_pieces, width), f32)
    for piece in range(wide_pieces):
        widened = dot(left, (column == row * wide_pieces + piece).astype(bf16)).astype(bf16)
        result = result + dot(widened, right[:, piece * width : (piece + 1) * width], 0, 0)
    at = base + count // pieces
    out[at : at + units * wide_pieces] = result.astype(bf16)


def spatial_alone(geometry, info, active, above, below, outer, out):
    images, rows, columns = geometry
    per_image = rows * columns
    width = active.shape[1]

    def edge(values, at):
        parts = [values[image * per_image + at : image * per_image + at + columns] for image in range(images)]
        return stack_rows(parts).astype(f32)

    top = edge(above, per_image - columns) * jnp.where(info[1] > 0, 1.0, 0.0)
    bottom = edge(below, 0) * jnp.where(info[1] < info[4], 1.0, 0.0)
    middle = extended(active[...].astype(f32), top, bottom, images, per_image, columns)
    by_column = (shifted(middle, 1, columns), middle, shifted(middle, -1, columns))
    one = unit(width)
    for tap in range(9):
        window = window_of(by_column[tap % 3], tap // 3, images, per_image, columns).astype(bf16)
        out[tap * width : (tap + 1) * width] = dot(turned(window, one), outer[...]).astype(bf16)


def weight_taps(windows, outer, out):
    taps, _, width = windows.shape
    one = unit(width)
    for tap in range(taps):
        out[tap * width : (tap + 1) * width] = dot(turned(windows[tap], one), outer[...]).astype(bf16)


class Band:
    def __init__(self, rows, half, lines, xs):
        self.rows, self.half, self.lines, self.xs = rows, half, lines, xs

    def shapes(self):
        lines = len(self.lines)
        left = ((lines, len(self.xs), self.rows, self.half), bf16)
        right = ((lines, 2, self.rows, self.half), bf16)
        return [left, left, right, right]


def spot_of(info):
    return info[2], jnp.right_shift(info[1], 1), jnp.bitwise_and(info[1], 1)


def send_piece(band, spot, piece, source, place, refs, semaphores, used):
    x, y, core = spot
    line, x_of, y_of, core_of = piece >> 3, (piece >> 2) & 1, (piece >> 1) & 1, piece & 1
    if line not in band.lines or x_of not in band.xs:
        return []
    slot = band.lines.index(line)
    copies = []
    for half in range(2):
        mine = (y == y_of) if half == 0 else (x == x_of)
        inner = band.xs.index(x_of) if half == 0 else y_of
        columns = pl.ds(band.half * half, band.half)
        for kept in (True, False):
            target = refs[2 * half + (0 if kept else 1)].at[slot, inner, place]
            copy = pltpu.make_async_copy(source.at[:, columns], target, semaphores.at[used[0]])
            used[0] += 1
            wanted = mine if kept else jnp.logical_not(mine)
            if core is not None:
                wanted = jnp.logical_and(core == core_of, wanted)
            copies.append((wanted, copy))
    return copies


def send_rows(band, spot, source, base, first, last, refs, semaphores, used):
    copies = []
    for piece in range(first // band.rows, (last - 1) // band.rows + 1):
        start = max(first, piece * band.rows)
        stop = min(last, (piece + 1) * band.rows)
        held = source.at[pl.ds(base + start - first, stop - start)]
        place = pl.ds(start - piece * band.rows, stop - start)
        copies += send_piece(band, spot, piece, held, place, refs, semaphores, used)
    return copies


def conduct(copies, action):
    for wanted, copy in copies:

        def act(copy=copy):
            getattr(copy, action)()

        pl.when(wanted)(act)


def paired(own, other):
    return stack_rows([own[...], other[...]])


def merged_rows(values):
    return values[...].reshape(-1, values.shape[-1])


def half_of(values, width, info):
    first, second = [], []
    for start in range(0, values.shape[1], width):
        first.append(values[:, start : start + width // 2])
        second.append(values[:, start + width // 2 : start + width])
    low = jnp.right_shift(info[1], 1) == 0
    return jnp.where(low, jnp.concatenate(first, 1), jnp.concatenate(second, 1))


def place_rows(slice_rows, core, source, first, last, target, semaphores, used):
    copies = []
    for piece in range(first // slice_rows, (last - 1) // slice_rows + 1):
        start = max(first, piece * slice_rows)
        stop = min(last, (piece + 1) * slice_rows)
        held = source.at[pl.ds(start - first, stop - start)]
        place = pl.ds(start - piece * slice_rows, stop - start)
        target_rows = target.at[piece >> 2, (piece >> 1) & 1, place]
        copies.append(
            (core == (piece & 1), pltpu.make_async_copy(held, target_rows, semaphores.at[used[0]]))
        )
        used[0] += 1
    return copies


def early_rows(images, share, starts, slice_rows, bands, info, *rest):
    (
        active,
        active_other,
        low,
        low_other,
        planes,
        planes_other,
        shortcut,
        shortcut_other,
        pooled,
        reduced,
        gate_grad,
        reduced_grad,
        *targets,
        gate_held,
        slices_held,
        expand_held,
        semaphores,
    ) = rest
    upper, lower = bands
    spot = spot_of(info)
    core = spot[2]
    used = [0]
    copies = []

    def go(added):
        conduct(added, "start")
        copies.extend(added)

    for one in (active, active_other, low, low_other, planes, planes_other, shortcut, shortcut_other):
        one.wait()
    right = right_parts(reduced_grad[...] * share)
    units = reduced_grad.shape[1]
    for number in range(pooled.shape[0]):
        squeezed_rows = dot(left_parts(pooled[number]), right, 0, 0)
        gate_held[0:units, number * units : (number + 1) * units] = squeezed_rows.astype(bf16)
    gate_held[units : 2 * units] = dot(
        left_parts(reduced[images : 2 * images]), right_parts(gate_grad[...] * share), 0, 0
    ).astype(bf16)

    pieces = starts[3] // slice_rows
    numbers = range(pieces // 4)
    found = {number: [] for number in numbers}

    def pick(first, last, count):
        near = [
            number
            for number in numbers
            if (pieces // 2 + 2 * number + 2) * slice_rows > first
            and (pieces // 2 + 2 * number) * slice_rows < last
        ]
        row = lax.broadcasted_iota(jnp.int32, (upper.rows, count), 0)
        column = lax.broadcasted_iota(jnp.int32, (upper.rows, count), 1)
        chosen = []
        for number in near:
            begin = (pieces // 2 + 2 * number + core) * slice_rows - first
            wanted = jnp.logical_and(column == row + begin, row < slice_rows)
            chosen.append(wanted.astype(f32))
        return near, stack_rows(chosen).astype(bf16)

    def add(near, result):
        for at, number in enumerate(near):
            found[number].append(result[at * upper.rows : (at + 1) * upper.rows])

    for first, last, inner, outer in (
        (starts[2], starts[3], (planes, planes_other), (shortcut, shortcut_other)),
        (starts[0], starts[1], (active, active_other), (low, low_other)),
    ):
        near, chosen = pick(first, last, inner[0].shape[1])
        left = dot(chosen, paired(*inner), 1, 1).astype(bf16)
        add(near, dot(left, paired(*outer)))
    near, chosen = pick(starts[1], starts[2], 2 * units)
    add(near, dot(chosen, gate_held[...]))
    for number in numbers:
        held = slices_held.at[number]
        held[...] = sum(found[number][1:], found[number][0]).astype(bf16)
        piece = pieces // 2 + 2 * number
        place = pl.ds(0, upper.rows)
        go(send_piece(upper, (*spot[:2], None), piece, held, place, targets[:4], semaphores, used))
    width = expand_held.shape[1]
    pieces = low.shape[1] // width
    count = expand_held.shape[0] // pieces
    outer_rows(
        stack_rows([active[:, 0:count], active_other[:, 0:count]]), paired(low, low_other), expand_held
    )
    first = starts[0] * pieces
    last = starts[3] * pieces // 2
    held = expand_held.at[pl.ds(0, last - first)]
    go(send_rows(lower, spot, held, 0, first, last, targets[4:], semaphores, used))
    conduct(copies, "wait")


def gate_slices(images, start, slice_rows, info, gates, reduced, gate_grad, reduced_grad, target, held, half_held, semaphores):
    core = jnp.bitwise_and(info[1], 1)
    gate_rows(images, 1.0, gates, reduced, gate_grad, reduced_grad, held)
    half_held[...] = half_of(held[...].astype(f32), held.shape[1], info).astype(bf16)
    last = start + held.shape[0]
    copies = place_rows(slice_rows, core, half_held, start, last, target, semaphores, [0])
    conduct(copies, "start")
    conduct(copies, "wait")


def whole_rows_of(start, slice_rows, info, active, low, target, held, semaphores):
    core = jnp.bitwise_and(info[1], 1)
    outer_rows(merged_rows(active), merged_rows(low), held)
    last = start + held.shape[0]
    copies = place_rows(slice_rows, core, held, start, last, target, semaphores, [0])
    conduct(copies, "start")
    conduct(copies, "wait")


def image_rows(values, image, images):
    span = values.shape[1] // images
    return [values[number, image * span : (image + 1) * span] for number in range(values.shape[0])]


def whole_spatial_rows(geometry, start, slice_rows, info, active, low, target, held, semaphores):
    images, _, columns = geometry
    core = jnp.bitwise_and(info[1], 1)
    used = [0]
    copies = []
    width = active.shape[-1]
    rim = jnp.zeros((columns, width), f32)
    outer, maps = [], []
    for image in range(images):
        outer += image_rows(low, image, images)
        parts = [part.astype(f32) for part in image_rows(active, image, images)]
        maps.append(stack_rows([rim] + parts + [rim]))
    outer = stack_rows(outer)
    span = maps[0].shape[0]
    every = stack_rows(maps)
    by_column = (shifted(every, 1, columns), every, shifted(every, -1, columns))
    by_column = [part.astype(bf16) for part in by_column]
    one = unit(width)
    for tap in range(9):
        tap_row, tap_column = tap // 3, tap % 3
        window = stack_rows(
            [
                by_column[tap_column][
                    image * span + tap_row * columns : (image + 1) * span - (2 - tap_row) * columns
                ]
                for image in range(images)
            ]
        )
        held[tap * width : (tap + 1) * width] = dot(turned(window, one), outer).astype(bf16)
        first = start + tap * width
        added = place_rows(
            slice_rows,
            core,
            held.at[pl.ds(tap * width, width)],
            first,
            first + width,
            target,
            semaphores,
            used,
        )
        conduct(added, "start")
        copies.extend(added)
    conduct(copies, "wait")


def spatial_rows(start, band, info, windows, windows_other, low, low_other, *rest):
    *targets, held, semaphores = rest
    spot = spot_of(info)
    used = [0]
    copies = []
    outer = paired(low, low_other)
    taps, _, width = windows.shape
    one = unit(width)
    for tap in range(taps):
        inner = stack_rows([windows[tap], windows_other[tap]])
        held[tap * width : (tap + 1) * width] = dot(turned(inner, one), outer).astype(bf16)
        first = start + tap * width
        added = send_rows(
            band, spot, held, tap * width, first, first + width, targets, semaphores, used
        )
        conduct(added, "start")
        copies.extend(added)
    conduct(copies, "wait")


def reduce_rows(band, info, planes, planes_other, low, low_other, *rest):
    *targets, held, semaphores = rest
    spot = spot_of(info)
    outer_rows(paired(planes, planes_other), paired(low, low_other), held)
    copies = send_rows(band, spot, held, 0, 0, held.shape[0], targets, semaphores, [0])
    conduct(copies, "start")
    conduct(copies, "wait")


def second_halves(band, info, left, left_came, right, right_came, *outs):
    x, y = info[2], jnp.right_shift(info[1], 1)

    def total(first, second, slot, inner):
        return first[slot, inner].astype(f32) + second[slot, inner].astype(f32)

    outs = list(outs)
    split = len(band.xs) == 2
    left_outs = [outs.pop(0) for _ in range(2 if split else 1)]
    right_outs = outs
    left.wait(), left_came.wait(), right.wait(), right_came.wait()
    for slot in range(len(band.lines)):
        if split:
            left_outs[0][slot] = total(left, left_came, slot, x).astype(bf16)
            left_outs[1][slot] = total(left, left_came, slot, 1 - x).astype(bf16)
        else:
            left_outs[0][slot] = total(left, left_came, slot, 0).astype(bf16)
        right_outs[0][slot] = total(right, right_came, slot, y).astype(bf16)
        right_outs[1][slot] = total(right, right_came, slot, 1 - y).astype(bf16)


def line_halves(band, info, left, left_came, right, right_came, *outs):
    low = jnp.bitwise_and(info[3], 1)
    half = band.half

    def put(out, at, slot):
        out[at, :, 0:half] = (left[slot].astype(f32) + left_came[slot].astype(f32)).astype(bf16)
        out[at, :, half:] = (right[slot].astype(f32) + right_came[slot].astype(f32)).astype(bf16)

    left.wait(), left_came.wait(), right.wait(), right_came.wait()
    if len(band.lines) == 1:
        put(outs[0], 0, 0)
        return
    for at in range(len(band.lines) // 2):
        put(outs[0], at, 2 * at + low)
        put(outs[1], at, 2 * at + 1 - low)


def line_sum(band, info, own, came, *outs):
    if len(band.lines) < 4:
        outs[0][...] = (own[0].astype(f32) + came[0].astype(f32)).astype(bf16)
        return
    top = jnp.right_shift(info[3], 1)
    own.wait(), came.wait()
    for out, slot in zip(outs, (top, 1 - top)):
        out[...] = (own[slot].astype(f32) + came[slot].astype(f32)).astype(bf16)


class Loaded:
    def __init__(self, source, held, semaphore):
        self.held = held
        self.shape = held.shape
        self.copy = pltpu.make_async_copy(source, held, semaphore)
        self.copy.start()
        self.arrived = False

    def wait(self):
        if not self.arrived:
            self.copy.wait()
            self.arrived = True

    def __getitem__(self, index):
        self.wait()
        return self.held[index]


class Gathered:
    def __init__(self, sources, held, semaphores, places):
        self.held = held
        self.shape = held.shape
        self.copies = []
        for number, (source, place) in enumerate(zip(sources, places)):
            copy = pltpu.make_async_copy(source, held.at[place], semaphores.at[number])
            copy.start()
            self.copies.append(copy)

    def wait(self):
        for copy in self.copies:
            copy.wait()
        self.copies = []

    def __getitem__(self, index):
        self.wait()
        return self.held[index]


class Kept:
    def __init__(self, held, target, semaphore):
        self.held = held
        self.shape = held.shape
        self.copy = pltpu.make_async_copy(held, target, semaphore)
        self.sent = False

    def __setitem__(self, index, value):
        assert not self.sent
        self.held[index] = value

    def send(self):
        if not self.sent:
            self.copy.start()
            self.sent = True


def extent(shape, index):
    sizes = []
    for size, part in zip(shape, index):
        start, stop, _ = part.indices(size)
        sizes.append(stop - start)
    return tuple(sizes) + tuple(shape[len(index) :])


def bounded(ref, index):
    parts = []
    for size, part in zip(ref.shape, index):
        start, stop, _ = part.indices(size)
        parts.append(pl.ds(start, stop - start))
    return ref.at[tuple(parts)]


def run_rows(kernel, shapes, buffers, held, copies, *args, limit=64, after=()):
    views = []
    for arg in args[1:]:
        if isinstance(arg, list):
            views.append((arg, None))
        else:
            views.append(arg if isinstance(arg, tuple) else (arg, ()))
    arrays = [args[0]]
    loaded_shapes, load_semaphores_of = [], []
    for source, index in views:
        if index is None:
            arrays += source
            loaded_shapes.append(pltpu.VMEM((len(source),) + source[0].shape, source[0].dtype))
            load_semaphores_of.append(len(source))
        else:
            arrays.append(source)
            loaded_shapes.append(pltpu.VMEM(extent(source.shape, index), source.dtype))
            load_semaphores_of.append(1)
    loads = len(views)
    given_count = len(arrays)
    shapes = [jax.ShapeDtypeStruct(*one) for one in shapes]
    aliases = {}
    if buffers is not None:
        aliases = {len(arrays) + number: number for number in range(len(buffers))}
        arrays += list(buffers)
    arrays += list(after)
    inputs = len(arrays)

    def body(*refs):
        info, given = refs[0], refs[1:given_count]
        targets = refs[inputs : inputs + len(shapes)]
        rest = refs[inputs + len(shapes) :]
        load_semaphores = rest[loads]
        loaded, at = [], 0
        for number in range(loads):
            index = views[number][1]
            if index is None:
                places = [info[1], info[1] ^ 2, info[1] ^ 1, info[1] ^ 3]
                span = len(places)
                semaphores = load_semaphores.at[pl.ds(at, span)]
                loaded.append(Gathered(given[at : at + span], rest[number], semaphores, places))
                at += span
                continue
            source = given[at]
            if index:
                source = bounded(source, index)
            loaded.append(Loaded(source, rest[number], load_semaphores.at[at]))
            at += 1
        kernel(info, *loaded, *targets, *rest[loads + 1 :])
        for one in loaded:
            one.wait()

    moved = sum(_size(one) for one in loaded_shapes) + sum(_size(one) for one in shapes)
    anywhere = pl.BlockSpec(memory_space=pl.ANY)
    return pl.pallas_call(
        body,
        out_shape=shapes,
        in_specs=[pl.BlockSpec(memory_space=pltpu.SMEM)] + [anywhere] * (inputs - 1),
        out_specs=[anywhere] * len(shapes),
        scratch_shapes=loaded_shapes
        + [pltpu.SemaphoreType.DMA((sum(load_semaphores_of),))]
        + [pltpu.VMEM(shape, bf16) for shape in held]
        + [pltpu.SemaphoreType.DMA((copies,))],
        input_output_aliases=aliases,
        compiler_params=pltpu.CompilerParams(vmem_limit_bytes=limit << 20),
        cost_estimate=pl.CostEstimate(flops=7 * 10**9, bytes_accessed=25 * 10**6, transcendentals=0),
    )(*arrays)


def run(kernel, outs, *args, scalars=1, limit=64, flops=0, into=None, after=()):
    views = [arg if isinstance(arg, tuple) else (arg, ()) for arg in args[scalars:]]
    arrays = list(args[:scalars]) + [array for array, _ in views]
    held = [pltpu.VMEM(extent(array.shape, index), array.dtype) for array, index in views]
    kept = [pltpu.VMEM(shape, dtype) for shape, dtype in outs]
    shapes = [jax.ShapeDtypeStruct(shape, dtype) for shape, dtype in outs]
    aliases = {}
    first_row = 0
    if into is not None:
        buffer, full, first_row = into
        shapes = [jax.ShapeDtypeStruct(full, outs[0][1])]
        if buffer is not None:
            aliases = {len(arrays): 0}
            arrays.append(buffer)
    single = len(shapes) == 1
    arrays += list(after)
    inputs, loads, results = len(arrays), len(views), len(outs)

    def body(*refs):
        given, targets = refs[:inputs], refs[inputs : inputs + results]
        rest = refs[inputs + results :]
        loaded_refs, kept_refs = rest[:loads], rest[loads : loads + results]
        load_semaphores, keep_semaphores = rest[loads + results :]
        order = sorted(range(loads), key=lambda number: held[number].shape and _size(held[number]))
        loaded = [None] * loads
        for number in order:
            source = given[scalars + number]
            index = views[number][1]
            if index:
                source = bounded(source, index)
            loaded[number] = Loaded(source, loaded_refs[number], load_semaphores.at[number])
        stored = []
        for number in range(results):
            target = targets[number]
            if into is not None:
                target = target.at[pl.ds(first_row, outs[0][0][0])]
            stored.append(Kept(kept_refs[number], target, keep_semaphores.at[number]))
        kernel(*given[:scalars], *loaded, *stored)
        for one in stored:
            one.send()
        for one in loaded:
            one.wait()
        for one in stored:
            one.copy.wait()

    moved = sum(_size(one) for one in held) + sum(_size(one) for one in kept)
    anywhere = pl.BlockSpec(memory_space=pl.ANY)
    return pl.pallas_call(
        body,
        out_shape=shapes[0] if single else shapes,
        in_specs=[pl.BlockSpec(memory_space=pltpu.SMEM)] * scalars + [anywhere] * (inputs - scalars),
        out_specs=anywhere if single else [anywhere] * len(shapes),
        scratch_shapes=held
        + kept
        + [pltpu.SemaphoreType.DMA((max(loads, 1),)), pltpu.SemaphoreType.DMA((results,))],
        input_output_aliases=aliases,
        compiler_params=pltpu.CompilerParams(vmem_limit_bytes=limit << 20),
        cost_estimate=pl.CostEstimate(flops=7 * 10**9, bytes_accessed=25 * 10**6, transcendentals=0),
    )(*arrays)


def _size(ref):
    total = jnp.dtype(ref.dtype).itemsize
    for one in ref.shape:
        total *= one
    return total


def exchanged(payload):
    return lax.all_to_all(payload, everywhere, 0, 0, tiled=True)


def swapped(shard, wide_bits, narrow_bits):
    wide, narrow = lax.axis_size("wide"), lax.axis_size("narrow")
    if not wide_bits:
        return lax.ppermute(shard, "narrow", [(i, i ^ narrow_bits) for i in range(narrow)])
    if not narrow_bits:
        return lax.ppermute(shard, "wide", [(i, i ^ wide_bits) for i in range(wide)])
    pairs = [
        (w * narrow + n, (w ^ wide_bits) * narrow + (n ^ narrow_bits))
        for w in range(wide)
        for n in range(narrow)
    ]
    return lax.ppermute(shard, everywhere, pairs)


def handed(shard, by):
    peers = lax.axis_size("narrow")
    pairs = [(i, i + by) for i in range(peers) if 0 <= i + by < peers]
    return lax.ppermute(shard, "narrow", pairs)


def later_stages():
    peers = lax.axis_size("wide")
    steps, bit = [], 2
    while bit < peers:
        if 2 * bit < peers:
            steps.append((bit, 2 * bit, 3 * bit))
            bit *= 4
        else:
            steps.append((bit,))
            bit *= 2
    return steps


def merged_state(images, state):
    def combined(state, others, adders):
        return run(
            functools.partial(merge_states, images, adders),
            [(state.shape, f32)],
            state,
            *others,
            scalars=0,
        )

    state = combined(state, [swapped(state, 0, 1)], (1,))
    others = [swapped(state, 0, 2), swapped(state, 1, 0), swapped(state, 1, 2)]
    state = combined(state, others, (1,))
    stages = later_stages()
    for step in stages[:-1]:
        state = combined(state, [swapped(state, bits, 0) for bits in step], ())
    return [state] + [swapped(state, bits, 0) for bits in stages[-1]]


def wide_parts(sums):
    sums = sums + swapped(sums, 1, 0)
    stages = later_stages()
    for step in stages[:-1]:
        sums = sum([swapped(sums, bits, 0) for bits in step], sums)
    return [sums] + [swapped(sums, bits, 0) for bits in stages[-1]]


def swapped_once(shard, axis, bits, sender):
    peers = lax.axis_size(axis)
    pairs = [(i, i ^ bits) for i in range(peers) if bool(i & bits) == sender]
    return lax.ppermute(shard, axis, pairs)


class Transfer:
    def __init__(self, band, info, arrays):
        self.band, self.info = band, info
        self.split = len(band.xs) == 2
        self.left, left_sent, self.right, right_sent = arrays
        self.left_came, self.right_came = swapped(left_sent, 0, 2), self.along_x(right_sent)

    def along_x(self, shard):
        return swapped(shard, 1, 0) if self.split else swapped_once(shard, "wide", 1, True)

    def second(self, after=()):
        band = self.band
        flat = ((len(band.lines), band.rows, band.half), bf16)
        outs = run(
            functools.partial(second_halves, band),
            [flat] * (4 if self.split else 3),
            self.info,
            self.left,
            self.left_came,
            self.right,
            self.right_came,
            after=after,
        )
        self.left, left_sent = outs[0], outs[1 if self.split else 0]
        self.right, right_sent = outs[-2], outs[-1]
        self.left_came, self.right_came = self.along_x(left_sent), swapped(right_sent, 0, 2)
        return (outs[0],)

    def third(self, after=()):
        band = self.band
        count = max(len(band.lines) // 2, 1)
        shape = ((count, band.rows, 2 * band.half), bf16)
        outs = run(
            functools.partial(line_halves, band),
            [shape] * min(len(band.lines), 2),
            self.info,
            self.left,
            self.left_came,
            self.right,
            self.right_came,
            after=after,
        )
        if len(band.lines) > 1:
            self.own, self.came = outs[0], swapped(outs[1], 2, 0)
        else:
            self.own, self.came = outs, swapped_once(outs, "wide", 2, True)
        return (self.own,)

    def fourth(self, after=()):
        band = self.band
        shape = ((band.rows, 2 * band.half), bf16)
        outs = run(
            functools.partial(line_sum, band),
            [shape] * (2 if len(band.lines) == 4 else 1),
            self.info,
            self.own,
            self.came,
            after=after,
        )
        if len(band.lines) == 4:
            self.own, self.came = outs[0], swapped(outs[1], 4, 0)
        else:
            self.own, self.came = outs, swapped_once(outs, "wide", 4, band.lines[0] < 2)
        return (self.own,)

    def result(self):
        return self.own.astype(f32) + self.came.astype(f32)


def swept(mine, info):
    low = info[1] < 2
    kept = jnp.where(low, mine[0], mine[1])
    came = swapped(jnp.where(low, mine[1], mine[0]), 0, 2)
    halves = [jnp.where(low, kept, came), jnp.where(low, came, kept)]
    return jnp.concatenate(halves, 1).astype(f32)


def scattered(rows, devices):
    done = lax.psum_scatter(rows, everywhere, scatter_dimension=0, tiled=True)
    return done.astype(f32).reshape(-1)


def on_device(
    images,
    first_reduce,
    first_spatial,
    first_expand,
    first_squeeze,
    first_excite,
    first_project,
    second_reduce,
    second_spatial,
    second_expand,
    second_squeeze,
    second_excite,
    norm_gains,
    norm_shifts,
    image_counts,
    out_grad,
):
    wide, narrow = lax.axis_size("wide"), lax.axis_size("narrow")
    assert narrow == 4
    devices = wide * narrow
    count, rows_in, cols_in, channels = images.shape
    rows, columns = rows_in // 2, cols_in // 2
    geometry = (count, rows, columns)
    plane = count * rows * columns
    edge = count * columns
    area = rows * columns * narrow
    last = narrow - 1
    mid = first_reduce.shape[1]
    out = first_expand.shape[1]
    chunks = mid // 128
    place = lax.axis_index("wide").astype(jnp.int32)
    info = jnp.stack(
        [
            image_counts[0],
            lax.axis_index("narrow").astype(jnp.int32),
            jnp.bitwise_and(place, 1),
            jnp.right_shift(place, 1),
            jnp.full((), narrow - 1, jnp.int32),
        ]
    )
    widths = [mid, mid, out, out, mid, mid, out]
    gains, shifts, at = [], [], 0
    for width in widths:
        part = (slice(0, 1), slice(at, at + width))
        gains.append((norm_gains[None], part))
        shifts.append((norm_shifts[None], part))
        at += width
    pair = ((devices, 2 * chunks, 128), f32)
    small = ((8, mid), f32)
    large = ((8, out), f32)
    edge_map = ((edge, mid), f32)
    taps = (9, mid, mid)
    spatial_one = first_spatial.reshape(taps)
    spatial_two = second_spatial.reshape(taps)
    bind = functools.partial

    planes, h1, pairs, edges = run(
        bind(reduce_first, geometry),
        [
            ((4 * plane, channels), bf16),
            ((4 * plane, mid), f32),
            ((devices, 2 * chunks + 8, 128), f32),
            ((2 * edge, mid), f32),
        ],
        info,
        images.reshape(4 * plane, channels),
        first_reduce,
    )
    halo = handed(edges, 1)
    pairs = exchanged(pairs)
    planes_other = swapped(planes, 0, 1)
    hp, moments_p = run(
        bind(project_first, geometry), [((plane, out), f32), large], info, planes, first_project
    )
    windows_1, h2, moments_1, counts, pairs, edges = run(
        bind(spatial_first, geometry),
        [
            ((9, plane, mid), bf16),
            ((plane, mid), f32),
            small,
            ((devices, 128), f32),
            pair,
            ((edge, mid), f32),
        ],
        info,
        h1,
        halo,
        pairs,
        gains[0],
        shifts[0],
        spatial_one,
    )
    h2_below = handed(edges, -1)
    pairs = exchanged(pairs)
    a2, h3, moments_2, state = run(
        bind(expand, geometry),
        [((plane, mid), bf16), ((plane, out), f32), small, large],
        info,
        h2,
        pairs,
        counts,
        gains[1],
        shifts[1],
        first_expand,
        moments_p,
        after=(h2_below,),
    )
    states = merged_state(count, state)
    moments_3, gates_1, reduced_1, r1, o1, k1, pairs, firsts, lasts = run(
        bind(reduce_second, geometry, len(states), area),
        [
            large,
            ((3 * count, out), f32),
            ((2 * count, first_squeeze.shape[1]), f32),
            ((plane, out), f32),
            ((plane, out), bf16),
            ((plane, mid), f32),
            pair,
            edge_map,
            edge_map,
        ],
        info,
        h3,
        hp,
        gains[2],
        shifts[2],
        gains[3],
        shifts[3],
        first_squeeze,
        first_excite,
        second_reduce,
        *states,
    )
    k1_above, k1_below = handed(lasts, 1), handed(firsts, -1)
    pairs = exchanged(pairs)
    a3, k2, moments_4, pairs, firsts, lasts = run(
        bind(spatial_second, geometry, last),
        [((plane, mid), bf16), ((plane, mid), f32), small, pair, edge_map, edge_map],
        info,
        k1,
        k1_above,
        k1_below,
        pairs,
        counts,
        gains[4],
        shifts[4],
        spatial_two,
    )
    k2_above, k2_below = handed(lasts, 1), handed(firsts, -1)
    pairs = exchanged(pairs)

    pack_widths = [out, mid, mid]
    a4, k3, moments_5, state, pack = run(
        bind(expand_packing, geometry),
        [
            ((plane, mid), bf16),
            ((plane, out), f32),
            small,
            large,
            ((plane, sum(pack_widths)), bf16),
        ],
        info,
        o1,
        a3,
        k2,
        pairs,
        counts,
        gains[5],
        shifts[5],
        second_expand,
        after=(k2_above, k2_below),
    )
    pack = lax.all_gather(pack, "narrow")
    packed, at = [], 0
    for width in pack_widths:
        packed.append((pack, (slice(0, narrow), slice(0, plane), slice(at, at + width))))
        at += width
    o1_all, a3_all, a4_all = packed

    def gathered_halves(mine, theirs):
        came = swapped(theirs, 0, 2)
        return [mine, came, swapped(mine, 0, 1), swapped(came, 0, 1)]

    def joined(mine, theirs, width):
        low = info[1] < 2
        first, second = jnp.where(low, mine, theirs), jnp.where(low, theirs, mine)
        parts = [one.reshape(plane, -1, width // 2) for one in (first, second)]
        return jnp.concatenate(parts, 2).reshape(plane, -1)

    states = merged_state(count, state)
    moments_6, gates_2, reduced_2, mixed, dr2, state = run(
        bind(finish_second, geometry, len(states), area),
        [
            large,
            ((3 * count, out), f32),
            ((2 * count, second_squeeze.shape[1]), f32),
            ((plane, out), bf16),
            ((plane, out), f32),
            large,
        ],
        info,
        k3,
        o1,
        out_grad.reshape(plane, out),
        gains[6],
        shifts[6],
        second_squeeze,
        second_excite,
        *states,
    )

    def excitation_back(state, has_others, number, gates, reduced, squeeze, excite):
        state = state + swapped(state, 0, 1)
        sums, pooled_grad, gate_grad, reduced_grad = run(
            bind(excite_back, count, area, has_others),
            [
                ((4, out), f32),
                ((count, out), f32),
                ((count, out), f32),
                ((count, squeeze.shape[1]), f32),
            ],
            info,
            gains[number],
            shifts[number],
            gates,
            reduced,
            squeeze,
            excite,
            state,
            swapped(state, 0, 2),
        )
        return wide_parts(sums), pooled_grad, (gates, reduced, gate_grad, reduced_grad)

    parts, pooled_grad, saved_two = excitation_back(
        state, False, 6, gates_2, reduced_2, second_squeeze, second_excite
    )
    half_out, half_mid = ((plane, out // 2), bf16), ((plane, mid // 2), bf16)
    back_outs = [((4, out), f32), half_out, half_out, ((plane, mid), f32), pair, edge_map, edge_map]
    sums_6, dk3_mine, dk3_theirs, du5, pairs, firsts, lasts = run(
        bind(expand_back, geometry, len(parts), mid),
        back_outs,
        info,
        dr2,
        k3,
        moments_6,
        gates_2,
        pooled_grad,
        gains[6],
        second_expand,
        k2,
        moments_5,
        gains[5],
        shifts[5],
        *parts,
    )
    du5_above, du5_below = handed(lasts, 1), handed(firsts, -1)
    pairs = exchanged(pairs)
    second_rows = [0, out, out + 9 * mid, 2 * out + 9 * mid]
    squeeze_rows = 2 * out * second_squeeze.shape[1] // mid
    second_shape = (second_rows[3] + squeeze_rows, mid)
    share = 1.0 / narrow
    first_rows = [0, channels, channels + 9 * mid]
    first_rows.append(first_rows[2] + out)
    first_rows.append(first_rows[3] + squeeze_rows)
    whole_rows = first_rows[4] + channels * out // mid
    slice_rows = whole_rows // devices
    second_slice = second_shape[0] // devices
    by_hand = wide == 8 and slice_rows % 16 == 0 and second_slice % 16 == 0
    if by_hand:
        second_shapes = [((wide, 2, second_slice, mid // 2), bf16)]
        second_sent = run_rows(
            bind(gate_slices, count, second_rows[3], second_slice),
            second_shapes,
            None,
            [(squeeze_rows, mid), (squeeze_rows, mid // 2)],
            16,
            info,
            *saved_two,
        )
        tie = second_sent[:1]
    else:
        tie = ()
        second_flat = run(
            weight_rows,
            [((out, mid), bf16)],
            a4,
            joined(dk3_mine, dk3_theirs, mid),
            scalars=0,
            into=(None, second_shape, second_rows[2]),
        )
        second_flat = run(
            bind(gate_rows, count, share),
            [((squeeze_rows, mid), bf16)],
            *saved_two,
            scalars=0,
            into=(second_flat, second_shape, second_rows[3]),
        )
    sums_5, dk2_mine, dk2_theirs, du4, pairs = run(
        bind(spatial_second_back, geometry, last),
        [small, half_mid, half_mid, ((plane, mid), f32), pair],
        info,
        du5,
        du5_above,
        du5_below,
        k2,
        k2_above,
        k2_below,
        moments_5,
        gains[5],
        pairs,
        spatial_two,
        k1,
        moments_4,
        gains[4],
        shifts[4],
        after=tie,
    )
    pairs = exchanged(pairs)
    if by_hand:
        second_sent = run_rows(
            bind(whole_rows_of, second_rows[2], second_slice),
            second_shapes,
            second_sent,
            [(out, mid // 2)],
            16,
            info,
            a4_all,
            gathered_halves(dk3_mine, dk3_theirs),
        )
        tie = second_sent
    else:
        tie = ()
    sums_4, dk1_mine, dk1_theirs, dr1, state = run(
        bind(reduce_second_back, geometry),
        [small, half_mid, half_mid, ((plane, out), f32), large],
        info,
        du4,
        k1,
        moments_4,
        gains[4],
        pairs,
        second_reduce,
        dr2,
        r1,
        h3,
        hp,
        moments_3,
        after=tie,
    )
    if by_hand:
        second_sent = run_rows(
            bind(whole_spatial_rows, geometry, second_rows[1], second_slice),
            second_shapes,
            second_sent,
            [(9 * mid, mid // 2)],
            9 * 3,
            info,
            a3_all,
            gathered_halves(dk2_mine, dk2_theirs),
        )
        tie = second_sent[:1]
    else:
        second_flat = run(
            bind(spatial_alone, geometry),
            [((9 * mid, mid), bf16)],
            info,
            a3,
            handed(a3, 1),
            handed(a3, -1),
            joined(dk2_mine, dk2_theirs, mid),
            into=(second_flat, second_shape, second_rows[1]),
        )
    if by_hand:
        second_sent = run_rows(
            bind(whole_rows_of, 0, second_slice),
            second_shapes,
            second_sent,
            [(out, mid // 2)],
            16,
            info,
            o1_all,
            gathered_halves(dk1_mine, dk1_theirs),
        )
        second_halves_summed = lax.psum_scatter(
            second_sent[0], "wide", scatter_dimension=0, tiled=False
        )
        tie = second_sent
    else:
        second_flat = run(
            weight_rows,
            [((out, mid), bf16)],
            o1,
            joined(dk1_mine, dk1_theirs, mid),
            scalars=0,
            into=(second_flat, second_shape, second_rows[0]),
        )
        second_done = scattered(second_flat, devices)
    parts, pooled_grad, saved_one = excitation_back(
        state, True, 2, gates_1, reduced_1, first_squeeze, first_excite
    )
    sums_3, dh3, du2, pairs, firsts, _ = run(
        bind(expand_back, geometry, len(parts), 0),
        [((4, out), f32), ((plane, out), bf16), ((plane, mid), f32), pair, edge_map, edge_map],
        info,
        dr1,
        h3,
        moments_3,
        gates_1,
        pooled_grad,
        gains[2],
        first_expand,
        h2,
        moments_2,
        gains[1],
        shifts[1],
        *parts,
        after=tie,
    )
    du2_below = handed(firsts, -1)
    pairs = exchanged(pairs)
    dhp, image_part = run(
        bind(shortcut_back, geometry, len(parts)),
        [((plane, out), bf16), ((plane, channels), f32)],
        info,
        dr1,
        hp,
        moments_3,
        gains[3],
        first_project,
        *parts,
        after=(du2,),
    )
    if by_hand:
        pieces = out // mid
        wide_slice = slice_rows // pieces
        lower = Band(slice_rows, mid // 2, [0, 1], [0, 1])
        upper = Band(-(-wide_slice // 16) * 16, out // 2, [2, 3], [0, 1])
        corner = Band(slice_rows, mid // 2, [0], [0])
        assert channels <= 4 * slice_rows and first_rows[2] <= whole_rows // 2 <= first_rows[3]
        units = first_squeeze.shape[1]
        pooled = gates_1[count : 2 * count].reshape(count, -1, out // units).transpose(2, 0, 1)
        low_part = -(-(whole_rows // 2 - first_rows[2]) // mid) * mid
        sent = run_rows(
            bind(
                early_rows,
                count,
                2 * share,
                [one // pieces for one in first_rows[2:] + [whole_rows]],
                wide_slice,
                (upper, lower),
            ),
            upper.shapes() + lower.shapes(),
            None,
            [(2 * units, out), (devices // 4, upper.rows, out), (low_part, mid)],
            128,
            info,
            a2,
            swapped(a2, 0, 1),
            dh3,
            swapped(dh3, 0, 1),
            (planes, (slice(0, plane),)),
            (planes_other, (slice(0, plane),)),
            dhp,
            swapped(dhp, 0, 1),
            pooled,
            *saved_one[1:],
        )
        upper_sent, lower_sent = sent[:4], sent[4:]
        early = Transfer(upper, info, upper_sent)
        tie = upper_sent[:1]
    else:
        tie = ()
        first_shape = (whole_rows, mid)
        first_flat = run(
            weight_rows,
            [((out, mid), bf16)],
            a2,
            dh3,
            scalars=0,
            into=(None, first_shape, first_rows[2]),
        )
        first_flat = run(
            bind(gate_rows, count, share),
            [((squeeze_rows, mid), bf16)],
            *saved_one,
            scalars=0,
            into=(first_flat, first_shape, first_rows[3]),
        )
        first_flat = run(
            weight_rows,
            [((channels * out // mid, mid), bf16)],
            (planes, (slice(0, plane),)),
            dhp,
            scalars=0,
            into=(first_flat, first_shape, first_rows[4]),
        )
    sums_2, dh2, du1, pairs = run(
        bind(spatial_first_back, geometry, last),
        [small, ((plane, mid), bf16), ((4 * plane, mid), f32), pair],
        info,
        du2,
        du2_below,
        h2,
        h2_below,
        moments_2,
        gains[1],
        pairs,
        spatial_one,
        h1,
        moments_1,
        gains[0],
        shifts[0],
        after=tie,
    )
    pairs = exchanged(pairs)
    if by_hand:
        lower_sent = run_rows(
            bind(spatial_rows, first_rows[1], lower),
            lower.shapes(),
            lower_sent,
            [(9 * mid, mid)],
            9 * 3 * 4,
            info,
            windows_1,
            swapped(windows_1, 0, 1),
            dh2,
            swapped(dh2, 0, 1),
        )
        late = Transfer(lower, info, lower_sent)
        tie = lower_sent[:1]
    else:
        first_flat = run(
            weight_taps,
            [((9 * mid, mid), bf16)],
            windows_1,
            dh2,
            scalars=0,
            into=(first_flat, first_shape, first_rows[1]),
        )
    channel_row = ((1, norm_gains.shape[0]), f32)
    gain_grad, shift_grad, dh1, image_grad = run(
        bind(reduce_first_back, geometry),
        [channel_row, channel_row, ((4 * plane, mid), bf16), ((4 * plane, channels), bf16)],
        info,
        du1,
        h1,
        moments_1,
        gains[0],
        pairs,
        first_reduce,
        image_part,
        sums_2,
        sums_3,
        sums_4,
        sums_5,
        sums_6,
        after=tie,
    )
    if by_hand:
        tie = early.second((image_grad,))
        corner_sent = run_rows(
            bind(reduce_rows, corner),
            corner.shapes(),
            None,
            [(channels, mid)],
            16,
            info,
            planes,
            planes_other,
            dh1,
            swapped(dh1, 0, 1),
            after=tie,
        )
        tie = list(corner_sent[:1])
        final = Transfer(corner, info, corner_sent)
        tie = late.second(tie + [second_halves_summed])
        second_done = swept(second_halves_summed, info)
        tie = early.third(tie)
        tie = final.second(tie)
        tie = late.third(tie)
        tie = early.fourth(tie)
        tie = final.third(tie + (second_done,))
        tie = late.fourth(tie)
        final.fourth(tie)
        upper_done, lower_done, corner_done = early.result(), late.result(), final.result()
        row = (place * narrow + info[1]) * slice_rows + lax.iota(jnp.int32, slice_rows)
        first_done = jnp.where(
            place >= wide // 2,
            upper_done[:wide_slice].reshape(-1),
            jnp.where(row[:, None] < channels, corner_done, lower_done).reshape(-1),
        )
        second_done = second_done.reshape(-1)
    else:
        first_flat = run(
            weight_rows,
            [((channels, mid), bf16)],
            planes,
            dh1,
            scalars=0,
            into=(first_flat, first_shape, 0),
        )
        first_done = scattered(first_flat, devices)
    return (
        mixed.reshape(out_grad.shape),
        image_grad.reshape(images.shape),
        first_done,
        second_done,
        gain_grad.reshape(-1),
        shift_grad.reshape(-1),
    )


def solution(mesh):
    in_specs = (
        (P("wide", "narrow", None, None),) + (P(),) * 13 + (P("wide"), P("wide", "narrow", None, None))
    )
    out_specs = (
        P("wide", "narrow", None, None),
        P("wide", "narrow", None, None),
        P(everywhere),
        P(everywhere),
        P(),
        P(),
    )
    return jax.shard_map(
        on_device, mesh=mesh, in_specs=in_specs, out_specs=out_specs, check_vma=False
    )
```

```python
import functools

import jax
import jax.numpy as jnp
from jax import lax
from jax.experimental import pallas as pl
from jax.experimental.pallas import tpu as pltpu
from jax.sharding import PartitionSpec as P

epsilon = 1e-05
highest = lax.Precision.HIGHEST
f32 = jnp.float32
bf16 = jnp.bfloat16
everywhere = ("wide", "narrow")


def iota_rows(rows, columns=1):
    return lax.broadcasted_iota(jnp.int32, (rows, columns), 0)


def dot(left, right, left_dim=1, right_dim=0):
    return lax.dot_general(
        left, right, (((left_dim,), (right_dim,)), ((), ())), preferred_element_type=f32
    )


def exact_dot(values, weight, weight_dim=0):
    first = values.astype(bf16)
    rest = values - first.astype(f32)
    second = rest.astype(bf16)
    third = (rest - second.astype(f32)).astype(bf16)
    rows = values.shape[0]
    product = dot(
        jnp.concatenate([first.astype(f32), second.astype(f32), third.astype(f32)], 0).astype(bf16),
        weight,
        1,
        weight_dim,
    )
    return product[:rows] + product[rows : 2 * rows] + product[2 * rows : 3 * rows]


def slope(values):
    logistic = jax.nn.sigmoid(values)
    return logistic * (1.0 + values * (1.0 - logistic))


def silu(values):
    return values * jax.nn.sigmoid(values)


def total_of(values):
    return jnp.sum(values, axis=0, keepdims=True)


def mask_of(info, rows, plane, images):
    per_image = plane // images
    index = iota_rows(rows)
    if rows > plane:
        index = jnp.bitwise_and(index, plane - 1)
    return (index < info[0] * per_image).astype(f32)


def images_of(info, images):
    return jnp.minimum(info[0], images).astype(f32)


def local_moments(hidden, mask, pixels):
    summed = total_of(hidden * mask)
    centred = (hidden - summed / pixels) * mask
    return summed, total_of(centred * centred)


def put_pair(out, first, second):
    peers = out.shape[0]
    chunks = first.shape[1] // 128
    for number, row in enumerate((first, second)):
        for chunk in range(chunks):
            part = row[:, chunk * 128 : chunk * 128 + 128]
            out[:, number * chunks + chunk, :] = jnp.broadcast_to(part, (peers, 128))


def gathered_moments(pairs, counts, chunks):
    total = total_of(counts)
    averages, inverses = [], []
    for chunk in range(chunks):
        sums = pairs[:, chunk, :]
        spread = total_of(pairs[:, chunks + chunk, :])
        average = total_of(sums) / total
        spread = spread + total_of(counts * jnp.square(sums / counts - average))
        averages.append(average)
        inverses.append(lax.rsqrt(spread / total + epsilon))
    return jnp.concatenate(averages, 1), jnp.concatenate(inverses, 1), total[:, :1]


def gathered_sums(pairs, chunks):
    rows = [total_of(pairs[:, chunk, :]) for chunk in range(2 * chunks)]
    return jnp.concatenate(rows[:chunks], 1), jnp.concatenate(rows[chunks:], 1)


def merge(groups):
    total = sum(group[0] for group in groups)
    summed = sum(group[1] for group in groups)
    average = summed / total
    spread = sum(group[2] + group[0] * jnp.square(group[1] / group[0] - average) for group in groups)
    return total, summed, spread


def norm_back(upstream, normed, inverse, gain, total, shift_part, gain_part, mask):
    return mask * (gain * inverse) * (upstream - (shift_part + normed * gain_part) / total)


def shifted(values, by, columns):
    rows = values.shape[0]
    column = jnp.bitwise_and(iota_rows(rows), columns - 1)
    edge = 0 if by == 1 else columns - 1
    return jnp.where(column == edge, 0.0, pltpu.roll(values, by % rows, 0))


def put_halves(mine_out, theirs_out, values, width, info):
    first, second = [], []
    for start in range(0, values.shape[1], width):
        first.append(values[:, start : start + width // 2])
        second.append(values[:, start + width // 2 : start + width])
    first, second = jnp.concatenate(first, 1), jnp.concatenate(second, 1)
    low = jnp.right_shift(info[1], 1) == 0
    mine_out[...] = jnp.where(low, first, second).astype(bf16)
    theirs_out[...] = jnp.where(low, second, first).astype(bf16)
    mine_out.send()
    theirs_out.send()


def stack_rows(parts):
    return jnp.concatenate(parts, axis=0)


def plane_order(pixels, images, rows, columns):
    plane = images * rows * columns
    index = iota_rows(4 * plane, 4 * plane)
    other = lax.broadcasted_iota(jnp.int32, (4 * plane, 4 * plane), 1)
    parity = index // plane
    within = index - parity * plane
    line = within // columns
    column = within - line * columns
    natural = (line * 2 + parity // 2) * (2 * columns) + 2 * column + (parity & 1)
    return (other == natural).astype(bf16)


def reduce_first(geometry, info, x, weight, planes_out, hidden_out, pair_out, edge_out):
    images, rows, columns = geometry
    plane = images * rows * columns
    order = plane_order(4 * plane, images, rows, columns)
    planes = dot(order, x[...]).astype(bf16)
    planes_out[...] = planes
    planes_out.send()
    hidden = dot(planes, weight[...])
    hidden_out[...] = hidden
    hidden_out.send()
    mask = mask_of(info, 4 * plane, plane, images)
    pixels = images_of(info, images) * (4 * rows * columns)
    summed, spread = local_moments(hidden, mask, pixels)
    put_pair(pair_out, summed, spread)
    chunks = hidden.shape[1] // 128
    pair_out[:, 2 * chunks, :] = jnp.full((pair_out.shape[0], 128), pixels, f32)
    per_image = rows * columns
    edges = []
    for parity in range(2):
        for image in range(images):
            end = (2 + parity) * plane + (image + 1) * per_image
            edges.append(hidden[end - columns : end])
    edge_out[...] = stack_rows(edges)


def project_first(geometry, info, planes, weight, hidden_out, moments_out):
    images, rows, columns = geometry
    plane = images * rows * columns
    hidden = dot(planes[:plane], weight[...])
    hidden_out[...] = hidden
    hidden_out.send()
    mask = mask_of(info, plane, plane, images)
    pixels = images_of(info, images) * (rows * columns)
    summed, spread = local_moments(hidden, mask, pixels)
    moments_out[0:1] = summed
    moments_out[1:2] = spread
    moments_out[2:8] = jnp.zeros((6, hidden.shape[1]), f32)


def spatial_first(
    geometry,
    info,
    hidden,
    halo,
    pairs,
    gain,
    shift,
    weight,
    active_out,
    moved_out,
    moments_out,
    counts_out,
    pair_out,
    edge_out,
):
    images, rows, columns = geometry
    plane = images * rows * columns
    per_image = rows * columns
    width = hidden.shape[1]
    chunks = width // 128
    counts = pairs[:, 2 * chunks, :]
    counts_out[...] = counts
    average, inverse, total = gathered_moments(pairs, counts, chunks)
    moments_out[0:1] = average
    moments_out[1:2] = inverse
    moments_out[2:3] = jnp.broadcast_to(total, (1, width))
    moments_out[3:8] = jnp.zeros((5, width), f32)
    moments_out.send()
    counts_out.send()

    def active(values):
        return silu((values - average) * inverse * gain[...] + shift[...])

    inside = jnp.where(info[1] > 0, 1.0, 0.0)
    above = active(halo[...]) * inside
    planes = [active(hidden[number * plane : (number + 1) * plane]) for number in range(4)]

    for number in range(4):
        active_out[:, number * width : (number + 1) * width] = planes[number].astype(bf16)
    active_out.send()

    def lifted(parity):
        parts = []
        for image in range(images):
            at = (parity * images + image) * columns
            parts.append(above[at : at + columns])
            start = image * per_image
            parts.append(planes[2 + parity][start : start + per_image - columns])
        return stack_rows(parts)

    by_row = [(lifted(0), lifted(1)), (planes[0], planes[1]), (planes[2], planes[3])]
    moved = jnp.zeros((plane, width), f32)
    for tap_row in range(3):
        even, odd = by_row[tap_row]
        for tap_column, window in enumerate((shifted(odd, 1, columns), even, odd)):
            tap = 3 * tap_row + tap_column
            window = window.astype(bf16)
            moved = moved + dot(window, weight[tap])
    moved_out[...] = moved
    moved_out.send()
    mask = mask_of(info, plane, plane, images)
    pixels = images_of(info, images) * per_image
    put_pair(pair_out, *local_moments(moved, mask, pixels))
    edge_out[...] = stack_rows(
        [moved[image * per_image : image * per_image + columns] for image in range(images)]
    )


def expand(geometry, info, hidden, pairs, counts, gain, shift, weight, others, active_out, hidden_out, moments_out, state_out):
    images, rows, columns = geometry
    plane = images * rows * columns
    per_image = rows * columns
    width = hidden.shape[1]
    average, inverse, total = gathered_moments(pairs, counts[...] * (per_image / (4 * per_image)), width // 128)
    moments_out[0:1] = average
    moments_out[1:2] = inverse
    moments_out[2:3] = jnp.broadcast_to(total, (1, width))
    moments_out[3:8] = jnp.zeros((5, width), f32)
    moments_out.send()
    active = silu((hidden[...] - average) * inverse * gain[...] + shift[...]).astype(bf16)
    active_out[...] = active
    active_out.send()
    wide = dot(active, weight[...])
    hidden_out[...] = wide
    hidden_out.send()
    mask = mask_of(info, plane, plane, images)
    pixels = images_of(info, images) * per_image
    summed, spread = local_moments(wide, mask, pixels)
    for image in range(images):
        state_out[image : image + 1] = total_of(wide[image * per_image : (image + 1) * per_image])
    state_out[images : images + 1] = summed
    state_out[images + 1 : images + 2] = spread
    if others is None:
        state_out[images + 2 : images + 4] = jnp.zeros((2, wide.shape[1]), f32)
    else:
        state_out[images + 2 : images + 4] = others[0:2]
    state_out[images + 4 : images + 5] = jnp.full((1, wide.shape[1]), pixels, f32)
    if state_out.shape[0] > images + 5:
        state_out[images + 5 :] = jnp.zeros((state_out.shape[0] - images - 5, wide.shape[1]), f32)


def expand_packing(geometry, early, has_others, info, *refs):
    *refs, pack_out = refs
    maps, refs = refs[:early], list(refs[early:])
    others = refs.pop(6) if has_others else None
    expand(geometry, info, *refs[:6], others, *refs[6:])
    at = 0
    for one in (*maps, refs[6].held):
        part = one[...]
        pack_out[:, at : at + part.shape[1]] = part
        at += part.shape[1]


def groups_of(states, images, at):
    return [
        (state[images + 4 : images + 5], state[at : at + 1], state[at + 1 : at + 2]) for state in states
    ]


def merge_states(images, adders, *refs):
    *states, out = refs
    image_sums = states[0][0:images]
    for adder in adders:
        image_sums = image_sums + states[adder][0:images]
    out[0:images] = image_sums
    total, summed, spread = merge(groups_of(states, images, images))
    out[images : images + 1] = summed
    out[images + 1 : images + 2] = spread
    _, summed, spread = merge(groups_of(states, images, images + 2))
    out[images + 2 : images + 3] = summed
    out[images + 3 : images + 4] = spread
    out[images + 4 : images + 5] = total
    if out.shape[0] > images + 5:
        out[images + 5 :] = states[0][images + 5 :]


def excited(image_sums, area, average, inverse, gain, shift, squeeze, excite):
    image_means = (image_sums / area - average) * inverse
    pooled = image_means * gain + shift
    reduced = exact_dot(pooled, squeeze)
    squeezed = silu(reduced)
    gate = jax.nn.sigmoid(exact_dot(squeezed, excite))
    return image_means, pooled, reduced, squeezed, gate


def wide_spread(values, per_image):
    return stack_rows(
        [
            jnp.broadcast_to(values[image : image + 1], (per_image, values.shape[1]))
            for image in range(values.shape[0])
        ]
    )


def finish_state(states, images, at):
    total, summed, spread = merge(groups_of(states, images, at))
    average = summed / total
    return average, lax.rsqrt(spread / total + epsilon), total


def put_gates(gates_out, reduced_out, image_means, pooled, gate, reduced, squeezed):
    images = gate.shape[0]
    gates_out[0:images] = image_means
    gates_out[images : 2 * images] = pooled
    gates_out[2 * images : 3 * images] = gate
    reduced_out[0:images] = reduced
    reduced_out[images : 2 * images] = squeezed


def reduce_second(
    geometry,
    peers,
    area,
    info,
    hidden,
    shortcut,
    gain,
    shift,
    gain_p,
    shift_p,
    squeeze,
    excite,
    weight,
    *rest,
):
    images, rows, columns = geometry
    plane = images * rows * columns
    per_image = rows * columns
    states = rest[:peers]
    moments_out, gates_out, reduced_out, summed_out, block_out, moved_out, pair_out, first_out, last_out = rest[peers:]
    average, inverse, total = finish_state(states, images, images)
    average_p, inverse_p, _ = finish_state(states, images, images + 2)
    for row, value in enumerate((average, inverse, total, average_p, inverse_p)):
        moments_out[row : row + 1] = value
    moments_out[5:8] = jnp.zeros((3, average.shape[1]), f32)
    image_means, pooled, reduced, squeezed, gate = excited(
        states[0][0:images], area, average, inverse, gain[...], shift[...], squeeze[...], excite[...]
    )
    put_gates(gates_out, reduced_out, image_means, pooled, gate, reduced, squeezed)
    branch = (hidden[...] - average) * inverse * gain[...] + shift[...]
    summed = (
        branch * wide_spread(gate, per_image)
        + (shortcut[...] - average_p) * inverse_p * gain_p[...]
        + shift_p[...]
    )
    summed_out[...] = summed
    for one in (moments_out, gates_out, reduced_out, summed_out):
        one.send()
    block = silu(summed).astype(bf16)
    block_out[...] = block
    block_out.send()
    moved = dot(block, weight[...])
    moved_out[...] = moved
    moved_out.send()
    mask = mask_of(info, plane, plane, images)
    pixels = images_of(info, images) * per_image
    put_pair(pair_out, *local_moments(moved, mask, pixels))
    put_edges(first_out, last_out, moved, images, per_image, columns)


def put_edges(first_out, last_out, values, images, per_image, columns):
    first_out[...] = stack_rows(
        [values[image * per_image : image * per_image + columns] for image in range(images)]
    )
    last_out[...] = stack_rows(
        [values[(image + 1) * per_image - columns : (image + 1) * per_image] for image in range(images)]
    )


def extended(values, above, below, images, per_image, columns):
    parts = []
    for image in range(images):
        parts.append(above[image * columns : (image + 1) * columns])
        parts.append(values[image * per_image : (image + 1) * per_image])
        parts.append(below[image * columns : (image + 1) * columns])
    return stack_rows(parts)


def window_of(values, lift, images, per_image, columns):
    span = per_image + 2 * columns
    return stack_rows(
        [
            values[image * span + lift * columns : image * span + lift * columns + per_image]
            for image in range(images)
        ]
    )


def spatial_second(
    geometry,
    last,
    info,
    hidden,
    above,
    below,
    pairs,
    counts,
    gain,
    shift,
    weight,
    active_out,
    moved_out,
    moments_out,
    pair_out,
    first_out,
    last_out,
):
    images, rows, columns = geometry
    plane = images * rows * columns
    per_image = rows * columns
    width = hidden.shape[1]
    average, inverse, total = gathered_moments(pairs, counts[...] * 0.25, width // 128)
    moments_out[0:1] = average
    moments_out[1:2] = inverse
    moments_out[2:3] = jnp.broadcast_to(total, (1, width))
    moments_out[3:8] = jnp.zeros((5, width), f32)

    def active(values):
        return silu((values - average) * inverse * gain[...] + shift[...])

    top = active(above[...]) * jnp.where(info[1] > 0, 1.0, 0.0)
    bottom = active(below[...]) * jnp.where(info[1] < last, 1.0, 0.0)
    middle = active(hidden[...])
    active_out[...] = middle.astype(bf16)
    active_out.send()
    moments_out.send()
    middle = extended(middle, top, bottom, images, per_image, columns)
    by_column = (shifted(middle, 1, columns), middle, shifted(middle, -1, columns))
    moved = jnp.zeros((plane, width), f32)
    for tap_column in range(3):
        for tap_row in range(3):
            tap = 3 * tap_row + tap_column
            window = window_of(by_column[tap_column], tap_row, images, per_image, columns).astype(bf16)
            moved = moved + dot(window, weight[tap])
    moved_out[...] = moved
    moved_out.send()
    mask = mask_of(info, plane, plane, images)
    pixels = images_of(info, images) * per_image
    put_pair(pair_out, *local_moments(moved, mask, pixels))
    put_edges(first_out, last_out, moved, images, per_image, columns)


def finish_second(
    geometry,
    peers,
    area,
    info,
    hidden,
    block,
    out_grad,
    gain,
    shift,
    squeeze,
    excite,
    *rest,
):
    images, rows, columns = geometry
    plane = images * rows * columns
    per_image = rows * columns
    states = rest[:peers]
    moments_out, gates_out, reduced_out, mixed_out, grad_out, state_out = rest[peers:]
    average, inverse, total = finish_state(states, images, images)
    for row, value in enumerate((average, inverse, total)):
        moments_out[row : row + 1] = value
    moments_out[3:8] = jnp.zeros((5, average.shape[1]), f32)
    image_means, pooled, reduced, squeezed, gate = excited(
        states[0][0:images], area, average, inverse, gain[...], shift[...], squeeze[...], excite[...]
    )
    put_gates(gates_out, reduced_out, image_means, pooled, gate, reduced, squeezed)
    normed = (hidden[...] - average) * inverse
    summed = (normed * gain[...] + shift[...]) * wide_spread(gate, per_image) + block[...].astype(f32)
    mask = mask_of(info, plane, plane, images)
    logistic = jax.nn.sigmoid(summed)
    mixed_out[...] = (summed * logistic * mask).astype(bf16)
    for one in (moments_out, gates_out, reduced_out, mixed_out):
        one.send()
    grad = out_grad[...].astype(f32) * mask * (logistic * (1.0 + summed * (1.0 - logistic)))
    grad_out[...] = grad
    grad_out.send()
    put_image_sums(state_out, grad, normed, images, per_image)
    state_out[2 * images :] = jnp.zeros((state_out.shape[0] - 2 * images, grad.shape[1]), f32)


def put_image_sums(state_out, grad, normed, images, per_image):
    crossed = grad * normed
    for image in range(images):
        part = slice(image * per_image, (image + 1) * per_image)
        state_out[image : image + 1] = total_of(grad[part])
        state_out[images + image : images + image + 1] = total_of(crossed[part])


def excite_back(
    images,
    area,
    has_others,
    info,
    gain,
    shift,
    gates,
    reduced,
    squeeze,
    excite,
    mine,
    core_other,
    y_other,
    both_other,
    sums_out,
    pooled_grad_out,
    gate_grad_out,
    reduced_grad_out,
):
    state = (mine[...] + core_other[...]) + (y_other[...] + both_other[...])
    plain = state[0:images]
    crossed = state[images : 2 * images]
    image_means = gates[0:images]
    gate = gates[2 * images : 3 * images]
    gate_grad = gain[...] * crossed + shift[...] * plain
    before_gate = gate_grad * gate * (1.0 - gate)
    squeezed_grad = exact_dot(before_gate, excite[...], 1)
    reduced_grad = squeezed_grad * slope(reduced[0:images])
    pooled_grad = exact_dot(reduced_grad, squeeze[...], 1)
    pooled_grad_out[...] = pooled_grad / area
    gate_grad_out[...] = before_gate
    reduced_grad_out[...] = reduced_grad
    mask = (iota_rows(images) < info[0]).astype(f32)
    sums_out[0:1] = total_of(mask * (plain * gate + pooled_grad))
    sums_out[1:2] = total_of(mask * (crossed * gate + pooled_grad * image_means))
    if has_others:
        sums_out[2:3] = total_of(mask * plain)
        sums_out[3:4] = state[2 * images : 2 * images + 1]
    else:
        sums_out[2:4] = jnp.zeros((2, plain.shape[1]), f32)


def expand_back(
    geometry,
    peers,
    cut,
    info,
    grad,
    hidden,
    moments,
    gates,
    pooled_grad,
    gain,
    weight,
    middle,
    middle_moments,
    middle_gain,
    middle_shift,
    *rest,
):
    images, rows, columns = geometry
    plane = images * rows * columns
    per_image = rows * columns
    sums = rest[0][...]
    for other in rest[1:peers]:
        sums = sums + other[...]
    sums_out, mine_out, *rest = rest[peers:]
    theirs_out = rest.pop(0) if cut else None
    middle_grad_out, pair_out, first_out, last_out = rest
    sums_out[...] = sums
    mask = mask_of(info, plane, plane, images)
    average, inverse, total = moments[0:1], moments[1:2], moments[2:3]
    normed = (hidden[...] - average) * inverse
    upstream = grad[...] * wide_spread(gates[2 * images : 3 * images], per_image) + wide_spread(
        pooled_grad[...], per_image
    )
    low = norm_back(upstream, normed, inverse, gain[...], total, sums[0:1], sums[1:2], mask)
    if cut:
        put_halves(mine_out, theirs_out, low, cut, info)
    low = low.astype(bf16)
    if not cut:
        mine_out[...] = low
        mine_out.send()
    average, inverse = middle_moments[0:1], middle_moments[1:2]
    normed = (middle[...] - average) * inverse
    middle_grad = dot(low, weight[...], 1, 1) * slope(normed * middle_gain[...] + middle_shift[...])
    middle_grad_out[...] = middle_grad
    middle_grad_out.send()
    masked = middle_grad * mask
    put_pair(pair_out, total_of(masked), total_of(masked * normed))
    put_edges(first_out, last_out, middle_grad, images, per_image, columns)


def spatial_second_back(
    geometry,
    last,
    info,
    grad,
    grad_above,
    grad_below,
    hidden,
    above,
    below,
    moments,
    gain,
    pairs,
    weight,
    earlier,
    earlier_moments,
    earlier_gain,
    earlier_shift,
    sums_out,
    mine_out,
    theirs_out,
    earlier_grad_out,
    pair_out,
):
    images, rows, columns = geometry
    plane = images * rows * columns
    per_image = rows * columns
    width = hidden.shape[1]
    shift_part, gain_part = gathered_sums(pairs, width // 128)
    sums_out[0:1] = shift_part
    sums_out[1:2] = gain_part
    sums_out[2:8] = jnp.zeros((6, width), f32)
    mask = mask_of(info, plane, plane, images)
    edge_mask = mask_of(info, images * columns, images * columns, images)
    average, inverse, total = moments[0:1], moments[1:2], moments[2:3]

    def lowered(upstream, values, rows_mask):
        normed = (values - average) * inverse
        return norm_back(upstream, normed, inverse, gain[...], total, shift_part, gain_part, rows_mask)

    middle = lowered(grad[...], hidden[...], mask)
    put_halves(mine_out, theirs_out, middle, width, info)
    top = lowered(grad_above[...], above[...], edge_mask * jnp.where(info[1] > 0, 1.0, 0.0))
    bottom = lowered(grad_below[...], below[...], edge_mask * jnp.where(info[1] < last, 1.0, 0.0))
    middle = extended(middle, top, bottom, images, per_image, columns)
    by_column = (shifted(middle, -1, columns), middle, shifted(middle, 1, columns))
    moved = jnp.zeros((plane, width), f32)
    for tap_column in range(3):
        for tap_row in range(3):
            window = window_of(by_column[tap_column], 2 - tap_row, images, per_image, columns)
            moved = moved + dot(window.astype(bf16), weight[3 * tap_row + tap_column], 1, 1)
    normed = (earlier[...] - earlier_moments[0:1]) * earlier_moments[1:2]
    earlier_grad = moved * slope(normed * earlier_gain[...] + earlier_shift[...])
    earlier_grad_out[...] = earlier_grad
    earlier_grad_out.send()
    masked = earlier_grad * mask
    put_pair(pair_out, total_of(masked), total_of(masked * normed))


def reduce_second_back(
    geometry,
    info,
    grad,
    hidden,
    moments,
    gain,
    pairs,
    weight,
    carried,
    summed,
    wide_hidden,
    shortcut,
    wide_moments,
    sums_out,
    mine_out,
    theirs_out,
    summed_grad_out,
    state_out,
):
    images, rows, columns = geometry
    plane = images * rows * columns
    per_image = rows * columns
    width = hidden.shape[1]
    shift_part, gain_part = gathered_sums(pairs, width // 128)
    sums_out[0:1] = shift_part
    sums_out[1:2] = gain_part
    sums_out[2:8] = jnp.zeros((6, width), f32)
    mask = mask_of(info, plane, plane, images)
    normed = (hidden[...] - moments[0:1]) * moments[1:2]
    low = norm_back(
        grad[...], normed, moments[1:2], gain[...], moments[2:3], shift_part, gain_part, mask
    )
    put_halves(mine_out, theirs_out, low, width, info)
    low = low.astype(bf16)
    summed_grad = (carried[...] + dot(low, weight[...], 1, 1)) * slope(summed[...])
    summed_grad_out[...] = summed_grad
    summed_grad_out.send()
    normed = (wide_hidden[...] - wide_moments[0:1]) * wide_moments[1:2]
    put_image_sums(state_out, summed_grad, normed, images, per_image)
    other = (shortcut[...] - wide_moments[3:4]) * wide_moments[4:5]
    state_out[2 * images : 2 * images + 1] = total_of(summed_grad * mask * other)
    rest = state_out.shape[0] - 2 * images - 1
    state_out[2 * images + 1 :] = jnp.zeros((rest, summed_grad.shape[1]), f32)


def put_quarters(out, maps):
    at = 0
    for one in maps:
        width = one.shape[1] // 4
        for quarter in range(4):
            out[quarter, :, at : at + width] = one[:, quarter * width : (quarter + 1) * width]
        at += width


def shortcut_back(geometry, peers, info, grad, shortcut, moments, gain, weight, *rest):
    images, rows, columns = geometry
    plane = images * rows * columns
    sums = rest[0][...]
    for other in rest[1:peers]:
        sums = sums + other[...]
    low_out, image_out = rest[peers:]
    mask = mask_of(info, plane, plane, images)
    normed = (shortcut[...] - moments[3:4]) * moments[4:5]
    low = norm_back(
        grad[...], normed, moments[4:5], gain[...], moments[2:3], sums[2:3], sums[3:4], mask
    )
    low = low.astype(bf16)
    low_out[...] = low
    low_out.send()
    image_out[...] = dot(low, weight[...], 1, 1)


def spatial_first_back(
    geometry,
    last,
    info,
    grad,
    grad_below,
    hidden,
    below,
    moments,
    gain,
    pairs,
    weight,
    earlier,
    earlier_moments,
    earlier_gain,
    earlier_shift,
    sums_out,
    low_out,
    earlier_grad_out,
    pair_out,
):
    images, rows, columns = geometry
    plane = images * rows * columns
    per_image = rows * columns
    width = hidden.shape[1]
    shift_part, gain_part = gathered_sums(pairs, width // 128)
    sums_out[0:1] = shift_part
    sums_out[1:2] = gain_part
    sums_out[2:8] = jnp.zeros((6, width), f32)
    mask = mask_of(info, plane, plane, images)
    edge_mask = mask_of(info, images * columns, images * columns, images)
    average, inverse, total = moments[0:1], moments[1:2], moments[2:3]

    def lowered(upstream, values, rows_mask):
        normed = (values - average) * inverse
        return norm_back(upstream, normed, inverse, gain[...], total, shift_part, gain_part, rows_mask)

    middle = lowered(grad[...], hidden[...], mask)
    bottom = lowered(grad_below[...], below[...], edge_mask * jnp.where(info[1] < last, 1.0, 0.0))
    parts = []
    for image in range(images):
        parts.append(middle[image * per_image + columns : (image + 1) * per_image])
        parts.append(bottom[image * columns : (image + 1) * columns])
    lower = stack_rows(parts)
    here = middle.astype(bf16)
    low_out[...] = here
    low_out.send()
    here_right = shifted(middle, -1, columns).astype(bf16)
    next_right = shifted(lower, -1, columns).astype(bf16)
    lower = lower.astype(bf16)

    def back(window, tap_row, tap_column):
        return dot(window, weight[3 * tap_row + tap_column], 1, 1)

    planes = [
        back(here, 1, 1),
        back(here, 1, 2) + back(here_right, 1, 0),
        back(here, 2, 1) + back(lower, 0, 1),
        back(here, 2, 2) + back(here_right, 2, 0) + back(lower, 0, 2) + back(next_right, 0, 0),
    ]
    shift_sum = jnp.zeros((1, width), f32)
    gain_sum = jnp.zeros((1, width), f32)
    for number in range(4):
        at = slice(number * plane, (number + 1) * plane)
        normed = (earlier[at] - earlier_moments[0:1]) * earlier_moments[1:2]
        earlier_grad = planes[number] * slope(normed * earlier_gain[...] + earlier_shift[...])
        earlier_grad_out[at] = earlier_grad
        masked = earlier_grad * mask
        shift_sum = shift_sum + total_of(masked)
        gain_sum = gain_sum + total_of(masked * normed)
    put_pair(pair_out, shift_sum, gain_sum)


def reduce_first_back(
    geometry,
    info,
    grad,
    hidden,
    moments,
    gain,
    pairs,
    weight,
    image_part,
    sums_2,
    sums_3,
    sums_4,
    sums_5,
    sums_6,
    *rest,
):
    *lows, gain_grad_out, shift_grad_out, low_out, image_out = rest
    if lows:
        *maps, quarters_out = lows
        put_quarters(quarters_out, [one[...] for one in maps])
        quarters_out.send()
    images, rows, columns = geometry
    plane = images * rows * columns
    width = hidden.shape[1]
    shift_part, gain_part = gathered_sums(pairs, width // 128)
    at = 0
    for shift_row, gain_row in (
        (shift_part, gain_part),
        (sums_2[0:1], sums_2[1:2]),
        (sums_3[0:1], sums_3[1:2]),
        (sums_3[2:3], sums_3[3:4]),
        (sums_4[0:1], sums_4[1:2]),
        (sums_5[0:1], sums_5[1:2]),
        (sums_6[0:1], sums_6[1:2]),
    ):
        shift_grad_out[:, at : at + shift_row.shape[1]] = shift_row
        gain_grad_out[:, at : at + shift_row.shape[1]] = gain_row
        at += shift_row.shape[1]
    mask = mask_of(info, 4 * plane, plane, images)
    normed = (hidden[...] - moments[0:1]) * moments[1:2]
    low = norm_back(
        grad[...], normed, moments[1:2], gain[...], moments[2:3], shift_part, gain_part, mask
    ).astype(bf16)
    low_out[...] = low
    low_out.send()
    gain_grad_out.send()
    shift_grad_out.send()
    image_grad = dot(low, weight[...], 1, 1)
    image_grad = stack_rows([image_grad[:plane] + image_part[...], image_grad[plane:]]).astype(bf16)
    order = plane_order(4 * plane, images, rows, columns)
    image_out[...] = dot(order, image_grad, 0, 0).astype(bf16)


def unit(size):
    rows = lax.broadcasted_iota(jnp.int32, (size, size), 0)
    columns = lax.broadcasted_iota(jnp.int32, (size, size), 1)
    return (rows == columns).astype(bf16)


def turned(values, one):
    return dot(one, values, 1, 1).astype(bf16)


def outer_rows(inner, outer, out, base=0):
    width = out.shape[1]
    pieces = outer.shape[1] // width
    count = inner.shape[1]
    if pieces == 1:
        step = min(512, count)
        one = unit(step)
        for start in range(0, count, step):
            part = turned(inner[:, start : start + step], one)
            out[base + start : base + start + step] = dot(part, outer).astype(bf16)
        return
    step = 512 // pieces
    row = lax.broadcasted_iota(jnp.int32, (step * pieces, step), 0)
    column = lax.broadcasted_iota(jnp.int32, (step * pieces, step), 1)
    spreads = [(row == column * pieces + piece).astype(bf16) for piece in range(pieces)]
    stacked = stack_rows([outer[:, piece * width : (piece + 1) * width] for piece in range(pieces)])
    for start in range(0, count, step):
        part = inner[:, start : start + step]
        widened = [dot(spread, part, 1, 1).astype(bf16) for spread in spreads]
        result = dot(jnp.concatenate(widened, 1), stacked)
        out[base + start * pieces : base + (start + step) * pieces] = result.astype(bf16)


def weight_rows(inner, outer, out):
    outer_rows(inner[...], outer[...], out)


def two_parts(values):
    first = values.astype(bf16).astype(f32)
    return first, values - first


def left_parts(values):
    first, second = two_parts(values)
    return stack_rows([first, second, first]).astype(bf16)


def right_parts(values):
    first, second = two_parts(values)
    return stack_rows([first, first, second]).astype(bf16)


def gate_rows(images, share, pooled, reduced, gate_grad, reduced_grad, out, base=0):
    width = out.shape[1]
    squeezed = reduced[images : 2 * images]
    right = right_parts(reduced_grad[...] * share)
    units = reduced_grad.shape[1]
    rows = pooled.shape[2]
    for piece in range(pooled.shape[0]):
        part = dot(left_parts(pooled[piece]), right, 0, 0)
        out[base : base + rows, piece * units : (piece + 1) * units] = part.astype(bf16)
    wide_pieces = gate_grad.shape[1] // width
    row = lax.broadcasted_iota(jnp.int32, (units, units * wide_pieces), 0)
    column = lax.broadcasted_iota(jnp.int32, (units, units * wide_pieces), 1)
    left = left_parts(squeezed)
    right = right_parts(gate_grad[...] * share)
    result = jnp.zeros((units * wide_pieces, width), f32)
    for piece in range(wide_pieces):
        widened = dot(left, (column == row * wide_pieces + piece).astype(bf16)).astype(bf16)
        result = result + dot(widened, right[:, piece * width : (piece + 1) * width], 0, 0)
    out[base + rows : base + rows + units * wide_pieces] = result.astype(bf16)


def spatial_alone(geometry, info, active, above, below, outer, out):
    images, rows, columns = geometry
    per_image = rows * columns
    width = active.shape[1]

    def edge(values, at):
        parts = [values[image * per_image + at : image * per_image + at + columns] for image in range(images)]
        return stack_rows(parts).astype(f32)

    top = edge(above, per_image - columns) * jnp.where(info[1] > 0, 1.0, 0.0)
    bottom = edge(below, 0) * jnp.where(info[1] < info[4], 1.0, 0.0)
    middle = extended(active[...].astype(f32), top, bottom, images, per_image, columns)
    by_column = (shifted(middle, 1, columns), middle, shifted(middle, -1, columns))
    one = unit(width)
    for tap in range(9):
        window = window_of(by_column[tap % 3], tap // 3, images, per_image, columns).astype(bf16)
        out[tap * width : (tap + 1) * width] = dot(turned(window, one), outer[...]).astype(bf16)


def first_alone(geometry, info, active, above, outer, out):
    images, rows, columns = geometry
    per_image = rows * columns
    width = active.shape[1] // 4
    inside = jnp.where(info[1] > 0, 1.0, 0.0)
    one = unit(width)
    for tap in range(9):
        tap_row, tap_column = tap // 3, tap % 3
        number = (0 if tap_row == 1 else 2) + (0 if tap_column == 1 else 1)
        at = slice(number * width, (number + 1) * width)
        window = active[:, at].astype(f32)
        if tap_row == 0:
            parts = []
            for image in range(images):
                start = image * per_image
                parts.append(above[start + per_image - columns : start + per_image, at].astype(f32) * inside)
                parts.append(window[start : start + per_image - columns])
            window = stack_rows(parts)
        if tap_column == 0:
            window = shifted(window, 1, columns)
        out[tap * width : (tap + 1) * width] = dot(turned(window.astype(bf16), one), outer[...]).astype(bf16)


class Band:
    def __init__(self, rows, half, lines, xs):
        self.rows, self.half, self.lines, self.xs = rows, half, lines, xs

    def shapes(self):
        lines = len(self.lines)
        left = ((lines, len(self.xs), self.rows, self.half), bf16)
        right = ((lines, 2, self.rows, self.half), bf16)
        return [left, left, right, right]


def spot_of(info):
    return info[2], jnp.right_shift(info[1], 1), jnp.bitwise_and(info[1], 1)


def send_piece(band, spot, piece, source, place, refs, semaphores, used):
    x, y, core = spot
    line, x_of, y_of, core_of = piece >> 3, (piece >> 2) & 1, (piece >> 1) & 1, piece & 1
    if line not in band.lines or x_of not in band.xs:
        return []
    slot = band.lines.index(line)
    copies = []
    for half in range(2):
        mine = (y == y_of) if half == 0 else (x == x_of)
        inner = band.xs.index(x_of) if half == 0 else y_of
        columns = pl.ds(band.half * half, band.half)
        for kept in (True, False):
            target = refs[2 * half + (0 if kept else 1)].at[slot, inner, place]
            copy = pltpu.make_async_copy(source.at[:, columns], target, semaphores.at[used[0]])
            used[0] += 1
            wanted = mine if kept else jnp.logical_not(mine)
            if core is not None:
                wanted = jnp.logical_and(core == core_of, wanted)
            copies.append((wanted, copy))
    return copies


def send_rows(band, spot, source, base, first, last, refs, semaphores, used):
    copies = []
    for piece in range(first // band.rows, (last - 1) // band.rows + 1):
        start = max(first, piece * band.rows)
        stop = min(last, (piece + 1) * band.rows)
        held = source.at[pl.ds(base + start - first, stop - start)]
        place = pl.ds(start - piece * band.rows, stop - start)
        copies += send_piece(band, spot, piece, held, place, refs, semaphores, used)
    return copies


def conduct(copies, action):
    for wanted, copy in copies:

        def act(copy=copy):
            getattr(copy, action)()

        pl.when(wanted)(act)


def paired(own, other):
    return stack_rows([own[...], other[...]])


def merged_rows(values):
    return values[...].reshape(-1, values.shape[-1])


def half_of(values, width, info):
    first, second = [], []
    for start in range(0, values.shape[1], width):
        first.append(values[:, start : start + width // 2])
        second.append(values[:, start + width // 2 : start + width])
    low = jnp.right_shift(info[1], 1) == 0
    return jnp.where(low, jnp.concatenate(first, 1), jnp.concatenate(second, 1))


def place_rows(slice_rows, core, source, first, last, target, semaphores, used):
    copies = []
    for piece in range(first // slice_rows, (last - 1) // slice_rows + 1):
        start = max(first, piece * slice_rows)
        stop = min(last, (piece + 1) * slice_rows)
        held = source.at[pl.ds(start - first, stop - start)]
        place = pl.ds(start - piece * slice_rows, stop - start)
        target_rows = target.at[piece >> 2, (piece >> 1) & 1, place]
        copies.append(
            (core == (piece & 1), pltpu.make_async_copy(held, target_rows, semaphores.at[used[0]]))
        )
        used[0] += 1
    return copies


def plane_rows(values):
    return values[...].reshape(-1, values.shape[-1])


def line_place(info, line):
    return jnp.bitwise_and(info[3], 1) == (line & 1)


def either_copy(stays, source, kept, sent, semaphores, used):
    copies = []
    for wanted, target in ((stays, kept), (jnp.logical_not(stays), sent)):
        copies.append((wanted, pltpu.make_async_copy(source, target, semaphores.at[used[0]])))
        used[0] += 1
    return copies


def early_rows(starts, slice_rows, info, *rest):
    (
        active,
        planes,
        lows,
        pooled,
        reduced,
        reduced_other,
        gate_grad,
        reduced_grad,
        gate_grad_other,
        reduced_grad_other,
        kept,
        sent,
        gate_held,
        slices_held,
        semaphores,
    ) = rest
    core = jnp.bitwise_and(info[1], 1)
    quarter = 2 * info[2] + jnp.right_shift(info[1], 1)
    rows, width = slices_held.shape[1:]
    units = reduced.shape[1]
    images = reduced.shape[0] // 2
    pooled.wait(), gate_grad.wait(), gate_grad_other.wait()
    right = right_parts(paired(reduced_grad, reduced_grad_other))
    share = pooled.shape[0] // 4
    for number in range(share):
        part = dot(left_parts(pooled[quarter * share + number]), right, 0, 0)
        gate_held[0:units, number * units : (number + 1) * units] = part.astype(bf16)
    columns = pl.ds(pl.multiple_of(quarter * width, width), width)
    gate_held[units : 2 * units] = dot(
        left_parts(stack_rows([reduced[images:], reduced_other[images:]])),
        right_parts(stack_rows([gate_grad[:, columns], gate_grad_other[:, columns]])),
        0,
        0,
    ).astype(bf16)
    lowest = starts[0] // slice_rows
    count = slices_held.shape[0]
    numbers = range(count)
    found = {number: [] for number in numbers}
    skipped = -(starts[0] - lowest * slice_rows) % 16

    def pick(first, last, channels):
        near = [
            number
            for number in numbers
            if (lowest + 2 * number + 2) * slice_rows > first
            and (lowest + 2 * number) * slice_rows - skipped < last
        ]
        row = lax.broadcasted_iota(jnp.int32, (rows, channels), 0)
        column = lax.broadcasted_iota(jnp.int32, (rows, channels), 1)
        chosen = []
        for number in near:
            begin = (lowest + 2 * number + core) * slice_rows - first
            limit = slice_rows
            if number == 0:
                moved = jnp.where(core == 0, skipped, 0)
                begin = begin - moved
                limit = limit + moved
            wanted = jnp.logical_and(column == row + begin, row < limit)
            chosen.append(wanted.astype(f32))
        return near, stack_rows(chosen).astype(bf16)

    def add(near, result):
        for at, number in enumerate(near):
            found[number].append(result[at * rows : (at + 1) * rows])

    near, chosen = pick(starts[1], starts[2], 2 * units)
    add(near, dot(chosen, gate_held[...]))
    for first, last, inner, at in ((starts[0], starts[1], active, 0), (starts[2], starts[3], planes, 1)):
        near, chosen = pick(first, last, inner.shape[-1])
        left = dot(chosen, plane_rows(inner), 1, 1).astype(bf16)
        outer = lows[:, :, at * width : (at + 1) * width].reshape(-1, width)
        add(near, dot(left, outer))
    used = [0]
    copies = []
    for number in numbers:
        slices_held[number] = sum(found[number][1:], found[number][0]).astype(bf16)
        piece = lowest + 2 * number
        line, spot = piece >> 3, (piece >> 1) & 3
        slot = spot if line >= 2 else 4
        added = either_copy(
            line_place(info, line), slices_held.at[number], kept.at[slot], sent.at[slot], semaphores, used
        )
        conduct(added, "start")
        copies += added
    conduct(copies, "wait")


def late_rows(geometry, start, slice_rows, info, active, low, kept, sent, held, semaphores):
    images, _, columns = geometry
    core = jnp.bitwise_and(info[1], 1)
    width = active.shape[-1] // 4
    span = active.shape[1] // images
    rim = jnp.zeros((columns, width), bf16)

    def whole_images(values, columns_of):
        return [
            [values[first + number, image * span : (image + 1) * span, columns_of] for number in range(4)]
            for first in range(0, active.shape[0], 4)
            for image in range(images)
        ]

    def plane_of(number):
        return whole_images(active, slice(number * width, (number + 1) * width))

    def level(image_list):
        return stack_rows([part for parts in image_list for part in parts])

    def lifted(values, height):
        parts = []
        for at in range(0, values.shape[0], height):
            parts += [rim, values[at : at + height - columns]]
        return stack_rows(parts)

    outer = level(whole_images(low, slice(0, low.shape[-1])))
    turned_low = turned(outer, unit(outer.shape[1]))
    one = unit(width)
    height = 4 * span
    by_row = []
    for parity in (1, 0, 1):
        even, odd = level(plane_of(2 * parity)), level(plane_of(2 * parity + 1))
        by_row.append((shifted(odd.astype(f32), 1, columns).astype(bf16), even, odd))
    by_row[0] = tuple(lifted(values, height) for values in by_row[0])
    used = [0]
    copies = []
    for tap in range(9):
        product = dot(turned_low, by_row[tap // 3][tap % 3]).astype(bf16)
        held[tap * width : (tap + 1) * width] = turned(product, one)
        first = start + tap * width
        last = first + width
        for piece in range(first // slice_rows, (last - 1) // slice_rows + 1):
            begin, stop = max(first, piece * slice_rows), min(last, (piece + 1) * slice_rows)
            line, spot = piece >> 3, (piece >> 1) & 3
            place = pl.ds(begin - piece * slice_rows, stop - begin)
            added = either_copy(
                line_place(info, line),
                held.at[pl.ds(begin - start, stop - begin)],
                kept.at[spot, place],
                sent.at[spot, place],
                semaphores,
                used,
            )
            added = [(jnp.logical_and(core == (piece & 1), wanted), copy) for wanted, copy in added]
            conduct(added, "start")
            copies += added
    conduct(copies, "wait")


def pair_sums(info, kept, came, *outs):
    outs[0][...] = (kept[0:4].astype(f32) + came[0:4].astype(f32)).astype(bf16)
    outs[0].send()
    if len(outs) == 2:
        outs[1][...] = (kept[4].astype(f32) + came[4].astype(f32)).astype(bf16)


def owner_sums(info, kept, came, *rest):
    *others, first, second, third, fourth = rest
    quarter = 2 * info[2] + jnp.right_shift(info[1], 1)
    kept.wait(), came.wait()
    for number, out in enumerate((first, second, third, fourth)):
        total = kept[quarter ^ number].astype(f32) + came[quarter ^ number].astype(f32)
        if others:
            lower = others[0][...].astype(f32) + others[1][...].astype(f32)
            total = jnp.where(info[3] >= 2, total, lower)
        out[...] = total.astype(bf16)
        out.send()


def gate_slices(images, start, slice_rows, info, pooled, reduced, gate_grad, reduced_grad, target, held, half_held, semaphores):
    core = jnp.bitwise_and(info[1], 1)
    gate_rows(images, 1.0, pooled, reduced, gate_grad, reduced_grad, held)
    half_held[...] = half_of(held[...].astype(f32), held.shape[1], info).astype(bf16)
    last = start + held.shape[0]
    copies = place_rows(slice_rows, core, half_held, start, last, target, semaphores, [0])
    conduct(copies, "start")
    conduct(copies, "wait")


def whole_rows_of(start, slice_rows, info, active, low, target, held, semaphores):
    core = jnp.bitwise_and(info[1], 1)
    outer_rows(merged_rows(active), merged_rows(low), held)
    last = start + held.shape[0]
    copies = place_rows(slice_rows, core, held, start, last, target, semaphores, [0])
    conduct(copies, "start")
    conduct(copies, "wait")


def image_rows(values, image, images):
    span = values.shape[1] // images
    return [values[number, image * span : (image + 1) * span] for number in range(values.shape[0])]


def whole_spatial_rows(geometry, start, slice_rows, info, active, low, target, held, semaphores):
    images, _, columns = geometry
    core = jnp.bitwise_and(info[1], 1)
    used = [0]
    copies = []
    width = active.shape[-1]
    rim = jnp.zeros((columns, width), f32)
    outer, maps = [], []
    for image in range(images):
        outer += image_rows(low, image, images)
        parts = [part.astype(f32) for part in image_rows(active, image, images)]
        maps.append(stack_rows([rim] + parts + [rim]))
    outer = stack_rows(outer)
    span = maps[0].shape[0]
    every = stack_rows(maps)
    by_column = (shifted(every, 1, columns), every, shifted(every, -1, columns))
    by_column = [part.astype(bf16) for part in by_column]
    one = unit(width)
    for tap in range(9):
        tap_row, tap_column = tap // 3, tap % 3
        window = stack_rows(
            [
                by_column[tap_column][
                    image * span + tap_row * columns : (image + 1) * span - (2 - tap_row) * columns
                ]
                for image in range(images)
            ]
        )
        held[tap * width : (tap + 1) * width] = dot(turned(window, one), outer).astype(bf16)
        first = start + tap * width
        added = place_rows(
            slice_rows,
            core,
            held.at[pl.ds(tap * width, width)],
            first,
            first + width,
            target,
            semaphores,
            used,
        )
        conduct(added, "start")
        copies.extend(added)
    conduct(copies, "wait")


def reduce_rows(band, info, planes, planes_other, low, low_other, *rest):
    *targets, held, semaphores = rest
    spot = spot_of(info)
    outer_rows(paired(planes, planes_other), paired(low, low_other), held)
    copies = send_rows(band, spot, held, 0, 0, held.shape[0], targets, semaphores, [0])
    conduct(copies, "start")
    conduct(copies, "wait")


def second_halves(band, info, left, left_came, right, right_came, *outs):
    x, y = info[2], jnp.right_shift(info[1], 1)

    def total(first, second, slot, inner):
        return first[slot, inner].astype(f32) + second[slot, inner].astype(f32)

    outs = list(outs)
    split = len(band.xs) == 2
    left_outs = [outs.pop(0) for _ in range(2 if split else 1)]
    right_outs = outs
    left.wait(), left_came.wait(), right.wait(), right_came.wait()
    for slot in range(len(band.lines)):
        if split:
            left_outs[0][slot] = total(left, left_came, slot, x).astype(bf16)
            left_outs[1][slot] = total(left, left_came, slot, 1 - x).astype(bf16)
        else:
            left_outs[0][slot] = total(left, left_came, slot, 0).astype(bf16)
        right_outs[0][slot] = total(right, right_came, slot, y).astype(bf16)
        right_outs[1][slot] = total(right, right_came, slot, 1 - y).astype(bf16)


def line_halves(band, info, left, left_came, right, right_came, *outs):
    low = jnp.bitwise_and(info[3], 1)
    half = band.half

    def put(out, at, slot):
        out[at, :, 0:half] = (left[slot].astype(f32) + left_came[slot].astype(f32)).astype(bf16)
        out[at, :, half:] = (right[slot].astype(f32) + right_came[slot].astype(f32)).astype(bf16)

    left.wait(), left_came.wait(), right.wait(), right_came.wait()
    if len(band.lines) == 1:
        put(outs[0], 0, 0)
        return
    for at in range(len(band.lines) // 2):
        put(outs[0], at, 2 * at + low)
        put(outs[1], at, 2 * at + 1 - low)


def line_sum(band, info, own, came, *outs):
    if len(band.lines) < 4:
        outs[0][...] = (own[0].astype(f32) + came[0].astype(f32)).astype(bf16)
        return
    top = jnp.right_shift(info[3], 1)
    own.wait(), came.wait()
    for out, slot in zip(outs, (top, 1 - top)):
        out[...] = (own[slot].astype(f32) + came[slot].astype(f32)).astype(bf16)


class Loaded:
    def __init__(self, source, held, semaphore):
        self.held = held
        self.shape = held.shape
        self.copy = pltpu.make_async_copy(source, held, semaphore)
        self.copy.start()
        self.arrived = False

    def wait(self):
        if not self.arrived:
            self.copy.wait()
            self.arrived = True

    def __getitem__(self, index):
        self.wait()
        return self.held[index]


class Gathered:
    def __init__(self, sources, held, semaphores, places):
        self.held = held
        self.shape = held.shape
        self.copies = []
        for number, (source, place) in enumerate(zip(sources, places)):
            copy = pltpu.make_async_copy(source, held.at[place], semaphores.at[number])
            copy.start()
            self.copies.append(copy)

    def wait(self):
        for copy in self.copies:
            copy.wait()
        self.copies = []

    def __getitem__(self, index):
        self.wait()
        return self.held[index]


class PlanePair:
    def __init__(self, own, other, first=0, last=None):
        self.arrays = [own, other]
        self.first, self.last = first, own.shape[2] if last is None else last

    def part(self, first, last):
        return PlanePair(*self.arrays, first, last)


class Kept:
    def __init__(self, held, target, semaphore):
        self.held = held
        self.shape = held.shape
        self.copy = pltpu.make_async_copy(held, target, semaphore)
        self.sent = False

    def __setitem__(self, index, value):
        assert not self.sent
        self.held[index] = value

    def send(self):
        if not self.sent:
            self.copy.start()
            self.sent = True


def extent(shape, index):
    sizes = []
    for size, part in zip(shape, index):
        start, stop, _ = part.indices(size)
        sizes.append(stop - start)
    return tuple(sizes) + tuple(shape[len(index) :])


def bounded(ref, index):
    parts = []
    for size, part in zip(ref.shape, index):
        start, stop, _ = part.indices(size)
        parts.append(pl.ds(start, stop - start))
    return ref.at[tuple(parts)]


def run_rows(kernel, shapes, buffers, held, copies, *args, limit=64, after=(), cost=7):
    views = []
    for arg in args[1:]:
        if isinstance(arg, (list, PlanePair)):
            views.append((arg, None))
        else:
            views.append(arg if isinstance(arg, tuple) else (arg, ()))
    arrays = [args[0]]
    loaded_shapes, load_semaphores_of = [], []
    for source, index in views:
        if isinstance(source, PlanePair):
            arrays += source.arrays
            blocks = source.arrays[0].shape
            blocks = (2 * blocks[0], blocks[1], source.last - source.first)
            loaded_shapes.append(pltpu.VMEM(blocks, source.arrays[0].dtype))
            load_semaphores_of.append(blocks[0])
        elif index is None:
            arrays += source
            loaded_shapes.append(pltpu.VMEM((len(source),) + source[0].shape, source[0].dtype))
            load_semaphores_of.append(len(source))
        else:
            arrays.append(source)
            loaded_shapes.append(pltpu.VMEM(extent(source.shape, index), source.dtype))
            load_semaphores_of.append(1)
    loads = len(views)
    given_count = len(arrays)
    shapes = [jax.ShapeDtypeStruct(*one) for one in shapes]
    aliases = {}
    if buffers is not None:
        aliases = {len(arrays) + number: number for number in range(len(buffers))}
        arrays += list(buffers)
    arrays += list(after)
    inputs = len(arrays)

    def body(*refs):
        info, given = refs[0], refs[1:given_count]
        targets = refs[inputs : inputs + len(shapes)]
        rest = refs[inputs + len(shapes) :]
        load_semaphores = rest[loads]
        loaded, at, first = [], 0, 0
        for number in range(loads):
            argument, index = views[number]
            span = load_semaphores_of[number]
            semaphores = load_semaphores.at[pl.ds(first, span)]
            first += span
            if isinstance(argument, PlanePair):
                core = jnp.bitwise_and(info[1], 1)
                own, other = given[at : at + 2]
                columns = pl.ds(argument.first, argument.last - argument.first)
                sources = [
                    one.at[block, :, columns] for block in range(span // 2) for one in (own, other)
                ]
                places = [2 * block + place for block in range(span // 2) for place in (core, 1 - core)]
                loaded.append(Gathered(sources, rest[number], semaphores, places))
                at += 2
                continue
            if index is None:
                places = [info[1], info[1] ^ 2, info[1] ^ 1, info[1] ^ 3]
                loaded.append(Gathered(given[at : at + span], rest[number], semaphores, places))
                at += span
                continue
            source = given[at]
            if index:
                source = bounded(source, index)
            loaded.append(Loaded(source, rest[number], semaphores.at[0]))
            at += 1
        kernel(info, *loaded, *targets, *rest[loads + 1 :])
        for one in loaded:
            one.wait()

    anywhere = pl.BlockSpec(memory_space=pl.ANY)
    return pl.pallas_call(
        body,
        out_shape=shapes,
        in_specs=[pl.BlockSpec(memory_space=pltpu.SMEM)] + [anywhere] * (inputs - 1),
        out_specs=[anywhere] * len(shapes),
        scratch_shapes=loaded_shapes
        + [pltpu.SemaphoreType.DMA((sum(load_semaphores_of),))]
        + [pltpu.VMEM(shape, bf16) for shape in held]
        + [pltpu.SemaphoreType.DMA((copies,))],
        input_output_aliases=aliases,
        compiler_params=pltpu.CompilerParams(vmem_limit_bytes=limit << 20),
        cost_estimate=pl.CostEstimate(
            flops=cost * 10**9, bytes_accessed=cost * 3 * 10**6, transcendentals=0
        ),
    )(*arrays)


def run(kernel, outs, *args, scalars=1, limit=64, into=None, after=(), cost=7):
    views = [arg if isinstance(arg, tuple) else (arg, ()) for arg in args[scalars:]]
    arrays = list(args[:scalars]) + [array for array, _ in views]
    held = [pltpu.VMEM(extent(array.shape, index), array.dtype) for array, index in views]
    kept = [pltpu.VMEM(shape, dtype) for shape, dtype in outs]
    shapes = [jax.ShapeDtypeStruct(shape, dtype) for shape, dtype in outs]
    aliases = {}
    first_row = 0
    if into is not None:
        buffer, full, first_row = into
        shapes = [jax.ShapeDtypeStruct(full, outs[0][1])]
        if buffer is not None:
            aliases = {len(arrays): 0}
            arrays.append(buffer)
    single = len(shapes) == 1
    arrays += list(after)
    inputs, loads, results = len(arrays), len(views), len(outs)

    def body(*refs):
        given, targets = refs[:inputs], refs[inputs : inputs + results]
        rest = refs[inputs + results :]
        loaded_refs, kept_refs = rest[:loads], rest[loads : loads + results]
        load_semaphores, keep_semaphores = rest[loads + results :]
        order = sorted(range(loads), key=lambda number: held[number].shape and _size(held[number]))
        loaded = [None] * loads
        for number in order:
            source = given[scalars + number]
            index = views[number][1]
            if index:
                source = bounded(source, index)
            loaded[number] = Loaded(source, loaded_refs[number], load_semaphores.at[number])
        stored = []
        for number in range(results):
            target = targets[number]
            if into is not None:
                target = target.at[pl.ds(first_row, outs[0][0][0])]
            stored.append(Kept(kept_refs[number], target, keep_semaphores.at[number]))
        kernel(*given[:scalars], *loaded, *stored)
        for one in stored:
            one.send()
        for one in loaded:
            one.wait()
        for one in stored:
            one.copy.wait()

    anywhere = pl.BlockSpec(memory_space=pl.ANY)
    return pl.pallas_call(
        body,
        out_shape=shapes[0] if single else shapes,
        in_specs=[pl.BlockSpec(memory_space=pltpu.SMEM)] * scalars + [anywhere] * (inputs - scalars),
        out_specs=anywhere if single else [anywhere] * len(shapes),
        scratch_shapes=held
        + kept
        + [pltpu.SemaphoreType.DMA((max(loads, 1),)), pltpu.SemaphoreType.DMA((results,))],
        input_output_aliases=aliases,
        compiler_params=pltpu.CompilerParams(vmem_limit_bytes=limit << 20),
        cost_estimate=pl.CostEstimate(
            flops=cost * 10**9, bytes_accessed=cost * 3 * 10**6, transcendentals=0
        ),
    )(*arrays)


def following(array, others):
    def body(*refs):
        pass

    anywhere = pl.BlockSpec(memory_space=pl.ANY)
    return pl.pallas_call(
        body,
        out_shape=jax.ShapeDtypeStruct(array.shape, array.dtype),
        in_specs=[anywhere] * (1 + len(others)),
        out_specs=anywhere,
        input_output_aliases={0: 0},
    )(array, *others)


def _size(ref):
    total = jnp.dtype(ref.dtype).itemsize
    for one in ref.shape:
        total *= one
    return total


def exchanged(payload):
    return lax.all_to_all(payload, everywhere, 0, 0, tiled=True)


def swapped(shard, wide_bits, narrow_bits):
    wide, narrow = lax.axis_size("wide"), lax.axis_size("narrow")
    if not wide_bits:
        return lax.ppermute(shard, "narrow", [(i, i ^ narrow_bits) for i in range(narrow)])
    if not narrow_bits:
        return lax.ppermute(shard, "wide", [(i, i ^ wide_bits) for i in range(wide)])
    pairs = [
        (w * narrow + n, (w ^ wide_bits) * narrow + (n ^ narrow_bits))
        for w in range(wide)
        for n in range(narrow)
    ]
    return lax.ppermute(shard, everywhere, pairs)


def handed(shard, by):
    peers = lax.axis_size("narrow")
    pairs = [(i, i + by) for i in range(peers) if 0 <= i + by < peers]
    return lax.ppermute(shard, "narrow", pairs)


def later_stages():
    peers = lax.axis_size("wide")
    steps, bit = [], 2
    while bit < peers:
        if 2 * bit < peers:
            steps.append((bit, 2 * bit, 3 * bit))
            bit *= 4
        else:
            steps.append((bit,))
            bit *= 2
    return steps


def merged_state(images, state):
    def combined(state, others, adders):
        return run(
            functools.partial(merge_states, images, adders),
            [(state.shape, f32)],
            state,
            *others,
            scalars=0,
        )

    state = combined(state, [swapped(state, 0, 1)], (1,))
    others = [swapped(state, 0, 2), swapped(state, 1, 0), swapped(state, 1, 2)]
    state = combined(state, others, (1,))
    stages = later_stages()
    for step in stages[:-1]:
        state = combined(state, [swapped(state, bits, 0) for bits in step], ())
    return [state] + [swapped(state, bits, 0) for bits in stages[-1]]


def wide_parts(sums):
    sums = sums + swapped(sums, 1, 0)
    stages = later_stages()
    for step in stages[:-1]:
        sums = sum([swapped(sums, bits, 0) for bits in step], sums)
    return [sums] + [swapped(sums, bits, 0) for bits in stages[-1]]


def swapped_once(shard, axis, bits, sender, only=None):
    peers = lax.axis_size(axis)
    pairs = [(i, i ^ bits) for i in range(peers) if bool(i & bits) == sender]
    if only is not None:
        pairs = [pair for pair in pairs if pair[1] in only]
    return lax.ppermute(shard, axis, pairs)


class Transfer:
    def __init__(self, band, info, arrays):
        self.band, self.info = band, info
        self.split = len(band.xs) == 2
        self.left, left_sent, self.right, right_sent = arrays
        self.left_came, self.right_came = swapped(left_sent, 0, 2), self.along_x(right_sent)

    def along_x(self, shard):
        return swapped(shard, 1, 0) if self.split else swapped_once(shard, "wide", 1, True)

    def second(self, after=()):
        band = self.band
        flat = ((len(band.lines), band.rows, band.half), bf16)
        outs = run(
            functools.partial(second_halves, band),
            [flat] * (4 if self.split else 3),
            self.info,
            self.left,
            self.left_came,
            self.right,
            self.right_came,
            after=after,
        )
        self.left, left_sent = outs[0], outs[1 if self.split else 0]
        self.right, right_sent = outs[-2], outs[-1]
        self.left_came, self.right_came = self.along_x(left_sent), swapped(right_sent, 0, 2)
        return (outs[0],)

    def third(self, after=()):
        band = self.band
        count = max(len(band.lines) // 2, 1)
        shape = ((count, band.rows, 2 * band.half), bf16)
        outs = run(
            functools.partial(line_halves, band),
            [shape] * min(len(band.lines), 2),
            self.info,
            self.left,
            self.left_came,
            self.right,
            self.right_came,
            after=after,
        )
        if len(band.lines) > 1:
            self.own, self.came = outs[0], swapped(outs[1], 2, 0)
        else:
            self.own, self.came = outs, swapped_once(outs, "wide", 2, True)
        return (self.own,)

    def fourth(self, after=()):
        band = self.band
        shape = ((band.rows, 2 * band.half), bf16)
        outs = run(
            functools.partial(line_sum, band),
            [shape] * (2 if len(band.lines) == 4 else 1),
            self.info,
            self.own,
            self.came,
            after=after,
        )
        if len(band.lines) == 4:
            self.own, self.came = outs[0], swapped(outs[1], 4, 0)
        else:
            only = [2 * line + x for line in band.lines for x in band.xs]
            self.own, self.came = outs, swapped_once(outs, "wide", 4, band.lines[0] < 2, only)
        return (self.own,)

    def result(self):
        return self.own.astype(f32) + self.came.astype(f32)


class PlaneTransfer:
    def __init__(self, info, kept, sent, upward):
        self.info, self.kept, self.upward = info, kept, upward
        self.came = swapped(sent, 2, 0)
        self.extra = ()

    def third(self, after=()):
        slots = self.kept.shape[0]
        shapes = [((4,) + self.kept.shape[1:], bf16)]
        if slots > 4:
            shapes.append((self.kept.shape[1:], bf16))
        outs = run(pair_sums, shapes, self.info, self.kept, self.came, after=after)
        if slots > 4:
            self.extra = (outs[1], swapped_once(outs[1], "wide", 4, self.upward, [2, 3]))
            outs = outs[0]
        self.kept, self.came = outs, swapped_once(outs, "wide", 4, not self.upward)
        return (outs,)

    def fourth(self, after=()):
        shapes = [(self.kept.shape[1:], bf16)] * 4
        outs = run(owner_sums, shapes, self.info, self.kept, self.came, *self.extra, after=after)
        self.parts = [outs[0], swapped(outs[1], 0, 2), swapped(outs[2], 1, 0), swapped(outs[3], 1, 2)]
        return (outs[0],)

    def result(self):
        quarter = 2 * self.info[2] + jnp.right_shift(self.info[1], 1)
        columns = [lax.select_n(quarter ^ number, *self.parts) for number in range(4)]
        return jnp.concatenate(columns, 1).astype(f32)


def swept(mine, info):
    low = info[1] < 2
    kept = jnp.where(low, mine[0], mine[1])
    came = swapped(jnp.where(low, mine[1], mine[0]), 0, 2)
    halves = [jnp.where(low, kept, came), jnp.where(low, came, kept)]
    return jnp.concatenate(halves, 1).astype(f32)


def scattered(rows, devices):
    done = lax.psum_scatter(rows, everywhere, scatter_dimension=0, tiled=True)
    return done.astype(f32).reshape(-1)


def on_device(
    images,
    first_reduce,
    first_spatial,
    first_expand,
    first_squeeze,
    first_excite,
    first_project,
    second_reduce,
    second_spatial,
    second_expand,
    second_squeeze,
    second_excite,
    norm_gains,
    norm_shifts,
    image_counts,
    out_grad,
):
    wide, narrow = lax.axis_size("wide"), lax.axis_size("narrow")
    assert narrow == 4
    devices = wide * narrow
    count, rows_in, cols_in, channels = images.shape
    rows, columns = rows_in // 2, cols_in // 2
    geometry = (count, rows, columns)
    plane = count * rows * columns
    edge = count * columns
    area = rows * columns * narrow
    last = narrow - 1
    mid = first_reduce.shape[1]
    out = first_expand.shape[1]
    chunks = mid // 128
    place = lax.axis_index("wide").astype(jnp.int32)
    info = jnp.stack(
        [
            image_counts[0],
            lax.axis_index("narrow").astype(jnp.int32),
            jnp.bitwise_and(place, 1),
            jnp.right_shift(place, 1),
            jnp.full((), narrow - 1, jnp.int32),
        ]
    )
    widths = [mid, mid, out, out, mid, mid, out]
    gains, shifts, at = [], [], 0
    for width in widths:
        part = (slice(0, 1), slice(at, at + width))
        gains.append((norm_gains[None], part))
        shifts.append((norm_shifts[None], part))
        at += width
    pair = ((devices, 2 * chunks, 128), f32)
    small = ((8, mid), f32)
    large = ((8, out), f32)
    edge_map = ((edge, mid), f32)
    taps = (9, mid, mid)
    spatial_one = first_spatial.reshape(taps)
    spatial_two = second_spatial.reshape(taps)
    bind = functools.partial

    planes, h1, pairs, edges = run(
        bind(reduce_first, geometry),
        [
            ((4 * plane, channels), bf16),
            ((4 * plane, mid), f32),
            ((devices, 2 * chunks + 8, 128), f32),
            ((2 * edge, mid), f32),
        ],
        info,
        images.reshape(4 * plane, channels),
        first_reduce,
    )
    halo = handed(edges, 1)
    pairs = exchanged(pairs)
    squeeze_rows = 2 * out * second_squeeze.shape[1] // mid
    first_rows = [0, channels, channels + 9 * mid]
    first_rows.append(first_rows[2] + out)
    first_rows.append(first_rows[3] + squeeze_rows)
    whole_rows = first_rows[4] + channels * out // mid
    second_rows = [0, out, out + 9 * mid, 2 * out + 9 * mid]
    second_shape = (second_rows[3] + squeeze_rows, mid)
    slice_rows = whole_rows // devices
    second_slice = second_shape[0] // devices
    by_hand = wide == 8 and slice_rows % 16 == 0 and second_slice % 16 == 0
    planes_other = swapped(planes, 0, 1)
    hp, moments_p = run(
        bind(project_first, geometry), [((plane, out), f32), large], info, planes, first_project
    )
    a1, h2, moments_1, counts, pairs, edges = run(
        bind(spatial_first, geometry),
        [
            ((plane, 4 * mid), bf16),
            ((plane, mid), f32),
            small,
            ((devices, 128), f32),
            pair,
            ((edge, mid), f32),
        ],
        info,
        h1,
        halo,
        pairs,
        gains[0],
        shifts[0],
        spatial_one,
    )
    h2_below = handed(edges, -1)
    pairs = exchanged(pairs)
    xs = (planes, (slice(0, plane),))
    a2, h3, moments_2, state, pack = run(
        bind(expand_packing, geometry, 2, True),
        [
            ((plane, mid), bf16),
            ((plane, out), f32),
            small,
            large,
            ((plane, 5 * mid + channels), bf16),
        ],
        info,
        a1,
        xs,
        h2,
        pairs,
        counts,
        gains[1],
        shifts[1],
        first_expand,
        moments_p,
        after=(h2_below,),
    )
    if by_hand:
        groups = [[first + number for number in range(8)] for first in range(0, devices, 8)]
        pack = lax.all_gather(pack, everywhere, axis_index_groups=groups)
        at = [0, 4 * mid, 4 * mid + channels, 5 * mid + channels]
        a1_plane, xs_plane, a2_plane = [
            (pack, (slice(0, 8), slice(0, plane), slice(at[number], at[number + 1])))
            for number in range(3)
        ]

    def spread(parts, after):
        cores = [group[core::2] for group in groups for core in range(2)]
        own = lax.all_to_all(parts, everywhere, 0, 0, axis_index_groups=cores, tiled=True)
        own = following(own, after)
        return PlanePair(own, swapped(own, 0, 1))

    states = merged_state(count, state)
    moments_3, gates_1, reduced_1, r1, o1, k1, pairs, firsts, lasts = run(
        bind(reduce_second, geometry, len(states), area),
        [
            large,
            ((3 * count, out), f32),
            ((2 * count, first_squeeze.shape[1]), f32),
            ((plane, out), f32),
            ((plane, out), bf16),
            ((plane, mid), f32),
            pair,
            edge_map,
            edge_map,
        ],
        info,
        h3,
        hp,
        gains[2],
        shifts[2],
        gains[3],
        shifts[3],
        first_squeeze,
        first_excite,
        second_reduce,
        *states,
        after=(planes_other,) if by_hand else (),
    )
    k1_above, k1_below = handed(lasts, 1), handed(firsts, -1)
    pairs = exchanged(pairs)
    a3, k2, moments_4, pairs, firsts, lasts = run(
        bind(spatial_second, geometry, last),
        [((plane, mid), bf16), ((plane, mid), f32), small, pair, edge_map, edge_map],
        info,
        k1,
        k1_above,
        k1_below,
        pairs,
        counts,
        gains[4],
        shifts[4],
        spatial_two,
    )
    k2_above, k2_below = handed(lasts, 1), handed(firsts, -1)
    pairs = exchanged(pairs)

    pack_widths = [out, mid, mid]
    a4, k3, moments_5, state, pack = run(
        bind(expand_packing, geometry, 2, False),
        [
            ((plane, mid), bf16),
            ((plane, out), f32),
            small,
            large,
            ((plane, sum(pack_widths)), bf16),
        ],
        info,
        o1,
        a3,
        k2,
        pairs,
        counts,
        gains[5],
        shifts[5],
        second_expand,
        after=(k2_above, k2_below),
    )
    pack = lax.all_gather(pack, "narrow")
    packed, at = [], 0
    for width in pack_widths:
        packed.append((pack, (slice(0, narrow), slice(0, plane), slice(at, at + width))))
        at += width
    o1_all, a3_all, a4_all = packed

    def gathered_halves(mine, theirs):
        came = swapped(theirs, 0, 2)
        return [mine, came, swapped(mine, 0, 1), swapped(came, 0, 1)]

    def joined(mine, theirs, width):
        low = info[1] < 2
        first, second = jnp.where(low, mine, theirs), jnp.where(low, theirs, mine)
        parts = [one.reshape(plane, -1, width // 2) for one in (first, second)]
        return jnp.concatenate(parts, 2).reshape(plane, -1)

    states = merged_state(count, state)
    if by_hand:
        units = first_squeeze.shape[1]
        pooled = gates_1[count : 2 * count]
        pooled = jnp.concatenate([pooled, swapped(pooled, 1, 0)], 0)
        pooled = pooled.reshape(2 * count, -1, out // units).transpose(2, 0, 1)
        reduced_other = swapped(reduced_1, 1, 0)
    moments_6, gates_2, reduced_2, mixed, dr2, state = run(
        bind(finish_second, geometry, len(states), area),
        [
            large,
            ((3 * count, out), f32),
            ((2 * count, second_squeeze.shape[1]), f32),
            ((plane, out), bf16),
            ((plane, out), f32),
            large,
        ],
        info,
        k3,
        o1,
        out_grad.reshape(plane, out),
        gains[6],
        shifts[6],
        second_squeeze,
        second_excite,
        *states,
        after=(a1_plane[0], pooled, reduced_other) if by_hand else (),
    )

    def excitation_back(state, has_others, number, gates, reduced, squeeze, excite):
        sums, pooled_grad, gate_grad, reduced_grad = run(
            bind(excite_back, count, area, has_others),
            [
                ((4, out), f32),
                ((count, out), f32),
                ((count, out), f32),
                ((count, squeeze.shape[1]), f32),
            ],
            info,
            gains[number],
            shifts[number],
            gates,
            reduced,
            squeeze,
            excite,
            state,
            swapped(state, 0, 1),
            swapped(state, 0, 2),
            swapped(state, 0, 3),
        )
        pooled = gates[count : 2 * count].reshape(count, -1, mid // squeeze.shape[1])
        return wide_parts(sums), pooled_grad, (pooled.transpose(2, 0, 1), reduced, gate_grad, reduced_grad)

    parts, pooled_grad, saved_two = excitation_back(
        state, False, 6, gates_2, reduced_2, second_squeeze, second_excite
    )
    half_out, half_mid = ((plane, out // 2), bf16), ((plane, mid // 2), bf16)
    back_outs = [((4, out), f32), half_out, half_out, ((plane, mid), f32), pair, edge_map, edge_map]
    sums_6, dk3_mine, dk3_theirs, du5, pairs, firsts, lasts = run(
        bind(expand_back, geometry, len(parts), mid),
        back_outs,
        info,
        dr2,
        k3,
        moments_6,
        gates_2,
        pooled_grad,
        gains[6],
        second_expand,
        k2,
        moments_5,
        gains[5],
        shifts[5],
        *parts,
    )
    du5_above, du5_below = handed(lasts, 1), handed(firsts, -1)
    pairs = exchanged(pairs)
    share = 1.0 / narrow
    if by_hand:
        second_shapes = [((wide, 2, second_slice, mid // 2), bf16)]
        second_sent = run_rows(
            bind(gate_slices, count, second_rows[3], second_slice),
            second_shapes,
            None,
            [(squeeze_rows, mid), (squeeze_rows, mid // 2)],
            16,
            info,
            *saved_two,
            cost=1,
        )
        tie = second_sent[:1]
    else:
        tie = ()
        second_flat = run(
            weight_rows,
            [((out, mid), bf16)],
            a4,
            joined(dk3_mine, dk3_theirs, mid),
            scalars=0,
            into=(None, second_shape, second_rows[2]),
        )
        second_flat = run(
            bind(gate_rows, count, share),
            [((squeeze_rows, mid), bf16)],
            *saved_two,
            scalars=0,
            into=(second_flat, second_shape, second_rows[3]),
        )
    sums_5, dk2_mine, dk2_theirs, du4, pairs = run(
        bind(spatial_second_back, geometry, last),
        [small, half_mid, half_mid, ((plane, mid), f32), pair],
        info,
        du5,
        du5_above,
        du5_below,
        k2,
        k2_above,
        k2_below,
        moments_5,
        gains[5],
        pairs,
        spatial_two,
        k1,
        moments_4,
        gains[4],
        shifts[4],
    )
    pairs = exchanged(pairs)
    if by_hand:
        second_sent = run_rows(
            bind(whole_rows_of, second_rows[2], second_slice),
            second_shapes,
            second_sent,
            [(out, mid // 2)],
            16,
            info,
            a4_all,
            gathered_halves(dk3_mine, dk3_theirs),
        )
        tie = second_sent
    else:
        tie = ()
    sums_4, dk1_mine, dk1_theirs, dr1, state = run(
        bind(reduce_second_back, geometry),
        [small, half_mid, half_mid, ((plane, out), f32), large],
        info,
        du4,
        k1,
        moments_4,
        gains[4],
        pairs,
        second_reduce,
        dr2,
        r1,
        h3,
        hp,
        moments_3,
        after=tuple(second_sent) if by_hand else (),
    )
    parts, pooled_grad, saved_one = excitation_back(
        state, True, 2, gates_1, reduced_1, first_squeeze, first_excite
    )
    if by_hand:
        second_sent = run_rows(
            bind(whole_spatial_rows, geometry, second_rows[1], second_slice),
            second_shapes,
            second_sent,
            [(9 * mid, mid // 2)],
            9 * 3,
            info,
            a3_all,
            gathered_halves(dk2_mine, dk2_theirs),
            after=(pooled_grad,),
        )
        tie = second_sent[:1]
    else:
        second_flat = run(
            bind(spatial_alone, geometry),
            [((9 * mid, mid), bf16)],
            info,
            a3,
            handed(a3, 1),
            handed(a3, -1),
            joined(dk2_mine, dk2_theirs, mid),
            into=(second_flat, second_shape, second_rows[1]),
        )
    if by_hand:
        second_sent = run_rows(
            bind(whole_rows_of, 0, second_slice),
            second_shapes,
            second_sent,
            [(out, mid // 2)],
            16,
            info,
            o1_all,
            gathered_halves(dk1_mine, dk1_theirs),
        )
        second_halves_summed = lax.psum_scatter(
            second_sent[0], "wide", scatter_dimension=0, tiled=False
        )
        tie = second_sent
    else:
        second_flat = run(
            weight_rows,
            [((out, mid), bf16)],
            o1,
            joined(dk1_mine, dk1_theirs, mid),
            scalars=0,
            into=(second_flat, second_shape, second_rows[0]),
        )
        second_done = scattered(second_flat, devices)
    sums_3, dh3, du2, pairs, firsts, _ = run(
        bind(expand_back, geometry, len(parts), 0),
        [((4, out), f32), ((plane, out), bf16), ((plane, mid), f32), pair, edge_map, edge_map],
        info,
        dr1,
        h3,
        moments_3,
        gates_1,
        pooled_grad,
        gains[2],
        first_expand,
        h2,
        moments_2,
        gains[1],
        shifts[1],
        *parts,
        after=tuple(second_sent) if by_hand else (),
    )
    du2_below = handed(firsts, -1)
    pairs = exchanged(pairs)
    dhp, image_part = run(
        bind(shortcut_back, geometry, len(parts)),
        [((plane, out), bf16), ((plane, channels), f32)],
        info,
        dr1,
        hp,
        moments_3,
        gains[3],
        first_project,
        *parts,
        after=(du2,),
    )
    if by_hand:
        pieces = out // mid
        wide_slice = slice_rows // pieces
        held_rows = -(-wide_slice // 16) * 16
        corner = Band(slice_rows, mid // 2, [0], [0])
        wide_rows = [one // pieces for one in first_rows[2:] + [whole_rows]]
        lowest = wide_rows[0] // wide_slice
        shared = wide_rows[0] - lowest * wide_slice
        skipped = -shared % 16
        assert channels <= 4 * slice_rows and lowest == devices // 2 - 2
        assert wide_slice + skipped <= held_rows
        tie = (image_part,)
    else:
        tie = ()
        first_shape = (whole_rows, mid)
        first_flat = run(
            weight_rows,
            [((out, mid), bf16)],
            a2,
            dh3,
            scalars=0,
            into=(None, first_shape, first_rows[2]),
        )
        first_flat = run(
            bind(gate_rows, count, share),
            [((squeeze_rows, mid), bf16)],
            *saved_one,
            scalars=0,
            into=(first_flat, first_shape, first_rows[3]),
        )
        first_flat = run(
            weight_rows,
            [((channels * out // mid, mid), bf16)],
            (planes, (slice(0, plane),)),
            dhp,
            scalars=0,
            into=(first_flat, first_shape, first_rows[4]),
        )
    sums_2, dh2, du1, pairs = run(
        bind(spatial_first_back, geometry, last),
        [small, ((plane, mid), bf16), ((4 * plane, mid), f32), pair],
        info,
        du2,
        du2_below,
        h2,
        h2_below,
        moments_2,
        gains[1],
        pairs,
        spatial_one,
        h1,
        moments_1,
        gains[0],
        shifts[0],
        after=tie,
    )
    pairs = exchanged(pairs)
    if by_hand:
        tie = ()
    else:
        first_flat = run(
            bind(first_alone, geometry),
            [((9 * mid, mid), bf16)],
            info,
            a1,
            handed(a1, 1),
            dh2,
            into=(first_flat, first_shape, first_rows[1]),
        )
    channel_row = ((1, norm_gains.shape[0]), f32)
    quarters = [((4, plane, out // 2 + mid // 4), bf16)] if by_hand else []
    *quarters, gain_grad, shift_grad, dh1, image_grad = run(
        bind(reduce_first_back, geometry),
        quarters
        + [channel_row, channel_row, ((4 * plane, mid), bf16), ((4 * plane, channels), bf16)],
        info,
        du1,
        h1,
        moments_1,
        gains[0],
        pairs,
        first_reduce,
        image_part,
        sums_2,
        sums_3,
        sums_4,
        sums_5,
        sums_6,
        *((dh3, dhp, dh2) if by_hand else ()),
        after=tie,
    )
    if by_hand:
        corner_sent = run_rows(
            bind(reduce_rows, corner),
            corner.shapes(),
            None,
            [(channels, mid)],
            16,
            info,
            planes,
            planes_other,
            dh1,
            swapped(dh1, 0, 1),
        )
        final = Transfer(corner, info, corner_sent)
        lows_plane = spread(quarters[0], corner_sent[:1])
        units = first_squeeze.shape[1]
        slots = ((5, held_rows, out // 4), bf16)
        upper_sent = run_rows(
            bind(early_rows, wide_rows, wide_slice),
            [slots, slots],
            None,
            [(2 * units, out // 4), ((devices - lowest) // 2, held_rows, out // 4)],
            devices - lowest,
            info,
            a2_plane,
            xs_plane,
            lows_plane.part(0, out // 2),
            pooled,
            reduced_1,
            reduced_other,
            *saved_one[2:],
            swapped(saved_one[2], 1, 0),
            swapped(saved_one[3], 1, 0),
        )
        early = PlaneTransfer(info, *upper_sent, True)
        slots = ((4, slice_rows, mid // 4), bf16)
        lower_sent = run_rows(
            bind(late_rows, geometry, first_rows[1], slice_rows),
            [slots, slots],
            None,
            [(9 * mid, mid // 4)],
            9 * 3 * 2,
            info,
            a1_plane,
            lows_plane.part(out // 2, out // 2 + mid // 4),
            after=(upper_sent[0], second_halves_summed),
        )
        late = PlaneTransfer(info, *lower_sent, False)
        tie = final.second(lower_sent[:1])
        second_done = swept(second_halves_summed, info)
        tie = early.third(tie)
        tie = final.third(tie)
        tie = late.third(tie)
        tie = final.fourth(tie)
        tie = early.fourth(tie)
        late.fourth(tie + (second_done,))
        upper_done, lower_done, corner_done = early.result(), late.result(), final.result()
        piece = place * narrow + info[1]
        row = piece * slice_rows + lax.iota(jnp.int32, slice_rows)
        lower_done = jnp.where(row[:, None] < channels, corner_done, lower_done)
        mixed_rows = jnp.concatenate(
            [
                lower_done[: shared * pieces].reshape(shared, out),
                upper_done[shared + skipped : wide_slice + skipped],
            ],
            0,
        )
        first_done = jnp.where(
            piece < lowest,
            lower_done.reshape(-1),
            jnp.where(piece == lowest, mixed_rows, upper_done[:wide_slice]).reshape(-1),
        )
        second_done = second_done.reshape(-1)
    else:
        first_flat = run(
            weight_rows,
            [((channels, mid), bf16)],
            planes,
            dh1,
            scalars=0,
            into=(first_flat, first_shape, 0),
        )
        first_done = scattered(first_flat, devices)
    return (
        mixed.reshape(out_grad.shape),
        image_grad.reshape(images.shape),
        first_done,
        second_done,
        gain_grad.reshape(-1),
        shift_grad.reshape(-1),
    )


def solution(mesh):
    in_specs = (
        (P("wide", "narrow", None, None),) + (P(),) * 13 + (P("wide"), P("wide", "narrow", None, None))
    )
    out_specs = (
        P("wide", "narrow", None, None),
        P("wide", "narrow", None, None),
        P(everywhere),
        P(everywhere),
        P(),
        P(),
    )
    return jax.shard_map(
        on_device, mesh=mesh, in_specs=in_specs, out_specs=out_specs, check_vma=False
    )
```

```python
import functools

import jax
import jax.numpy as jnp
from jax import lax
from jax.experimental import pallas as pl
from jax.experimental.pallas import tpu as pltpu
from jax.sharding import PartitionSpec as P

epsilon = 1e-05
highest = lax.Precision.HIGHEST
f32 = jnp.float32
bf16 = jnp.bfloat16
everywhere = ("wide", "narrow")


def iota_rows(rows, columns=1):
    return lax.broadcasted_iota(jnp.int32, (rows, columns), 0)


def dot(left, right, left_dim=1, right_dim=0):
    return lax.dot_general(
        left, right, (((left_dim,), (right_dim,)), ((), ())), preferred_element_type=f32
    )


def exact_dot(values, weight, weight_dim=0):
    first = values.astype(bf16)
    rest = values - first.astype(f32)
    second = rest.astype(bf16)
    third = (rest - second.astype(f32)).astype(bf16)
    rows = values.shape[0]
    product = dot(
        jnp.concatenate([first.astype(f32), second.astype(f32), third.astype(f32)], 0).astype(bf16),
        weight,
        1,
        weight_dim,
    )
    return product[:rows] + product[rows : 2 * rows] + product[2 * rows : 3 * rows]


def slope(values):
    logistic = jax.nn.sigmoid(values)
    return logistic * (1.0 + values * (1.0 - logistic))


def silu(values):
    return values * jax.nn.sigmoid(values)


def total_of(values):
    return jnp.sum(values, axis=0, keepdims=True)


def mask_of(info, rows, plane, images):
    per_image = plane // images
    index = iota_rows(rows)
    if rows > plane:
        index = jnp.bitwise_and(index, plane - 1)
    return (index < info[0] * per_image).astype(f32)


def images_of(info, images):
    return jnp.minimum(info[0], images).astype(f32)


def local_moments(hidden, mask, pixels):
    summed = total_of(hidden * mask)
    centred = (hidden - summed / pixels) * mask
    return summed, total_of(centred * centred)


def put_pair(out, first, second):
    peers = out.shape[0]
    chunks = first.shape[1] // 128
    for number, row in enumerate((first, second)):
        for chunk in range(chunks):
            part = row[:, chunk * 128 : chunk * 128 + 128]
            out[:, number * chunks + chunk, :] = jnp.broadcast_to(part, (peers, 128))


def gathered_moments(pairs, counts, chunks):
    total = total_of(counts)
    averages, inverses = [], []
    for chunk in range(chunks):
        sums = pairs[:, chunk, :]
        spread = total_of(pairs[:, chunks + chunk, :])
        average = total_of(sums) / total
        spread = spread + total_of(counts * jnp.square(sums / counts - average))
        averages.append(average)
        inverses.append(lax.rsqrt(spread / total + epsilon))
    return jnp.concatenate(averages, 1), jnp.concatenate(inverses, 1), total[:, :1]


def gathered_sums(pairs, chunks):
    rows = [total_of(pairs[:, chunk, :]) for chunk in range(2 * chunks)]
    return jnp.concatenate(rows[:chunks], 1), jnp.concatenate(rows[chunks:], 1)


def merge(groups):
    total = sum(group[0] for group in groups)
    summed = sum(group[1] for group in groups)
    average = summed / total
    spread = sum(group[2] + group[0] * jnp.square(group[1] / group[0] - average) for group in groups)
    return total, summed, spread


def norm_back(upstream, normed, inverse, gain, total, shift_part, gain_part, mask):
    return mask * (gain * inverse) * (upstream - (shift_part + normed * gain_part) / total)


def shifted(values, by, columns):
    rows = values.shape[0]
    column = jnp.bitwise_and(iota_rows(rows), columns - 1)
    edge = 0 if by == 1 else columns - 1
    return jnp.where(column == edge, 0.0, pltpu.roll(values, by % rows, 0))


def put_halves(mine_out, theirs_out, values, width, info):
    first, second = [], []
    for start in range(0, values.shape[1], width):
        first.append(values[:, start : start + width // 2])
        second.append(values[:, start + width // 2 : start + width])
    first, second = jnp.concatenate(first, 1), jnp.concatenate(second, 1)
    low = jnp.right_shift(info[1], 1) == 0
    mine_out[...] = jnp.where(low, first, second).astype(bf16)
    theirs_out[...] = jnp.where(low, second, first).astype(bf16)
    mine_out.send()
    theirs_out.send()


def stack_rows(parts):
    return jnp.concatenate(parts, axis=0)


def plane_order(pixels, images, rows, columns):
    plane = images * rows * columns
    index = iota_rows(4 * plane, 4 * plane)
    other = lax.broadcasted_iota(jnp.int32, (4 * plane, 4 * plane), 1)
    parity = index // plane
    within = index - parity * plane
    line = within // columns
    column = within - line * columns
    natural = (line * 2 + parity // 2) * (2 * columns) + 2 * column + (parity & 1)
    return (other == natural).astype(bf16)


def reduce_first(geometry, info, x, weight, planes_out, hidden_out, pair_out, edge_out):
    images, rows, columns = geometry
    plane = images * rows * columns
    order = plane_order(4 * plane, images, rows, columns)
    planes = dot(order, x[...]).astype(bf16)
    planes_out[...] = planes
    planes_out.send()
    hidden = dot(planes, weight[...])
    hidden_out[...] = hidden
    hidden_out.send()
    mask = mask_of(info, 4 * plane, plane, images)
    pixels = images_of(info, images) * (4 * rows * columns)
    summed, spread = local_moments(hidden, mask, pixels)
    put_pair(pair_out, summed, spread)
    chunks = hidden.shape[1] // 128
    pair_out[:, 2 * chunks, :] = jnp.full((pair_out.shape[0], 128), pixels, f32)
    per_image = rows * columns
    edges = []
    for parity in range(2):
        for image in range(images):
            end = (2 + parity) * plane + (image + 1) * per_image
            edges.append(hidden[end - columns : end])
    edge_out[...] = stack_rows(edges)


def project_first(geometry, info, planes, weight, hidden_out, moments_out):
    images, rows, columns = geometry
    plane = images * rows * columns
    hidden = dot(planes[:plane], weight[...])
    hidden_out[...] = hidden
    hidden_out.send()
    mask = mask_of(info, plane, plane, images)
    pixels = images_of(info, images) * (rows * columns)
    summed, spread = local_moments(hidden, mask, pixels)
    moments_out[0:1] = summed
    moments_out[1:2] = spread
    moments_out[2:8] = jnp.zeros((6, hidden.shape[1]), f32)


def spatial_first(
    geometry,
    info,
    hidden,
    halo,
    pairs,
    gain,
    shift,
    weight,
    active_out,
    moved_out,
    moments_out,
    counts_out,
    pair_out,
    edge_out,
):
    images, rows, columns = geometry
    plane = images * rows * columns
    per_image = rows * columns
    width = hidden.shape[1]
    chunks = width // 128
    counts = pairs[:, 2 * chunks, :]
    counts_out[...] = counts
    average, inverse, total = gathered_moments(pairs, counts, chunks)
    moments_out[0:1] = average
    moments_out[1:2] = inverse
    moments_out[2:3] = jnp.broadcast_to(total, (1, width))
    moments_out[3:8] = jnp.zeros((5, width), f32)
    moments_out.send()
    counts_out.send()

    def active(values):
        return silu((values - average) * inverse * gain[...] + shift[...])

    inside = jnp.where(info[1] > 0, 1.0, 0.0)
    above = active(halo[...]) * inside
    planes = [active(hidden[number * plane : (number + 1) * plane]) for number in range(4)]

    for number in range(4):
        active_out[:, number * width : (number + 1) * width] = planes[number].astype(bf16)
    active_out.send()

    def lifted(parity):
        parts = []
        for image in range(images):
            at = (parity * images + image) * columns
            parts.append(above[at : at + columns])
            start = image * per_image
            parts.append(planes[2 + parity][start : start + per_image - columns])
        return stack_rows(parts)

    by_row = [(lifted(0), lifted(1)), (planes[0], planes[1]), (planes[2], planes[3])]
    moved = jnp.zeros((plane, width), f32)
    for tap_row in range(3):
        even, odd = by_row[tap_row]
        for tap_column, window in enumerate((shifted(odd, 1, columns), even, odd)):
            tap = 3 * tap_row + tap_column
            window = window.astype(bf16)
            moved = moved + dot(window, weight[tap])
    moved_out[...] = moved
    moved_out.send()
    mask = mask_of(info, plane, plane, images)
    pixels = images_of(info, images) * per_image
    put_pair(pair_out, *local_moments(moved, mask, pixels))
    edge_out[...] = stack_rows(
        [moved[image * per_image : image * per_image + columns] for image in range(images)]
    )


def expand(geometry, info, hidden, pairs, counts, gain, shift, weight, others, active_out, hidden_out, moments_out, state_out):
    images, rows, columns = geometry
    plane = images * rows * columns
    per_image = rows * columns
    width = hidden.shape[1]
    average, inverse, total = gathered_moments(pairs, counts[...] * (per_image / (4 * per_image)), width // 128)
    moments_out[0:1] = average
    moments_out[1:2] = inverse
    moments_out[2:3] = jnp.broadcast_to(total, (1, width))
    moments_out[3:8] = jnp.zeros((5, width), f32)
    moments_out.send()
    active = silu((hidden[...] - average) * inverse * gain[...] + shift[...]).astype(bf16)
    active_out[...] = active
    active_out.send()
    wide = dot(active, weight[...])
    hidden_out[...] = wide
    hidden_out.send()
    mask = mask_of(info, plane, plane, images)
    pixels = images_of(info, images) * per_image
    summed, spread = local_moments(wide, mask, pixels)
    for image in range(images):
        state_out[image : image + 1] = total_of(wide[image * per_image : (image + 1) * per_image])
    state_out[images : images + 1] = summed
    state_out[images + 1 : images + 2] = spread
    if others is None:
        state_out[images + 2 : images + 4] = jnp.zeros((2, wide.shape[1]), f32)
    else:
        state_out[images + 2 : images + 4] = others[0:2]
    state_out[images + 4 : images + 5] = jnp.full((1, wide.shape[1]), pixels, f32)
    if state_out.shape[0] > images + 5:
        state_out[images + 5 :] = jnp.zeros((state_out.shape[0] - images - 5, wide.shape[1]), f32)


def expand_packing(geometry, early, has_others, info, *refs):
    *refs, pack_out = refs
    maps, refs = refs[:early], list(refs[early:])
    others = refs.pop(6) if has_others else None
    expand(geometry, info, *refs[:6], others, *refs[6:])
    at = 0
    for one in (*maps, refs[6].held):
        part = one[...]
        pack_out[:, at : at + part.shape[1]] = part
        at += part.shape[1]


def groups_of(states, images, at):
    return [
        (state[images + 4 : images + 5], state[at : at + 1], state[at + 1 : at + 2]) for state in states
    ]


def merge_states(images, adders, *refs):
    *states, out = refs
    image_sums = states[0][0:images]
    for adder in adders:
        image_sums = image_sums + states[adder][0:images]
    out[0:images] = image_sums
    total, summed, spread = merge(groups_of(states, images, images))
    out[images : images + 1] = summed
    out[images + 1 : images + 2] = spread
    _, summed, spread = merge(groups_of(states, images, images + 2))
    out[images + 2 : images + 3] = summed
    out[images + 3 : images + 4] = spread
    out[images + 4 : images + 5] = total
    if out.shape[0] > images + 5:
        out[images + 5 :] = states[0][images + 5 :]


def excited(image_sums, area, average, inverse, gain, shift, squeeze, excite):
    image_means = (image_sums / area - average) * inverse
    pooled = image_means * gain + shift
    reduced = exact_dot(pooled, squeeze)
    squeezed = silu(reduced)
    gate = jax.nn.sigmoid(exact_dot(squeezed, excite))
    return image_means, pooled, reduced, squeezed, gate


def wide_spread(values, per_image):
    return stack_rows(
        [
            jnp.broadcast_to(values[image : image + 1], (per_image, values.shape[1]))
            for image in range(values.shape[0])
        ]
    )


def finish_state(states, images, at):
    total, summed, spread = merge(groups_of(states, images, at))
    average = summed / total
    return average, lax.rsqrt(spread / total + epsilon), total


def put_gates(gates_out, reduced_out, image_means, pooled, gate, reduced, squeezed):
    images = gate.shape[0]
    gates_out[0:images] = image_means
    gates_out[images : 2 * images] = pooled
    gates_out[2 * images : 3 * images] = gate
    reduced_out[0:images] = reduced
    reduced_out[images : 2 * images] = squeezed


def reduce_second(
    geometry,
    peers,
    area,
    info,
    hidden,
    shortcut,
    gain,
    shift,
    gain_p,
    shift_p,
    squeeze,
    excite,
    weight,
    *rest,
):
    images, rows, columns = geometry
    plane = images * rows * columns
    per_image = rows * columns
    states = rest[:peers]
    moments_out, gates_out, reduced_out, summed_out, block_out, moved_out, pair_out, first_out, last_out = rest[peers:]
    average, inverse, total = finish_state(states, images, images)
    average_p, inverse_p, _ = finish_state(states, images, images + 2)
    for row, value in enumerate((average, inverse, total, average_p, inverse_p)):
        moments_out[row : row + 1] = value
    moments_out[5:8] = jnp.zeros((3, average.shape[1]), f32)
    image_means, pooled, reduced, squeezed, gate = excited(
        states[0][0:images], area, average, inverse, gain[...], shift[...], squeeze[...], excite[...]
    )
    put_gates(gates_out, reduced_out, image_means, pooled, gate, reduced, squeezed)
    branch = (hidden[...] - average) * inverse * gain[...] + shift[...]
    summed = (
        branch * wide_spread(gate, per_image)
        + (shortcut[...] - average_p) * inverse_p * gain_p[...]
        + shift_p[...]
    )
    summed_out[...] = summed
    for one in (moments_out, gates_out, reduced_out, summed_out):
        one.send()
    block = silu(summed).astype(bf16)
    block_out[...] = block
    block_out.send()
    moved = dot(block, weight[...])
    moved_out[...] = moved
    moved_out.send()
    mask = mask_of(info, plane, plane, images)
    pixels = images_of(info, images) * per_image
    put_pair(pair_out, *local_moments(moved, mask, pixels))
    put_edges(first_out, last_out, moved, images, per_image, columns)


def put_edges(first_out, last_out, values, images, per_image, columns):
    first_out[...] = stack_rows(
        [values[image * per_image : image * per_image + columns] for image in range(images)]
    )
    last_out[...] = stack_rows(
        [values[(image + 1) * per_image - columns : (image + 1) * per_image] for image in range(images)]
    )


def extended(values, above, below, images, per_image, columns):
    parts = []
    for image in range(images):
        parts.append(above[image * columns : (image + 1) * columns])
        parts.append(values[image * per_image : (image + 1) * per_image])
        parts.append(below[image * columns : (image + 1) * columns])
    return stack_rows(parts)


def window_of(values, lift, images, per_image, columns):
    span = per_image + 2 * columns
    return stack_rows(
        [
            values[image * span + lift * columns : image * span + lift * columns + per_image]
            for image in range(images)
        ]
    )


def spatial_second(
    geometry,
    last,
    info,
    hidden,
    above,
    below,
    pairs,
    counts,
    gain,
    shift,
    weight,
    active_out,
    moved_out,
    moments_out,
    pair_out,
    first_out,
    last_out,
):
    images, rows, columns = geometry
    plane = images * rows * columns
    per_image = rows * columns
    width = hidden.shape[1]
    average, inverse, total = gathered_moments(pairs, counts[...] * 0.25, width // 128)
    moments_out[0:1] = average
    moments_out[1:2] = inverse
    moments_out[2:3] = jnp.broadcast_to(total, (1, width))
    moments_out[3:8] = jnp.zeros((5, width), f32)

    def active(values):
        return silu((values - average) * inverse * gain[...] + shift[...])

    top = active(above[...]) * jnp.where(info[1] > 0, 1.0, 0.0)
    bottom = active(below[...]) * jnp.where(info[1] < last, 1.0, 0.0)
    middle = active(hidden[...])
    active_out[...] = middle.astype(bf16)
    active_out.send()
    moments_out.send()
    middle = extended(middle, top, bottom, images, per_image, columns)
    by_column = (shifted(middle, 1, columns), middle, shifted(middle, -1, columns))
    moved = jnp.zeros((plane, width), f32)
    for tap_column in range(3):
        for tap_row in range(3):
            tap = 3 * tap_row + tap_column
            window = window_of(by_column[tap_column], tap_row, images, per_image, columns).astype(bf16)
            moved = moved + dot(window, weight[tap])
    moved_out[...] = moved
    moved_out.send()
    mask = mask_of(info, plane, plane, images)
    pixels = images_of(info, images) * per_image
    put_pair(pair_out, *local_moments(moved, mask, pixels))
    put_edges(first_out, last_out, moved, images, per_image, columns)


def finish_second(
    geometry,
    peers,
    area,
    info,
    hidden,
    block,
    out_grad,
    gain,
    shift,
    squeeze,
    excite,
    *rest,
):
    images, rows, columns = geometry
    plane = images * rows * columns
    per_image = rows * columns
    states = rest[:peers]
    moments_out, gates_out, reduced_out, mixed_out, grad_out, state_out = rest[peers:]
    average, inverse, total = finish_state(states, images, images)
    for row, value in enumerate((average, inverse, total)):
        moments_out[row : row + 1] = value
    moments_out[3:8] = jnp.zeros((5, average.shape[1]), f32)
    image_means, pooled, reduced, squeezed, gate = excited(
        states[0][0:images], area, average, inverse, gain[...], shift[...], squeeze[...], excite[...]
    )
    put_gates(gates_out, reduced_out, image_means, pooled, gate, reduced, squeezed)
    normed = (hidden[...] - average) * inverse
    summed = (normed * gain[...] + shift[...]) * wide_spread(gate, per_image) + block[...].astype(f32)
    mask = mask_of(info, plane, plane, images)
    logistic = jax.nn.sigmoid(summed)
    mixed_out[...] = (summed * logistic * mask).astype(bf16)
    for one in (moments_out, gates_out, reduced_out, mixed_out):
        one.send()
    grad = out_grad[...].astype(f32) * mask * (logistic * (1.0 + summed * (1.0 - logistic)))
    grad_out[...] = grad
    grad_out.send()
    put_image_sums(state_out, grad, normed, images, per_image)
    state_out[2 * images :] = jnp.zeros((state_out.shape[0] - 2 * images, grad.shape[1]), f32)


def put_image_sums(state_out, grad, normed, images, per_image):
    crossed = grad * normed
    for image in range(images):
        part = slice(image * per_image, (image + 1) * per_image)
        state_out[image : image + 1] = total_of(grad[part])
        state_out[images + image : images + image + 1] = total_of(crossed[part])


def excite_back(
    images,
    area,
    has_others,
    info,
    gain,
    shift,
    gates,
    reduced,
    squeeze,
    excite,
    mine,
    core_other,
    y_other,
    both_other,
    sums_out,
    pooled_grad_out,
    gate_grad_out,
    reduced_grad_out,
):
    state = (mine[...] + core_other[...]) + (y_other[...] + both_other[...])
    plain = state[0:images]
    crossed = state[images : 2 * images]
    image_means = gates[0:images]
    gate = gates[2 * images : 3 * images]
    gate_grad = gain[...] * crossed + shift[...] * plain
    before_gate = gate_grad * gate * (1.0 - gate)
    squeezed_grad = exact_dot(before_gate, excite[...], 1)
    reduced_grad = squeezed_grad * slope(reduced[0:images])
    pooled_grad = exact_dot(reduced_grad, squeeze[...], 1)
    pooled_grad_out[...] = pooled_grad / area
    gate_grad_out[...] = before_gate
    reduced_grad_out[...] = reduced_grad
    mask = (iota_rows(images) < info[0]).astype(f32)
    sums_out[0:1] = total_of(mask * (plain * gate + pooled_grad))
    sums_out[1:2] = total_of(mask * (crossed * gate + pooled_grad * image_means))
    if has_others:
        sums_out[2:3] = total_of(mask * plain)
        sums_out[3:4] = state[2 * images : 2 * images + 1]
    else:
        sums_out[2:4] = jnp.zeros((2, plain.shape[1]), f32)


def expand_back(
    geometry,
    peers,
    cut,
    info,
    grad,
    hidden,
    moments,
    gates,
    pooled_grad,
    gain,
    weight,
    middle,
    middle_moments,
    middle_gain,
    middle_shift,
    *rest,
):
    images, rows, columns = geometry
    plane = images * rows * columns
    per_image = rows * columns
    sums = rest[0][...]
    for other in rest[1:peers]:
        sums = sums + other[...]
    sums_out, mine_out, *rest = rest[peers:]
    theirs_out = rest.pop(0) if cut else None
    middle_grad_out, pair_out, first_out, last_out = rest
    sums_out[...] = sums
    mask = mask_of(info, plane, plane, images)
    average, inverse, total = moments[0:1], moments[1:2], moments[2:3]
    normed = (hidden[...] - average) * inverse
    upstream = grad[...] * wide_spread(gates[2 * images : 3 * images], per_image) + wide_spread(
        pooled_grad[...], per_image
    )
    low = norm_back(upstream, normed, inverse, gain[...], total, sums[0:1], sums[1:2], mask)
    if cut:
        put_halves(mine_out, theirs_out, low, cut, info)
    low = low.astype(bf16)
    if not cut:
        mine_out[...] = low
        mine_out.send()
    average, inverse = middle_moments[0:1], middle_moments[1:2]
    normed = (middle[...] - average) * inverse
    middle_grad = dot(low, weight[...], 1, 1) * slope(normed * middle_gain[...] + middle_shift[...])
    middle_grad_out[...] = middle_grad
    middle_grad_out.send()
    masked = middle_grad * mask
    put_pair(pair_out, total_of(masked), total_of(masked * normed))
    put_edges(first_out, last_out, middle_grad, images, per_image, columns)


def spatial_second_back(
    geometry,
    last,
    info,
    grad,
    grad_above,
    grad_below,
    hidden,
    above,
    below,
    moments,
    gain,
    pairs,
    weight,
    earlier,
    earlier_moments,
    earlier_gain,
    earlier_shift,
    sums_out,
    mine_out,
    theirs_out,
    earlier_grad_out,
    pair_out,
):
    images, rows, columns = geometry
    plane = images * rows * columns
    per_image = rows * columns
    width = hidden.shape[1]
    shift_part, gain_part = gathered_sums(pairs, width // 128)
    sums_out[0:1] = shift_part
    sums_out[1:2] = gain_part
    sums_out[2:8] = jnp.zeros((6, width), f32)
    mask = mask_of(info, plane, plane, images)
    edge_mask = mask_of(info, images * columns, images * columns, images)
    average, inverse, total = moments[0:1], moments[1:2], moments[2:3]

    def lowered(upstream, values, rows_mask):
        normed = (values - average) * inverse
        return norm_back(upstream, normed, inverse, gain[...], total, shift_part, gain_part, rows_mask)

    middle = lowered(grad[...], hidden[...], mask)
    put_halves(mine_out, theirs_out, middle, width, info)
    top = lowered(grad_above[...], above[...], edge_mask * jnp.where(info[1] > 0, 1.0, 0.0))
    bottom = lowered(grad_below[...], below[...], edge_mask * jnp.where(info[1] < last, 1.0, 0.0))
    middle = extended(middle, top, bottom, images, per_image, columns)
    by_column = (shifted(middle, -1, columns), middle, shifted(middle, 1, columns))
    moved = jnp.zeros((plane, width), f32)
    for tap_column in range(3):
        for tap_row in range(3):
            window = window_of(by_column[tap_column], 2 - tap_row, images, per_image, columns)
            moved = moved + dot(window.astype(bf16), weight[3 * tap_row + tap_column], 1, 1)
    normed = (earlier[...] - earlier_moments[0:1]) * earlier_moments[1:2]
    earlier_grad = moved * slope(normed * earlier_gain[...] + earlier_shift[...])
    earlier_grad_out[...] = earlier_grad
    earlier_grad_out.send()
    masked = earlier_grad * mask
    put_pair(pair_out, total_of(masked), total_of(masked * normed))


def reduce_second_back(
    geometry,
    info,
    grad,
    hidden,
    moments,
    gain,
    pairs,
    weight,
    carried,
    summed,
    wide_hidden,
    shortcut,
    wide_moments,
    sums_out,
    mine_out,
    theirs_out,
    summed_grad_out,
    state_out,
):
    images, rows, columns = geometry
    plane = images * rows * columns
    per_image = rows * columns
    width = hidden.shape[1]
    shift_part, gain_part = gathered_sums(pairs, width // 128)
    sums_out[0:1] = shift_part
    sums_out[1:2] = gain_part
    sums_out[2:8] = jnp.zeros((6, width), f32)
    mask = mask_of(info, plane, plane, images)
    normed = (hidden[...] - moments[0:1]) * moments[1:2]
    low = norm_back(
        grad[...], normed, moments[1:2], gain[...], moments[2:3], shift_part, gain_part, mask
    )
    put_halves(mine_out, theirs_out, low, width, info)
    low = low.astype(bf16)
    summed_grad = (carried[...] + dot(low, weight[...], 1, 1)) * slope(summed[...])
    summed_grad_out[...] = summed_grad
    summed_grad_out.send()
    normed = (wide_hidden[...] - wide_moments[0:1]) * wide_moments[1:2]
    put_image_sums(state_out, summed_grad, normed, images, per_image)
    other = (shortcut[...] - wide_moments[3:4]) * wide_moments[4:5]
    state_out[2 * images : 2 * images + 1] = total_of(summed_grad * mask * other)
    rest = state_out.shape[0] - 2 * images - 1
    state_out[2 * images + 1 :] = jnp.zeros((rest, summed_grad.shape[1]), f32)


def put_quarters(outs, maps, info):
    quarter = 2 * info[2] + jnp.right_shift(info[1], 1)
    for number, out in enumerate(outs):
        at = 0
        for one in maps:
            width = one.shape[1] // 4
            first = pl.multiple_of((quarter ^ number) * width, width)
            out[:, at : at + width] = one[:, pl.ds(first, width)]
            at += width
        out.send()


def shortcut_back(geometry, peers, info, grad, shortcut, moments, gain, weight, *rest):
    images, rows, columns = geometry
    plane = images * rows * columns
    sums = rest[0][...]
    for other in rest[1:peers]:
        sums = sums + other[...]
    low_out, image_out = rest[peers:]
    mask = mask_of(info, plane, plane, images)
    normed = (shortcut[...] - moments[3:4]) * moments[4:5]
    low = norm_back(
        grad[...], normed, moments[4:5], gain[...], moments[2:3], sums[2:3], sums[3:4], mask
    )
    low = low.astype(bf16)
    low_out[...] = low
    low_out.send()
    image_out[...] = dot(low, weight[...], 1, 1)


def spatial_first_back(
    geometry,
    last,
    info,
    grad,
    grad_below,
    hidden,
    below,
    moments,
    gain,
    pairs,
    weight,
    earlier,
    earlier_moments,
    earlier_gain,
    earlier_shift,
    sums_out,
    low_out,
    earlier_grad_out,
    pair_out,
):
    images, rows, columns = geometry
    plane = images * rows * columns
    per_image = rows * columns
    width = hidden.shape[1]
    shift_part, gain_part = gathered_sums(pairs, width // 128)
    sums_out[0:1] = shift_part
    sums_out[1:2] = gain_part
    sums_out[2:8] = jnp.zeros((6, width), f32)
    mask = mask_of(info, plane, plane, images)
    edge_mask = mask_of(info, images * columns, images * columns, images)
    average, inverse, total = moments[0:1], moments[1:2], moments[2:3]

    def lowered(upstream, values, rows_mask):
        normed = (values - average) * inverse
        return norm_back(upstream, normed, inverse, gain[...], total, shift_part, gain_part, rows_mask)

    middle = lowered(grad[...], hidden[...], mask)
    bottom = lowered(grad_below[...], below[...], edge_mask * jnp.where(info[1] < last, 1.0, 0.0))
    parts = []
    for image in range(images):
        parts.append(middle[image * per_image + columns : (image + 1) * per_image])
        parts.append(bottom[image * columns : (image + 1) * columns])
    lower = stack_rows(parts)
    here = middle.astype(bf16)
    low_out[...] = here
    low_out.send()
    here_right = shifted(middle, -1, columns).astype(bf16)
    next_right = shifted(lower, -1, columns).astype(bf16)
    lower = lower.astype(bf16)

    def back(window, tap_row, tap_column):
        return dot(window, weight[3 * tap_row + tap_column], 1, 1)

    planes = [
        back(here, 1, 1),
        back(here, 1, 2) + back(here_right, 1, 0),
        back(here, 2, 1) + back(lower, 0, 1),
        back(here, 2, 2) + back(here_right, 2, 0) + back(lower, 0, 2) + back(next_right, 0, 0),
    ]
    shift_sum = jnp.zeros((1, width), f32)
    gain_sum = jnp.zeros((1, width), f32)
    for number in range(4):
        at = slice(number * plane, (number + 1) * plane)
        normed = (earlier[at] - earlier_moments[0:1]) * earlier_moments[1:2]
        earlier_grad = planes[number] * slope(normed * earlier_gain[...] + earlier_shift[...])
        earlier_grad_out[at] = earlier_grad
        masked = earlier_grad * mask
        shift_sum = shift_sum + total_of(masked)
        gain_sum = gain_sum + total_of(masked * normed)
    put_pair(pair_out, shift_sum, gain_sum)


def reduce_first_back(
    geometry,
    info,
    grad,
    hidden,
    moments,
    gain,
    pairs,
    weight,
    image_part,
    sums_2,
    sums_3,
    sums_4,
    sums_5,
    sums_6,
    *rest,
):
    *lows, gain_grad_out, shift_grad_out, low_out, image_out = rest
    if lows:
        maps, quarters_out = lows[:-4], lows[-4:]
        for one in maps:
            one.wait()
        put_quarters(quarters_out, maps, info)
    images, rows, columns = geometry
    plane = images * rows * columns
    width = hidden.shape[1]
    shift_part, gain_part = gathered_sums(pairs, width // 128)
    at = 0
    for shift_row, gain_row in (
        (shift_part, gain_part),
        (sums_2[0:1], sums_2[1:2]),
        (sums_3[0:1], sums_3[1:2]),
        (sums_3[2:3], sums_3[3:4]),
        (sums_4[0:1], sums_4[1:2]),
        (sums_5[0:1], sums_5[1:2]),
        (sums_6[0:1], sums_6[1:2]),
    ):
        shift_grad_out[:, at : at + shift_row.shape[1]] = shift_row
        gain_grad_out[:, at : at + shift_row.shape[1]] = gain_row
        at += shift_row.shape[1]
    mask = mask_of(info, 4 * plane, plane, images)
    normed = (hidden[...] - moments[0:1]) * moments[1:2]
    low = norm_back(
        grad[...], normed, moments[1:2], gain[...], moments[2:3], shift_part, gain_part, mask
    ).astype(bf16)
    low_out[...] = low
    low_out.send()
    gain_grad_out.send()
    shift_grad_out.send()
    image_grad = dot(low, weight[...], 1, 1)
    image_grad = stack_rows([image_grad[:plane] + image_part[...], image_grad[plane:]]).astype(bf16)
    order = plane_order(4 * plane, images, rows, columns)
    image_out[...] = dot(order, image_grad, 0, 0).astype(bf16)


def unit(size):
    rows = lax.broadcasted_iota(jnp.int32, (size, size), 0)
    columns = lax.broadcasted_iota(jnp.int32, (size, size), 1)
    return (rows == columns).astype(bf16)


def turned(values, one):
    return dot(one, values, 1, 1).astype(bf16)


def outer_rows(inner, outer, out, base=0):
    width = out.shape[1]
    pieces = outer.shape[1] // width
    count = inner.shape[1]
    if pieces == 1:
        step = min(512, count)
        one = unit(step)
        for start in range(0, count, step):
            part = turned(inner[:, start : start + step], one)
            out[base + start : base + start + step] = dot(part, outer).astype(bf16)
        return
    step = 512 // pieces
    row = lax.broadcasted_iota(jnp.int32, (step * pieces, step), 0)
    column = lax.broadcasted_iota(jnp.int32, (step * pieces, step), 1)
    spreads = [(row == column * pieces + piece).astype(bf16) for piece in range(pieces)]
    stacked = stack_rows([outer[:, piece * width : (piece + 1) * width] for piece in range(pieces)])
    for start in range(0, count, step):
        part = inner[:, start : start + step]
        widened = [dot(spread, part, 1, 1).astype(bf16) for spread in spreads]
        result = dot(jnp.concatenate(widened, 1), stacked)
        out[base + start * pieces : base + (start + step) * pieces] = result.astype(bf16)


def weight_rows(inner, outer, out):
    outer_rows(inner[...], outer[...], out)


def two_parts(values):
    first = values.astype(bf16).astype(f32)
    return first, values - first


def left_parts(values):
    first, second = two_parts(values)
    return stack_rows([first, second, first]).astype(bf16)


def right_parts(values):
    first, second = two_parts(values)
    return stack_rows([first, first, second]).astype(bf16)


def gate_rows(images, share, pooled, reduced, gate_grad, reduced_grad, out, base=0):
    width = out.shape[1]
    squeezed = reduced[images : 2 * images]
    right = right_parts(reduced_grad[...] * share)
    units = reduced_grad.shape[1]
    rows = pooled.shape[2]
    for piece in range(pooled.shape[0]):
        part = dot(left_parts(pooled[piece]), right, 0, 0)
        out[base : base + rows, piece * units : (piece + 1) * units] = part.astype(bf16)
    wide_pieces = gate_grad.shape[1] // width
    row = lax.broadcasted_iota(jnp.int32, (units, units * wide_pieces), 0)
    column = lax.broadcasted_iota(jnp.int32, (units, units * wide_pieces), 1)
    left = left_parts(squeezed)
    right = right_parts(gate_grad[...] * share)
    result = jnp.zeros((units * wide_pieces, width), f32)
    for piece in range(wide_pieces):
        widened = dot(left, (column == row * wide_pieces + piece).astype(bf16)).astype(bf16)
        result = result + dot(widened, right[:, piece * width : (piece + 1) * width], 0, 0)
    out[base + rows : base + rows + units * wide_pieces] = result.astype(bf16)


def spatial_alone(geometry, info, active, above, below, outer, out):
    images, rows, columns = geometry
    per_image = rows * columns
    width = active.shape[1]

    def edge(values, at):
        parts = [values[image * per_image + at : image * per_image + at + columns] for image in range(images)]
        return stack_rows(parts).astype(f32)

    top = edge(above, per_image - columns) * jnp.where(info[1] > 0, 1.0, 0.0)
    bottom = edge(below, 0) * jnp.where(info[1] < info[4], 1.0, 0.0)
    middle = extended(active[...].astype(f32), top, bottom, images, per_image, columns)
    by_column = (shifted(middle, 1, columns), middle, shifted(middle, -1, columns))
    one = unit(width)
    for tap in range(9):
        window = window_of(by_column[tap % 3], tap // 3, images, per_image, columns).astype(bf16)
        out[tap * width : (tap + 1) * width] = dot(turned(window, one), outer[...]).astype(bf16)


def first_alone(geometry, info, active, above, outer, out):
    images, rows, columns = geometry
    per_image = rows * columns
    width = active.shape[1] // 4
    inside = jnp.where(info[1] > 0, 1.0, 0.0)
    one = unit(width)
    for tap in range(9):
        tap_row, tap_column = tap // 3, tap % 3
        number = (0 if tap_row == 1 else 2) + (0 if tap_column == 1 else 1)
        at = slice(number * width, (number + 1) * width)
        window = active[:, at].astype(f32)
        if tap_row == 0:
            parts = []
            for image in range(images):
                start = image * per_image
                parts.append(above[start + per_image - columns : start + per_image, at].astype(f32) * inside)
                parts.append(window[start : start + per_image - columns])
            window = stack_rows(parts)
        if tap_column == 0:
            window = shifted(window, 1, columns)
        out[tap * width : (tap + 1) * width] = dot(turned(window.astype(bf16), one), outer[...]).astype(bf16)


class Band:
    def __init__(self, rows, half, lines, xs):
        self.rows, self.half, self.lines, self.xs = rows, half, lines, xs

    def shapes(self):
        lines = len(self.lines)
        left = ((lines, len(self.xs), self.rows, self.half), bf16)
        right = ((lines, 2, self.rows, self.half), bf16)
        return [left, left, right, right]


def spot_of(info):
    return info[2], jnp.right_shift(info[1], 1), jnp.bitwise_and(info[1], 1)


def send_piece(band, spot, piece, source, place, refs, semaphores, used):
    x, y, core = spot
    line, x_of, y_of, core_of = piece >> 3, (piece >> 2) & 1, (piece >> 1) & 1, piece & 1
    if line not in band.lines or x_of not in band.xs:
        return []
    slot = band.lines.index(line)
    copies = []
    for half in range(2):
        mine = (y == y_of) if half == 0 else (x == x_of)
        inner = band.xs.index(x_of) if half == 0 else y_of
        columns = pl.ds(band.half * half, band.half)
        for kept in (True, False):
            target = refs[2 * half + (0 if kept else 1)].at[slot, inner, place]
            copy = pltpu.make_async_copy(source.at[:, columns], target, semaphores.at[used[0]])
            used[0] += 1
            wanted = mine if kept else jnp.logical_not(mine)
            if core is not None:
                wanted = jnp.logical_and(core == core_of, wanted)
            copies.append((wanted, copy))
    return copies


def send_rows(band, spot, source, base, first, last, refs, semaphores, used):
    copies = []
    for piece in range(first // band.rows, (last - 1) // band.rows + 1):
        start = max(first, piece * band.rows)
        stop = min(last, (piece + 1) * band.rows)
        held = source.at[pl.ds(base + start - first, stop - start)]
        place = pl.ds(start - piece * band.rows, stop - start)
        copies += send_piece(band, spot, piece, held, place, refs, semaphores, used)
    return copies


def conduct(copies, action):
    for wanted, copy in copies:

        def act(copy=copy):
            getattr(copy, action)()

        pl.when(wanted)(act)


def paired(own, other):
    return stack_rows([own[...], other[...]])


def merged_rows(values):
    return values[...].reshape(-1, values.shape[-1])


def half_of(values, width, info):
    first, second = [], []
    for start in range(0, values.shape[1], width):
        first.append(values[:, start : start + width // 2])
        second.append(values[:, start + width // 2 : start + width])
    low = jnp.right_shift(info[1], 1) == 0
    return jnp.where(low, jnp.concatenate(first, 1), jnp.concatenate(second, 1))


def place_rows(slice_rows, core, source, first, last, target, semaphores, used):
    copies = []
    for piece in range(first // slice_rows, (last - 1) // slice_rows + 1):
        start = max(first, piece * slice_rows)
        stop = min(last, (piece + 1) * slice_rows)
        held = source.at[pl.ds(start - first, stop - start)]
        place = pl.ds(start - piece * slice_rows, stop - start)
        target_rows = target.at[piece >> 2, (piece >> 1) & 1, place]
        copies.append(
            (core == (piece & 1), pltpu.make_async_copy(held, target_rows, semaphores.at[used[0]]))
        )
        used[0] += 1
    return copies


def plane_rows(values):
    return values[...].reshape(-1, values.shape[-1])


def line_place(info, line):
    return jnp.bitwise_and(info[3], 1) == (line & 1)


def either_copy(stays, source, kept, sent, semaphores, used):
    copies = []
    for wanted, target in ((stays, kept), (jnp.logical_not(stays), sent)):
        copies.append((wanted, pltpu.make_async_copy(source, target, semaphores.at[used[0]])))
        used[0] += 1
    return copies


def early_rows(starts, slice_rows, info, *rest):
    (
        active,
        planes,
        lows,
        pooled,
        reduced,
        reduced_other,
        gate_grad,
        reduced_grad,
        gate_grad_other,
        reduced_grad_other,
        kept,
        sent,
        gate_held,
        slices_held,
        semaphores,
    ) = rest
    core = jnp.bitwise_and(info[1], 1)
    quarter = 2 * info[2] + jnp.right_shift(info[1], 1)
    rows, width = slices_held.shape[1:]
    units = reduced.shape[1]
    images = reduced.shape[0] // 2
    pooled.wait(), gate_grad.wait(), gate_grad_other.wait()
    right = right_parts(paired(reduced_grad, reduced_grad_other))
    share = pooled.shape[0] // 4
    for number in range(share):
        part = dot(left_parts(pooled[quarter * share + number]), right, 0, 0)
        gate_held[0:units, number * units : (number + 1) * units] = part.astype(bf16)
    columns = pl.ds(pl.multiple_of(quarter * width, width), width)
    gate_held[units : 2 * units] = dot(
        left_parts(stack_rows([reduced[images:], reduced_other[images:]])),
        right_parts(stack_rows([gate_grad[:, columns], gate_grad_other[:, columns]])),
        0,
        0,
    ).astype(bf16)
    lowest = starts[0] // slice_rows
    count = slices_held.shape[0]
    numbers = range(count)
    found = {number: [] for number in numbers}
    skipped = -(starts[0] - lowest * slice_rows) % 16

    def pick(first, last, channels):
        near = [
            number
            for number in numbers
            if (lowest + 2 * number + 2) * slice_rows > first
            and (lowest + 2 * number) * slice_rows - skipped < last
        ]
        row = lax.broadcasted_iota(jnp.int32, (rows, channels), 0)
        column = lax.broadcasted_iota(jnp.int32, (rows, channels), 1)
        chosen = []
        for number in near:
            begin = (lowest + 2 * number + core) * slice_rows - first
            limit = slice_rows
            if number == 0:
                moved = jnp.where(core == 0, skipped, 0)
                begin = begin - moved
                limit = limit + moved
            wanted = jnp.logical_and(column == row + begin, row < limit)
            chosen.append(wanted.astype(f32))
        return near, stack_rows(chosen).astype(bf16)

    def add(near, result):
        for at, number in enumerate(near):
            found[number].append(result[at * rows : (at + 1) * rows])

    near, chosen = pick(starts[1], starts[2], 2 * units)
    add(near, dot(chosen, gate_held[...]))
    for first, last, inner, at in ((starts[0], starts[1], active, 0), (starts[2], starts[3], planes, 1)):
        near, chosen = pick(first, last, inner.shape[-1])
        left = dot(chosen, plane_rows(inner), 1, 1).astype(bf16)
        outer = lows[:, :, at * width : (at + 1) * width].reshape(-1, width)
        add(near, dot(left, outer))
    used = [0]
    copies = []
    for number in numbers:
        slices_held[number] = sum(found[number][1:], found[number][0]).astype(bf16)
        piece = lowest + 2 * number
        line, spot = piece >> 3, (piece >> 1) & 3
        slot = spot if line >= 2 else 4
        added = either_copy(
            line_place(info, line), slices_held.at[number], kept.at[slot], sent.at[slot], semaphores, used
        )
        conduct(added, "start")
        copies += added
    conduct(copies, "wait")


def late_rows(geometry, start, slice_rows, info, active, low, kept, sent, held, semaphores):
    images, _, columns = geometry
    core = jnp.bitwise_and(info[1], 1)
    width = active.shape[-1] // 4
    span = active.shape[1] // images
    rim = jnp.zeros((columns, width), bf16)

    def whole_images(values, columns_of):
        return [
            [values[first + number, image * span : (image + 1) * span, columns_of] for number in range(4)]
            for first in range(0, active.shape[0], 4)
            for image in range(images)
        ]

    def plane_of(number):
        return whole_images(active, slice(number * width, (number + 1) * width))

    def level(image_list):
        return stack_rows([part for parts in image_list for part in parts])

    def lifted(values, height):
        parts = []
        for at in range(0, values.shape[0], height):
            parts += [rim, values[at : at + height - columns]]
        return stack_rows(parts)

    outer = level(whole_images(low, slice(0, low.shape[-1])))
    turned_low = turned(outer, unit(outer.shape[1]))
    one = unit(width)
    height = 4 * span
    by_row = []
    for parity in (1, 0, 1):
        even, odd = level(plane_of(2 * parity)), level(plane_of(2 * parity + 1))
        by_row.append((shifted(odd.astype(f32), 1, columns).astype(bf16), even, odd))
    by_row[0] = tuple(lifted(values, height) for values in by_row[0])
    used = [0]
    copies = []
    for tap in range(9):
        product = dot(turned_low, by_row[tap // 3][tap % 3]).astype(bf16)
        held[tap * width : (tap + 1) * width] = turned(product, one)
        first = start + tap * width
        last = first + width
        for piece in range(first // slice_rows, (last - 1) // slice_rows + 1):
            begin, stop = max(first, piece * slice_rows), min(last, (piece + 1) * slice_rows)
            line, spot = piece >> 3, (piece >> 1) & 3
            place = pl.ds(begin - piece * slice_rows, stop - begin)
            added = either_copy(
                line_place(info, line),
                held.at[pl.ds(begin - start, stop - begin)],
                kept.at[spot, place],
                sent.at[spot, place],
                semaphores,
                used,
            )
            added = [(jnp.logical_and(core == (piece & 1), wanted), copy) for wanted, copy in added]
            conduct(added, "start")
            copies += added
    conduct(copies, "wait")


def pair_sums(info, kept, came, *outs):
    outs[0][...] = (kept[0:4].astype(f32) + came[0:4].astype(f32)).astype(bf16)
    outs[0].send()
    if len(outs) == 2:
        outs[1][...] = (kept[4].astype(f32) + came[4].astype(f32)).astype(bf16)


def owner_sums(info, kept, came, *rest):
    *others, first, second, third, fourth = rest
    quarter = 2 * info[2] + jnp.right_shift(info[1], 1)
    kept.wait(), came.wait()
    for number, out in enumerate((first, second, third, fourth)):
        total = kept[quarter ^ number].astype(f32) + came[quarter ^ number].astype(f32)
        if others:
            lower = others[0][...].astype(f32) + others[1][...].astype(f32)
            total = jnp.where(info[3] >= 2, total, lower)
        out[...] = total.astype(bf16)
        out.send()


def gate_slices(images, start, slice_rows, info, pooled, reduced, gate_grad, reduced_grad, target, held, half_held, semaphores):
    core = jnp.bitwise_and(info[1], 1)
    gate_rows(images, 1.0, pooled, reduced, gate_grad, reduced_grad, held)
    half_held[...] = half_of(held[...].astype(f32), held.shape[1], info).astype(bf16)
    last = start + held.shape[0]
    copies = place_rows(slice_rows, core, half_held, start, last, target, semaphores, [0])
    conduct(copies, "start")
    conduct(copies, "wait")


def whole_rows_of(start, slice_rows, info, active, low, target, held, semaphores):
    core = jnp.bitwise_and(info[1], 1)
    outer_rows(merged_rows(active), merged_rows(low), held)
    last = start + held.shape[0]
    copies = place_rows(slice_rows, core, held, start, last, target, semaphores, [0])
    conduct(copies, "start")
    conduct(copies, "wait")


def image_rows(values, image, images):
    span = values.shape[1] // images
    return [values[number, image * span : (image + 1) * span] for number in range(values.shape[0])]


def whole_spatial_rows(geometry, start, slice_rows, info, active, low, target, held, semaphores):
    images, _, columns = geometry
    core = jnp.bitwise_and(info[1], 1)
    used = [0]
    copies = []
    width = active.shape[-1]
    rim = jnp.zeros((columns, width), f32)
    outer, maps = [], []
    for image in range(images):
        outer += image_rows(low, image, images)
        parts = [part.astype(f32) for part in image_rows(active, image, images)]
        maps.append(stack_rows([rim] + parts + [rim]))
    outer = stack_rows(outer)
    span = maps[0].shape[0]
    every = stack_rows(maps)
    by_column = (shifted(every, 1, columns), every, shifted(every, -1, columns))
    by_column = [part.astype(bf16) for part in by_column]
    one = unit(width)
    for tap in range(9):
        tap_row, tap_column = tap // 3, tap % 3
        window = stack_rows(
            [
                by_column[tap_column][
                    image * span + tap_row * columns : (image + 1) * span - (2 - tap_row) * columns
                ]
                for image in range(images)
            ]
        )
        held[tap * width : (tap + 1) * width] = dot(turned(window, one), outer).astype(bf16)
        first = start + tap * width
        added = place_rows(
            slice_rows,
            core,
            held.at[pl.ds(tap * width, width)],
            first,
            first + width,
            target,
            semaphores,
            used,
        )
        conduct(added, "start")
        copies.extend(added)
    conduct(copies, "wait")


def reduce_rows(band, info, planes, planes_other, low, low_other, *rest):
    *targets, held, semaphores = rest
    spot = spot_of(info)
    outer_rows(paired(planes, planes_other), paired(low, low_other), held)
    copies = send_rows(band, spot, held, 0, 0, held.shape[0], targets, semaphores, [0])
    conduct(copies, "start")
    conduct(copies, "wait")


def second_halves(band, info, left, left_came, right, right_came, *outs):
    x, y = info[2], jnp.right_shift(info[1], 1)

    def total(first, second, slot, inner):
        return first[slot, inner].astype(f32) + second[slot, inner].astype(f32)

    outs = list(outs)
    split = len(band.xs) == 2
    left_outs = [outs.pop(0) for _ in range(2 if split else 1)]
    right_outs = outs
    left.wait(), left_came.wait(), right.wait(), right_came.wait()
    for slot in range(len(band.lines)):
        if split:
            left_outs[0][slot] = total(left, left_came, slot, x).astype(bf16)
            left_outs[1][slot] = total(left, left_came, slot, 1 - x).astype(bf16)
        else:
            left_outs[0][slot] = total(left, left_came, slot, 0).astype(bf16)
        right_outs[0][slot] = total(right, right_came, slot, y).astype(bf16)
        right_outs[1][slot] = total(right, right_came, slot, 1 - y).astype(bf16)


def line_halves(band, info, left, left_came, right, right_came, *outs):
    low = jnp.bitwise_and(info[3], 1)
    half = band.half

    def put(out, at, slot):
        out[at, :, 0:half] = (left[slot].astype(f32) + left_came[slot].astype(f32)).astype(bf16)
        out[at, :, half:] = (right[slot].astype(f32) + right_came[slot].astype(f32)).astype(bf16)

    left.wait(), left_came.wait(), right.wait(), right_came.wait()
    if len(band.lines) == 1:
        put(outs[0], 0, 0)
        return
    for at in range(len(band.lines) // 2):
        put(outs[0], at, 2 * at + low)
        put(outs[1], at, 2 * at + 1 - low)


def line_sum(band, info, own, came, *outs):
    if len(band.lines) < 4:
        outs[0][...] = (own[0].astype(f32) + came[0].astype(f32)).astype(bf16)
        return
    top = jnp.right_shift(info[3], 1)
    own.wait(), came.wait()
    for out, slot in zip(outs, (top, 1 - top)):
        out[...] = (own[slot].astype(f32) + came[slot].astype(f32)).astype(bf16)


class Loaded:
    def __init__(self, source, held, semaphore):
        self.held = held
        self.shape = held.shape
        self.copy = pltpu.make_async_copy(source, held, semaphore)
        self.copy.start()
        self.arrived = False

    def wait(self):
        if not self.arrived:
            self.copy.wait()
            self.arrived = True

    def __getitem__(self, index):
        self.wait()
        return self.held[index]


class Gathered:
    def __init__(self, sources, held, semaphores, places):
        self.held = held
        self.shape = held.shape
        self.copies = []
        for number, (source, place) in enumerate(zip(sources, places)):
            copy = pltpu.make_async_copy(source, held.at[place], semaphores.at[number])
            copy.start()
            self.copies.append(copy)

    def wait(self):
        for copy in self.copies:
            copy.wait()
        self.copies = []

    def __getitem__(self, index):
        self.wait()
        return self.held[index]


class PlanePair:
    def __init__(self, own, other, first=0, last=None):
        self.own, self.other = list(own), list(other)
        self.first, self.last = first, own[0].shape[1] if last is None else last

    def part(self, first, last):
        return PlanePair(self.own, self.other, first, last)


class Kept:
    def __init__(self, held, target, semaphore):
        self.held = held
        self.shape = held.shape
        self.copy = pltpu.make_async_copy(held, target, semaphore)
        self.sent = False

    def __setitem__(self, index, value):
        assert not self.sent
        self.held[index] = value

    def send(self):
        if not self.sent:
            self.copy.start()
            self.sent = True


def extent(shape, index):
    sizes = []
    for size, part in zip(shape, index):
        start, stop, _ = part.indices(size)
        sizes.append(stop - start)
    return tuple(sizes) + tuple(shape[len(index) :])


def bounded(ref, index):
    parts = []
    for size, part in zip(ref.shape, index):
        start, stop, _ = part.indices(size)
        parts.append(pl.ds(start, stop - start))
    return ref.at[tuple(parts)]


def run_rows(kernel, shapes, buffers, held, copies, *args, limit=64, after=(), cost=7):
    views = []
    for arg in args[1:]:
        if isinstance(arg, (list, PlanePair)):
            views.append((arg, None))
        else:
            views.append(arg if isinstance(arg, tuple) else (arg, ()))
    arrays = [args[0]]
    loaded_shapes, load_semaphores_of = [], []
    for source, index in views:
        if isinstance(source, PlanePair):
            arrays += source.own + source.other
            blocks = (8, source.own[0].shape[0], source.last - source.first)
            loaded_shapes.append(pltpu.VMEM(blocks, source.own[0].dtype))
            load_semaphores_of.append(8)
        elif index is None:
            arrays += source
            loaded_shapes.append(pltpu.VMEM((len(source),) + source[0].shape, source[0].dtype))
            load_semaphores_of.append(len(source))
        else:
            arrays.append(source)
            loaded_shapes.append(pltpu.VMEM(extent(source.shape, index), source.dtype))
            load_semaphores_of.append(1)
    loads = len(views)
    given_count = len(arrays)
    shapes = [jax.ShapeDtypeStruct(*one) for one in shapes]
    aliases = {}
    if buffers is not None:
        aliases = {len(arrays) + number: number for number in range(len(buffers))}
        arrays += list(buffers)
    arrays += list(after)
    inputs = len(arrays)

    def body(*refs):
        info, given = refs[0], refs[1:given_count]
        targets = refs[inputs : inputs + len(shapes)]
        rest = refs[inputs + len(shapes) :]
        load_semaphores = rest[loads]
        loaded, at, first = [], 0, 0
        for number in range(loads):
            argument, index = views[number]
            span = load_semaphores_of[number]
            semaphores = load_semaphores.at[pl.ds(first, span)]
            first += span
            if isinstance(argument, PlanePair):
                core = jnp.bitwise_and(info[1], 1)
                quarter = 2 * info[2] + jnp.right_shift(info[1], 1)
                columns = pl.ds(argument.first, argument.last - argument.first)
                sources = [one.at[:, columns] for one in given[at : at + span]]
                places = [2 * (quarter ^ number) + core for number in range(4)]
                places += [2 * (quarter ^ number) + 1 - core for number in range(4)]
                loaded.append(Gathered(sources, rest[number], semaphores, places))
                at += span
                continue
            if index is None:
                places = [info[1], info[1] ^ 2, info[1] ^ 1, info[1] ^ 3]
                loaded.append(Gathered(given[at : at + span], rest[number], semaphores, places))
                at += span
                continue
            source = given[at]
            if index:
                source = bounded(source, index)
            loaded.append(Loaded(source, rest[number], semaphores.at[0]))
            at += 1
        kernel(info, *loaded, *targets, *rest[loads + 1 :])
        for one in loaded:
            one.wait()

    anywhere = pl.BlockSpec(memory_space=pl.ANY)
    return pl.pallas_call(
        body,
        out_shape=shapes,
        in_specs=[pl.BlockSpec(memory_space=pltpu.SMEM)] + [anywhere] * (inputs - 1),
        out_specs=[anywhere] * len(shapes),
        scratch_shapes=loaded_shapes
        + [pltpu.SemaphoreType.DMA((sum(load_semaphores_of),))]
        + [pltpu.VMEM(shape, bf16) for shape in held]
        + [pltpu.SemaphoreType.DMA((copies,))],
        input_output_aliases=aliases,
        compiler_params=pltpu.CompilerParams(vmem_limit_bytes=limit << 20),
        cost_estimate=pl.CostEstimate(
            flops=cost * 10**9, bytes_accessed=cost * 3 * 10**6, transcendentals=0
        ),
    )(*arrays)


def run(kernel, outs, *args, scalars=1, limit=64, into=None, after=(), cost=7):
    views = [arg if isinstance(arg, tuple) else (arg, ()) for arg in args[scalars:]]
    arrays = list(args[:scalars]) + [array for array, _ in views]
    held = [pltpu.VMEM(extent(array.shape, index), array.dtype) for array, index in views]
    kept = [pltpu.VMEM(shape, dtype) for shape, dtype in outs]
    shapes = [jax.ShapeDtypeStruct(shape, dtype) for shape, dtype in outs]
    aliases = {}
    first_row = 0
    if into is not None:
        buffer, full, first_row = into
        shapes = [jax.ShapeDtypeStruct(full, outs[0][1])]
        if buffer is not None:
            aliases = {len(arrays): 0}
            arrays.append(buffer)
    single = len(shapes) == 1
    arrays += list(after)
    inputs, loads, results = len(arrays), len(views), len(outs)

    def body(*refs):
        given, targets = refs[:inputs], refs[inputs : inputs + results]
        rest = refs[inputs + results :]
        loaded_refs, kept_refs = rest[:loads], rest[loads : loads + results]
        load_semaphores, keep_semaphores = rest[loads + results :]
        order = sorted(range(loads), key=lambda number: held[number].shape and _size(held[number]))
        loaded = [None] * loads
        for number in order:
            source = given[scalars + number]
            index = views[number][1]
            if index:
                source = bounded(source, index)
            loaded[number] = Loaded(source, loaded_refs[number], load_semaphores.at[number])
        stored = []
        for number in range(results):
            target = targets[number]
            if into is not None:
                target = target.at[pl.ds(first_row, outs[0][0][0])]
            stored.append(Kept(kept_refs[number], target, keep_semaphores.at[number]))
        kernel(*given[:scalars], *loaded, *stored)
        for one in stored:
            one.send()
        for one in loaded:
            one.wait()
        for one in stored:
            one.copy.wait()

    anywhere = pl.BlockSpec(memory_space=pl.ANY)
    return pl.pallas_call(
        body,
        out_shape=shapes[0] if single else shapes,
        in_specs=[pl.BlockSpec(memory_space=pltpu.SMEM)] * scalars + [anywhere] * (inputs - scalars),
        out_specs=anywhere if single else [anywhere] * len(shapes),
        scratch_shapes=held
        + kept
        + [pltpu.SemaphoreType.DMA((max(loads, 1),)), pltpu.SemaphoreType.DMA((results,))],
        input_output_aliases=aliases,
        compiler_params=pltpu.CompilerParams(vmem_limit_bytes=limit << 20),
        cost_estimate=pl.CostEstimate(
            flops=cost * 10**9, bytes_accessed=cost * 3 * 10**6, transcendentals=0
        ),
    )(*arrays)


def following(arrays, others):
    def body(*refs):
        pass

    anywhere = pl.BlockSpec(memory_space=pl.ANY)
    return pl.pallas_call(
        body,
        out_shape=[jax.ShapeDtypeStruct(array.shape, array.dtype) for array in arrays],
        in_specs=[anywhere] * (len(arrays) + len(others)),
        out_specs=[anywhere] * len(arrays),
        input_output_aliases={number: number for number in range(len(arrays))},
    )(*arrays, *others)


def _size(ref):
    total = jnp.dtype(ref.dtype).itemsize
    for one in ref.shape:
        total *= one
    return total


def exchanged(payload):
    return lax.all_to_all(payload, everywhere, 0, 0, tiled=True)


def swapped(shard, wide_bits, narrow_bits):
    wide, narrow = lax.axis_size("wide"), lax.axis_size("narrow")
    if not wide_bits:
        return lax.ppermute(shard, "narrow", [(i, i ^ narrow_bits) for i in range(narrow)])
    if not narrow_bits:
        return lax.ppermute(shard, "wide", [(i, i ^ wide_bits) for i in range(wide)])
    pairs = [
        (w * narrow + n, (w ^ wide_bits) * narrow + (n ^ narrow_bits))
        for w in range(wide)
        for n in range(narrow)
    ]
    return lax.ppermute(shard, everywhere, pairs)


def handed(shard, by):
    peers = lax.axis_size("narrow")
    pairs = [(i, i + by) for i in range(peers) if 0 <= i + by < peers]
    return lax.ppermute(shard, "narrow", pairs)


def later_stages():
    peers = lax.axis_size("wide")
    steps, bit = [], 2
    while bit < peers:
        if 2 * bit < peers:
            steps.append((bit, 2 * bit, 3 * bit))
            bit *= 4
        else:
            steps.append((bit,))
            bit *= 2
    return steps


def merged_state(images, state):
    def combined(state, others, adders):
        return run(
            functools.partial(merge_states, images, adders),
            [(state.shape, f32)],
            state,
            *others,
            scalars=0,
        )

    state = combined(state, [swapped(state, 0, 1)], (1,))
    others = [swapped(state, 0, 2), swapped(state, 1, 0), swapped(state, 1, 2)]
    state = combined(state, others, (1,))
    stages = later_stages()
    for step in stages[:-1]:
        state = combined(state, [swapped(state, bits, 0) for bits in step], ())
    return [state] + [swapped(state, bits, 0) for bits in stages[-1]]


def wide_parts(sums):
    sums = sums + swapped(sums, 1, 0)
    stages = later_stages()
    for step in stages[:-1]:
        sums = sum([swapped(sums, bits, 0) for bits in step], sums)
    return [sums] + [swapped(sums, bits, 0) for bits in stages[-1]]


def swapped_once(shard, axis, bits, sender, only=None):
    peers = lax.axis_size(axis)
    pairs = [(i, i ^ bits) for i in range(peers) if bool(i & bits) == sender]
    if only is not None:
        pairs = [pair for pair in pairs if pair[1] in only]
    return lax.ppermute(shard, axis, pairs)


class Transfer:
    def __init__(self, band, info, arrays):
        self.band, self.info = band, info
        self.split = len(band.xs) == 2
        self.left, left_sent, self.right, right_sent = arrays
        self.left_came, self.right_came = swapped(left_sent, 0, 2), self.along_x(right_sent)

    def along_x(self, shard):
        return swapped(shard, 1, 0) if self.split else swapped_once(shard, "wide", 1, True)

    def second(self, after=()):
        band = self.band
        flat = ((len(band.lines), band.rows, band.half), bf16)
        outs = run(
            functools.partial(second_halves, band),
            [flat] * (4 if self.split else 3),
            self.info,
            self.left,
            self.left_came,
            self.right,
            self.right_came,
            after=after,
        )
        self.left, left_sent = outs[0], outs[1 if self.split else 0]
        self.right, right_sent = outs[-2], outs[-1]
        self.left_came, self.right_came = self.along_x(left_sent), swapped(right_sent, 0, 2)
        return (outs[0],)

    def third(self, after=()):
        band = self.band
        count = max(len(band.lines) // 2, 1)
        shape = ((count, band.rows, 2 * band.half), bf16)
        outs = run(
            functools.partial(line_halves, band),
            [shape] * min(len(band.lines), 2),
            self.info,
            self.left,
            self.left_came,
            self.right,
            self.right_came,
            after=after,
        )
        if len(band.lines) > 1:
            self.own, self.came = outs[0], swapped(outs[1], 2, 0)
        else:
            self.own, self.came = outs, swapped_once(outs, "wide", 2, True)
        return (self.own,)

    def fourth(self, after=()):
        band = self.band
        shape = ((band.rows, 2 * band.half), bf16)
        outs = run(
            functools.partial(line_sum, band),
            [shape] * (2 if len(band.lines) == 4 else 1),
            self.info,
            self.own,
            self.came,
            after=after,
        )
        if len(band.lines) == 4:
            self.own, self.came = outs[0], swapped(outs[1], 4, 0)
        else:
            only = [2 * line + x for line in band.lines for x in band.xs]
            self.own, self.came = outs, swapped_once(outs, "wide", 4, band.lines[0] < 2, only)
        return (self.own,)

    def result(self):
        return self.own.astype(f32) + self.came.astype(f32)


class PlaneTransfer:
    def __init__(self, info, kept, sent, upward):
        self.info, self.kept, self.upward = info, kept, upward
        self.came = swapped(sent, 2, 0)
        self.extra = ()

    def third(self, after=()):
        slots = self.kept.shape[0]
        shapes = [((4,) + self.kept.shape[1:], bf16)]
        if slots > 4:
            shapes.append((self.kept.shape[1:], bf16))
        outs = run(pair_sums, shapes, self.info, self.kept, self.came, after=after)
        if slots > 4:
            self.extra = (outs[1], swapped_once(outs[1], "wide", 4, self.upward, [2, 3]))
            outs = outs[0]
        self.kept, self.came = outs, swapped_once(outs, "wide", 4, not self.upward)
        return (outs,)

    def fourth(self, after=()):
        shapes = [(self.kept.shape[1:], bf16)] * 4
        outs = run(owner_sums, shapes, self.info, self.kept, self.came, *self.extra, after=after)
        self.parts = [outs[0], swapped(outs[1], 0, 2), swapped(outs[2], 1, 0), swapped(outs[3], 1, 2)]
        return (outs[0],)

    def result(self):
        quarter = 2 * self.info[2] + jnp.right_shift(self.info[1], 1)
        columns = [lax.select_n(quarter ^ number, *self.parts) for number in range(4)]
        return jnp.concatenate(columns, 1).astype(f32)


def swept(mine, info):
    low = info[1] < 2
    kept = jnp.where(low, mine[0], mine[1])
    came = swapped(jnp.where(low, mine[1], mine[0]), 0, 2)
    halves = [jnp.where(low, kept, came), jnp.where(low, came, kept)]
    return jnp.concatenate(halves, 1).astype(f32)


def scattered(rows, devices):
    done = lax.psum_scatter(rows, everywhere, scatter_dimension=0, tiled=True)
    return done.astype(f32).reshape(-1)


def on_device(
    images,
    first_reduce,
    first_spatial,
    first_expand,
    first_squeeze,
    first_excite,
    first_project,
    second_reduce,
    second_spatial,
    second_expand,
    second_squeeze,
    second_excite,
    norm_gains,
    norm_shifts,
    image_counts,
    out_grad,
):
    wide, narrow = lax.axis_size("wide"), lax.axis_size("narrow")
    assert narrow == 4
    devices = wide * narrow
    count, rows_in, cols_in, channels = images.shape
    rows, columns = rows_in // 2, cols_in // 2
    geometry = (count, rows, columns)
    plane = count * rows * columns
    edge = count * columns
    area = rows * columns * narrow
    last = narrow - 1
    mid = first_reduce.shape[1]
    out = first_expand.shape[1]
    chunks = mid // 128
    place = lax.axis_index("wide").astype(jnp.int32)
    info = jnp.stack(
        [
            image_counts[0],
            lax.axis_index("narrow").astype(jnp.int32),
            jnp.bitwise_and(place, 1),
            jnp.right_shift(place, 1),
            jnp.full((), narrow - 1, jnp.int32),
        ]
    )
    widths = [mid, mid, out, out, mid, mid, out]
    gains, shifts, at = [], [], 0
    for width in widths:
        part = (slice(0, 1), slice(at, at + width))
        gains.append((norm_gains[None], part))
        shifts.append((norm_shifts[None], part))
        at += width
    pair = ((devices, 2 * chunks, 128), f32)
    small = ((8, mid), f32)
    large = ((8, out), f32)
    edge_map = ((edge, mid), f32)
    taps = (9, mid, mid)
    spatial_one = first_spatial.reshape(taps)
    spatial_two = second_spatial.reshape(taps)
    bind = functools.partial

    planes, h1, pairs, edges = run(
        bind(reduce_first, geometry),
        [
            ((4 * plane, channels), bf16),
            ((4 * plane, mid), f32),
            ((devices, 2 * chunks + 8, 128), f32),
            ((2 * edge, mid), f32),
        ],
        info,
        images.reshape(4 * plane, channels),
        first_reduce,
    )
    halo = handed(edges, 1)
    pairs = exchanged(pairs)
    squeeze_rows = 2 * out * second_squeeze.shape[1] // mid
    first_rows = [0, channels, channels + 9 * mid]
    first_rows.append(first_rows[2] + out)
    first_rows.append(first_rows[3] + squeeze_rows)
    whole_rows = first_rows[4] + channels * out // mid
    second_rows = [0, out, out + 9 * mid, 2 * out + 9 * mid]
    second_shape = (second_rows[3] + squeeze_rows, mid)
    slice_rows = whole_rows // devices
    second_slice = second_shape[0] // devices
    by_hand = wide == 8 and slice_rows % 16 == 0 and second_slice % 16 == 0
    planes_other = swapped(planes, 0, 1)
    hp, moments_p = run(
        bind(project_first, geometry), [((plane, out), f32), large], info, planes, first_project
    )
    a1, h2, moments_1, counts, pairs, edges = run(
        bind(spatial_first, geometry),
        [
            ((plane, 4 * mid), bf16),
            ((plane, mid), f32),
            small,
            ((devices, 128), f32),
            pair,
            ((edge, mid), f32),
        ],
        info,
        h1,
        halo,
        pairs,
        gains[0],
        shifts[0],
        spatial_one,
    )
    h2_below = handed(edges, -1)
    pairs = exchanged(pairs)
    xs = (planes, (slice(0, plane),))
    a2, h3, moments_2, state, pack = run(
        bind(expand_packing, geometry, 2, True),
        [
            ((plane, mid), bf16),
            ((plane, out), f32),
            small,
            large,
            ((plane, 5 * mid + channels), bf16),
        ],
        info,
        a1,
        xs,
        h2,
        pairs,
        counts,
        gains[1],
        shifts[1],
        first_expand,
        moments_p,
        after=(h2_below,),
    )
    if by_hand:
        groups = [[first + number for number in range(8)] for first in range(0, devices, 8)]
        pack = lax.all_gather(pack, everywhere, axis_index_groups=groups)
        at = [0, 4 * mid, 4 * mid + channels, 5 * mid + channels]
        a1_plane, xs_plane, a2_plane = [
            (pack, (slice(0, 8), slice(0, plane), slice(at[number], at[number + 1])))
            for number in range(3)
        ]

    def spread(parts, after):
        came = [swapped(parts[1], 0, 2), swapped(parts[2], 1, 0), swapped(parts[3], 1, 2)]
        own = [parts[0], *following(came, after)]
        return PlanePair(own, [swapped(one, 0, 1) for one in own])

    states = merged_state(count, state)
    moments_3, gates_1, reduced_1, r1, o1, k1, pairs, firsts, lasts = run(
        bind(reduce_second, geometry, len(states), area),
        [
            large,
            ((3 * count, out), f32),
            ((2 * count, first_squeeze.shape[1]), f32),
            ((plane, out), f32),
            ((plane, out), bf16),
            ((plane, mid), f32),
            pair,
            edge_map,
            edge_map,
        ],
        info,
        h3,
        hp,
        gains[2],
        shifts[2],
        gains[3],
        shifts[3],
        first_squeeze,
        first_excite,
        second_reduce,
        *states,
        after=(planes_other,) if by_hand else (),
    )
    k1_above, k1_below = handed(lasts, 1), handed(firsts, -1)
    pairs = exchanged(pairs)
    a3, k2, moments_4, pairs, firsts, lasts = run(
        bind(spatial_second, geometry, last),
        [((plane, mid), bf16), ((plane, mid), f32), small, pair, edge_map, edge_map],
        info,
        k1,
        k1_above,
        k1_below,
        pairs,
        counts,
        gains[4],
        shifts[4],
        spatial_two,
    )
    k2_above, k2_below = handed(lasts, 1), handed(firsts, -1)
    pairs = exchanged(pairs)

    pack_widths = [out, mid, mid]
    a4, k3, moments_5, state, pack = run(
        bind(expand_packing, geometry, 2, False),
        [
            ((plane, mid), bf16),
            ((plane, out), f32),
            small,
            large,
            ((plane, sum(pack_widths)), bf16),
        ],
        info,
        o1,
        a3,
        k2,
        pairs,
        counts,
        gains[5],
        shifts[5],
        second_expand,
        after=(k2_above, k2_below),
    )
    pack = lax.all_gather(pack, "narrow")
    packed, at = [], 0
    for width in pack_widths:
        packed.append((pack, (slice(0, narrow), slice(0, plane), slice(at, at + width))))
        at += width
    o1_all, a3_all, a4_all = packed

    def gathered_halves(mine, theirs):
        came = swapped(theirs, 0, 2)
        return [mine, came, swapped(mine, 0, 1), swapped(came, 0, 1)]

    def joined(mine, theirs, width):
        low = info[1] < 2
        first, second = jnp.where(low, mine, theirs), jnp.where(low, theirs, mine)
        parts = [one.reshape(plane, -1, width // 2) for one in (first, second)]
        return jnp.concatenate(parts, 2).reshape(plane, -1)

    states = merged_state(count, state)
    if by_hand:
        units = first_squeeze.shape[1]
        pooled = gates_1[count : 2 * count]
        pooled = jnp.concatenate([pooled, swapped(pooled, 1, 0)], 0)
        pooled = pooled.reshape(2 * count, -1, out // units).transpose(2, 0, 1)
        reduced_other = swapped(reduced_1, 1, 0)
    moments_6, gates_2, reduced_2, mixed, dr2, state = run(
        bind(finish_second, geometry, len(states), area),
        [
            large,
            ((3 * count, out), f32),
            ((2 * count, second_squeeze.shape[1]), f32),
            ((plane, out), bf16),
            ((plane, out), f32),
            large,
        ],
        info,
        k3,
        o1,
        out_grad.reshape(plane, out),
        gains[6],
        shifts[6],
        second_squeeze,
        second_excite,
        *states,
        after=(a1_plane[0], pooled, reduced_other) if by_hand else (),
    )

    def excitation_back(state, has_others, number, gates, reduced, squeeze, excite):
        pooled = gates[count : 2 * count].reshape(count, -1, mid // squeeze.shape[1])
        pooled = pooled.transpose(2, 0, 1)
        sums, pooled_grad, gate_grad, reduced_grad = run(
            bind(excite_back, count, area, has_others),
            [
                ((4, out), f32),
                ((count, out), f32),
                ((count, out), f32),
                ((count, squeeze.shape[1]), f32),
            ],
            info,
            gains[number],
            shifts[number],
            gates,
            reduced,
            squeeze,
            excite,
            state,
            swapped(state, 0, 1),
            swapped(state, 0, 2),
            swapped(state, 0, 3),
            after=() if has_others else (pooled,),
        )
        return wide_parts(sums), pooled_grad, (pooled, reduced, gate_grad, reduced_grad)

    parts, pooled_grad, saved_two = excitation_back(
        state, False, 6, gates_2, reduced_2, second_squeeze, second_excite
    )
    half_out, half_mid = ((plane, out // 2), bf16), ((plane, mid // 2), bf16)
    back_outs = [((4, out), f32), half_out, half_out, ((plane, mid), f32), pair, edge_map, edge_map]
    sums_6, dk3_mine, dk3_theirs, du5, pairs, firsts, lasts = run(
        bind(expand_back, geometry, len(parts), mid),
        back_outs,
        info,
        dr2,
        k3,
        moments_6,
        gates_2,
        pooled_grad,
        gains[6],
        second_expand,
        k2,
        moments_5,
        gains[5],
        shifts[5],
        *parts,
    )
    du5_above, du5_below = handed(lasts, 1), handed(firsts, -1)
    pairs = exchanged(pairs)
    share = 1.0 / narrow
    if by_hand:
        second_shapes = [((wide, 2, second_slice, mid // 2), bf16)]
        second_sent = run_rows(
            bind(gate_slices, count, second_rows[3], second_slice),
            second_shapes,
            None,
            [(squeeze_rows, mid), (squeeze_rows, mid // 2)],
            16,
            info,
            *saved_two,
            cost=1,
        )
        tie = second_sent[:1]
    else:
        tie = ()
        second_flat = run(
            weight_rows,
            [((out, mid), bf16)],
            a4,
            joined(dk3_mine, dk3_theirs, mid),
            scalars=0,
            into=(None, second_shape, second_rows[2]),
        )
        second_flat = run(
            bind(gate_rows, count, share),
            [((squeeze_rows, mid), bf16)],
            *saved_two,
            scalars=0,
            into=(second_flat, second_shape, second_rows[3]),
        )
    sums_5, dk2_mine, dk2_theirs, du4, pairs = run(
        bind(spatial_second_back, geometry, last),
        [small, half_mid, half_mid, ((plane, mid), f32), pair],
        info,
        du5,
        du5_above,
        du5_below,
        k2,
        k2_above,
        k2_below,
        moments_5,
        gains[5],
        pairs,
        spatial_two,
        k1,
        moments_4,
        gains[4],
        shifts[4],
    )
    pairs = exchanged(pairs)
    if by_hand:
        second_sent = run_rows(
            bind(whole_rows_of, second_rows[2], second_slice),
            second_shapes,
            second_sent,
            [(out, mid // 2)],
            16,
            info,
            a4_all,
            gathered_halves(dk3_mine, dk3_theirs),
        )
        tie = second_sent
    else:
        tie = ()
    sums_4, dk1_mine, dk1_theirs, dr1, state = run(
        bind(reduce_second_back, geometry),
        [small, half_mid, half_mid, ((plane, out), f32), large],
        info,
        du4,
        k1,
        moments_4,
        gains[4],
        pairs,
        second_reduce,
        dr2,
        r1,
        h3,
        hp,
        moments_3,
        after=tuple(second_sent) if by_hand else (),
    )
    parts, pooled_grad, saved_one = excitation_back(
        state, True, 2, gates_1, reduced_1, first_squeeze, first_excite
    )
    if by_hand:
        second_sent = run_rows(
            bind(whole_spatial_rows, geometry, second_rows[1], second_slice),
            second_shapes,
            second_sent,
            [(9 * mid, mid // 2)],
            9 * 3,
            info,
            a3_all,
            gathered_halves(dk2_mine, dk2_theirs),
            after=(pooled_grad,),
        )
        tie = second_sent[:1]
    else:
        second_flat = run(
            bind(spatial_alone, geometry),
            [((9 * mid, mid), bf16)],
            info,
            a3,
            handed(a3, 1),
            handed(a3, -1),
            joined(dk2_mine, dk2_theirs, mid),
            into=(second_flat, second_shape, second_rows[1]),
        )
    if by_hand:
        second_sent = run_rows(
            bind(whole_rows_of, 0, second_slice),
            second_shapes,
            second_sent,
            [(out, mid // 2)],
            16,
            info,
            o1_all,
            gathered_halves(dk1_mine, dk1_theirs),
            after=parts[:1],
        )
        second_halves_summed = lax.psum_scatter(
            second_sent[0], "wide", scatter_dimension=0, tiled=False
        )
        tie = second_sent
    else:
        second_flat = run(
            weight_rows,
            [((out, mid), bf16)],
            o1,
            joined(dk1_mine, dk1_theirs, mid),
            scalars=0,
            into=(second_flat, second_shape, second_rows[0]),
        )
        second_done = scattered(second_flat, devices)
    sums_3, dh3, du2, pairs, firsts, _ = run(
        bind(expand_back, geometry, len(parts), 0),
        [((4, out), f32), ((plane, out), bf16), ((plane, mid), f32), pair, edge_map, edge_map],
        info,
        dr1,
        h3,
        moments_3,
        gates_1,
        pooled_grad,
        gains[2],
        first_expand,
        h2,
        moments_2,
        gains[1],
        shifts[1],
        *parts,
        after=tuple(second_sent) if by_hand else (),
    )
    du2_below = handed(firsts, -1)
    pairs = exchanged(pairs)
    dhp, image_part = run(
        bind(shortcut_back, geometry, len(parts)),
        [((plane, out), bf16), ((plane, channels), f32)],
        info,
        dr1,
        hp,
        moments_3,
        gains[3],
        first_project,
        *parts,
        after=(du2,),
    )
    if by_hand:
        pieces = out // mid
        wide_slice = slice_rows // pieces
        held_rows = -(-wide_slice // 16) * 16
        corner = Band(slice_rows, mid // 2, [0], [0])
        wide_rows = [one // pieces for one in first_rows[2:] + [whole_rows]]
        lowest = wide_rows[0] // wide_slice
        shared = wide_rows[0] - lowest * wide_slice
        skipped = -shared % 16
        assert channels <= 4 * slice_rows and lowest == devices // 2 - 2
        assert wide_slice + skipped <= held_rows
        tie = (image_part,)
    else:
        tie = ()
        first_shape = (whole_rows, mid)
        first_flat = run(
            weight_rows,
            [((out, mid), bf16)],
            a2,
            dh3,
            scalars=0,
            into=(None, first_shape, first_rows[2]),
        )
        first_flat = run(
            bind(gate_rows, count, share),
            [((squeeze_rows, mid), bf16)],
            *saved_one,
            scalars=0,
            into=(first_flat, first_shape, first_rows[3]),
        )
        first_flat = run(
            weight_rows,
            [((channels * out // mid, mid), bf16)],
            (planes, (slice(0, plane),)),
            dhp,
            scalars=0,
            into=(first_flat, first_shape, first_rows[4]),
        )
    sums_2, dh2, du1, pairs = run(
        bind(spatial_first_back, geometry, last),
        [small, ((plane, mid), bf16), ((4 * plane, mid), f32), pair],
        info,
        du2,
        du2_below,
        h2,
        h2_below,
        moments_2,
        gains[1],
        pairs,
        spatial_one,
        h1,
        moments_1,
        gains[0],
        shifts[0],
        after=tie,
    )
    pairs = exchanged(pairs)
    if by_hand:
        tie = ()
    else:
        first_flat = run(
            bind(first_alone, geometry),
            [((9 * mid, mid), bf16)],
            info,
            a1,
            handed(a1, 1),
            dh2,
            into=(first_flat, first_shape, first_rows[1]),
        )
    channel_row = ((1, norm_gains.shape[0]), f32)
    quarters = [((plane, out // 2 + mid // 4), bf16)] * 4 if by_hand else []
    *quarters, gain_grad, shift_grad, dh1, image_grad = run(
        bind(reduce_first_back, geometry),
        quarters
        + [channel_row, channel_row, ((4 * plane, mid), bf16), ((4 * plane, channels), bf16)],
        info,
        du1,
        h1,
        moments_1,
        gains[0],
        pairs,
        first_reduce,
        image_part,
        sums_2,
        sums_3,
        sums_4,
        sums_5,
        sums_6,
        *((dh3, dhp, dh2) if by_hand else ()),
        after=tie,
    )
    if by_hand:
        units = first_squeeze.shape[1]
        tie = (image_grad,)
        corner_sent = run_rows(
            bind(reduce_rows, corner),
            corner.shapes(),
            None,
            [(channels, mid)],
            16,
            info,
            planes,
            planes_other,
            dh1,
            swapped(dh1, 0, 1),
            after=tie,
            cost=7,
        )
        final = Transfer(corner, info, corner_sent)
        tie = (corner_sent[0],)
        lows_plane = spread(quarters, tie)
        slots = ((5, held_rows, out // 4), bf16)
        upper_sent = run_rows(
            bind(early_rows, wide_rows, wide_slice),
            [slots, slots],
            None,
            [(2 * units, out // 4), ((devices - lowest) // 2, held_rows, out // 4)],
            devices - lowest,
            info,
            a2_plane,
            xs_plane,
            lows_plane.part(0, out // 2),
            pooled,
            reduced_1,
            reduced_other,
            *saved_one[2:],
            swapped(saved_one[2], 1, 0),
            swapped(saved_one[3], 1, 0),
            after=tie,
            cost=7,
        )
        early = PlaneTransfer(info, *upper_sent, True)
        tie = (upper_sent[0],)
        slots = ((4, slice_rows, mid // 4), bf16)
        lower_sent = run_rows(
            bind(late_rows, geometry, first_rows[1], slice_rows),
            [slots, slots],
            None,
            [(9 * mid, mid // 4)],
            9 * 3 * 2,
            info,
            a1_plane,
            lows_plane.part(out // 2, out // 2 + mid // 4),
            after=tie,
            cost=7,
        )
        late = PlaneTransfer(info, *lower_sent, False)
        tie = (lower_sent[0],)
        tie = tie + (second_halves_summed,)
        second_done = swept(second_halves_summed, info)
        tie = final.second(tie)
        tie = early.third(tie)
        tie = final.third(tie)
        tie = late.third(tie)
        tie = final.fourth(tie)
        tie = early.fourth(tie)
        late.fourth(tie + (second_done, *early.parts[1:]))
        upper_done, lower_done, corner_done = early.result(), late.result(), final.result()
        piece = place * narrow + info[1]
        row = piece * slice_rows + lax.iota(jnp.int32, slice_rows)
        lower_done = jnp.where(row[:, None] < channels, corner_done, lower_done)
        mixed_rows = jnp.concatenate(
            [
                lower_done[: shared * pieces].reshape(shared, out),
                upper_done[shared + skipped : wide_slice + skipped],
            ],
            0,
        )
        first_done = jnp.where(
            piece < lowest,
            lower_done.reshape(-1),
            jnp.where(piece == lowest, mixed_rows, upper_done[:wide_slice]).reshape(-1),
        )
        second_done = second_done.reshape(-1)
    else:
        first_flat = run(
            weight_rows,
            [((channels, mid), bf16)],
            planes,
            dh1,
            scalars=0,
            into=(first_flat, first_shape, 0),
        )
        first_done = scattered(first_flat, devices)
    return (
        mixed.reshape(out_grad.shape),
        image_grad.reshape(images.shape),
        first_done,
        second_done,
        gain_grad.reshape(-1),
        shift_grad.reshape(-1),
    )


def solution(mesh):
    in_specs = (
        (P("wide", "narrow", None, None),) + (P(),) * 13 + (P("wide"), P("wide", "narrow", None, None))
    )
    out_specs = (
        P("wide", "narrow", None, None),
        P("wide", "narrow", None, None),
        P(everywhere),
        P(everywhere),
        P(),
        P(),
    )
    return jax.shard_map(
        on_device, mesh=mesh, in_specs=in_specs, out_specs=out_specs, check_vma=False
    )
```

```python
import functools

import jax
import jax.numpy as jnp
from jax import lax
from jax.experimental import pallas as pl
from jax.experimental.pallas import tpu as pltpu
from jax.sharding import PartitionSpec as P

epsilon = 1e-05
highest = lax.Precision.HIGHEST
f32 = jnp.float32
bf16 = jnp.bfloat16
everywhere = ("wide", "narrow")


def iota_rows(rows, columns=1):
    return lax.broadcasted_iota(jnp.int32, (rows, columns), 0)


def dot(left, right, left_dim=1, right_dim=0):
    return lax.dot_general(
        left, right, (((left_dim,), (right_dim,)), ((), ())), preferred_element_type=f32
    )


def exact_dot(values, weight, weight_dim=0):
    first = values.astype(bf16)
    rest = values - first.astype(f32)
    second = rest.astype(bf16)
    third = (rest - second.astype(f32)).astype(bf16)
    rows = values.shape[0]
    product = dot(
        jnp.concatenate([first.astype(f32), second.astype(f32), third.astype(f32)], 0).astype(bf16),
        weight,
        1,
        weight_dim,
    )
    return product[:rows] + product[rows : 2 * rows] + product[2 * rows : 3 * rows]


def slope(values):
    logistic = jax.nn.sigmoid(values)
    return logistic * (1.0 + values * (1.0 - logistic))


def silu(values):
    return values * jax.nn.sigmoid(values)


def total_of(values):
    return jnp.sum(values, axis=0, keepdims=True)


def mask_of(info, rows, plane, images):
    per_image = plane // images
    index = iota_rows(rows)
    if rows > plane:
        index = jnp.bitwise_and(index, plane - 1)
    return (index < info[0] * per_image).astype(f32)


def images_of(info, images):
    return jnp.minimum(info[0], images).astype(f32)


def local_moments(hidden, mask, pixels):
    summed = total_of(hidden * mask)
    centred = (hidden - summed / pixels) * mask
    return summed, total_of(centred * centred)


def put_pair(out, first, second):
    peers = out.shape[0]
    chunks = first.shape[1] // 128
    for number, row in enumerate((first, second)):
        for chunk in range(chunks):
            part = row[:, chunk * 128 : chunk * 128 + 128]
            out[:, number * chunks + chunk, :] = jnp.broadcast_to(part, (peers, 128))


def gathered_moments(pairs, counts, chunks):
    total = total_of(counts)
    averages, inverses = [], []
    for chunk in range(chunks):
        sums = pairs[:, chunk, :]
        spread = total_of(pairs[:, chunks + chunk, :])
        average = total_of(sums) / total
        spread = spread + total_of(counts * jnp.square(sums / counts - average))
        averages.append(average)
        inverses.append(lax.rsqrt(spread / total + epsilon))
    return jnp.concatenate(averages, 1), jnp.concatenate(inverses, 1), total[:, :1]


def gathered_sums(pairs, chunks):
    rows = [total_of(pairs[:, chunk, :]) for chunk in range(2 * chunks)]
    return jnp.concatenate(rows[:chunks], 1), jnp.concatenate(rows[chunks:], 1)


def merge(groups):
    total = sum(group[0] for group in groups)
    summed = sum(group[1] for group in groups)
    average = summed / total
    spread = sum(group[2] + group[0] * jnp.square(group[1] / group[0] - average) for group in groups)
    return total, summed, spread


def norm_back(upstream, normed, inverse, gain, total, shift_part, gain_part, mask):
    return mask * (gain * inverse) * (upstream - (shift_part + normed * gain_part) / total)


def shifted(values, by, columns):
    rows = values.shape[0]
    column = jnp.bitwise_and(iota_rows(rows), columns - 1)
    edge = 0 if by == 1 else columns - 1
    return jnp.where(column == edge, 0.0, pltpu.roll(values, by % rows, 0))


def put_halves(mine_out, theirs_out, values, width, info):
    first, second = [], []
    for start in range(0, values.shape[1], width):
        first.append(values[:, start : start + width // 2])
        second.append(values[:, start + width // 2 : start + width])
    first, second = jnp.concatenate(first, 1), jnp.concatenate(second, 1)
    low = jnp.right_shift(info[1], 1) == 0
    mine_out[...] = jnp.where(low, first, second).astype(bf16)
    theirs_out[...] = jnp.where(low, second, first).astype(bf16)
    mine_out.send()
    theirs_out.send()


def stack_rows(parts):
    return jnp.concatenate(parts, axis=0)


def plane_order(pixels, images, rows, columns):
    plane = images * rows * columns
    index = iota_rows(4 * plane, 4 * plane)
    other = lax.broadcasted_iota(jnp.int32, (4 * plane, 4 * plane), 1)
    parity = index // plane
    within = index - parity * plane
    line = within // columns
    column = within - line * columns
    natural = (line * 2 + parity // 2) * (2 * columns) + 2 * column + (parity & 1)
    return (other == natural).astype(bf16)


def reduce_first(geometry, info, x, weight, planes_out, hidden_out, pair_out, edge_out):
    images, rows, columns = geometry
    plane = images * rows * columns
    order = plane_order(4 * plane, images, rows, columns)
    planes = dot(order, x[...]).astype(bf16)
    planes_out[...] = planes
    planes_out.send()
    hidden = dot(planes, weight[...])
    hidden_out[...] = hidden
    hidden_out.send()
    mask = mask_of(info, 4 * plane, plane, images)
    pixels = images_of(info, images) * (4 * rows * columns)
    summed, spread = local_moments(hidden, mask, pixels)
    put_pair(pair_out, summed, spread)
    chunks = hidden.shape[1] // 128
    pair_out[:, 2 * chunks, :] = jnp.full((pair_out.shape[0], 128), pixels, f32)
    per_image = rows * columns
    edges = []
    for parity in range(2):
        for image in range(images):
            end = (2 + parity) * plane + (image + 1) * per_image
            edges.append(hidden[end - columns : end])
    edge_out[...] = stack_rows(edges)


def project_first(geometry, info, planes, weight, hidden_out, moments_out):
    images, rows, columns = geometry
    plane = images * rows * columns
    hidden = dot(planes[:plane], weight[...])
    hidden_out[...] = hidden
    hidden_out.send()
    mask = mask_of(info, plane, plane, images)
    pixels = images_of(info, images) * (rows * columns)
    summed, spread = local_moments(hidden, mask, pixels)
    moments_out[0:1] = summed
    moments_out[1:2] = spread
    moments_out[2:8] = jnp.zeros((6, hidden.shape[1]), f32)


def spatial_first(
    geometry,
    info,
    hidden,
    halo,
    pairs,
    gain,
    shift,
    weight,
    active_out,
    moved_out,
    moments_out,
    counts_out,
    pair_out,
    edge_out,
):
    images, rows, columns = geometry
    plane = images * rows * columns
    per_image = rows * columns
    width = hidden.shape[1]
    chunks = width // 128
    counts = pairs[:, 2 * chunks, :]
    counts_out[...] = counts
    average, inverse, total = gathered_moments(pairs, counts, chunks)
    moments_out[0:1] = average
    moments_out[1:2] = inverse
    moments_out[2:3] = jnp.broadcast_to(total, (1, width))
    moments_out[3:8] = jnp.zeros((5, width), f32)
    moments_out.send()
    counts_out.send()

    def active(values):
        return silu((values - average) * inverse * gain[...] + shift[...])

    inside = jnp.where(info[1] > 0, 1.0, 0.0)
    above = active(halo[...]) * inside
    planes = [active(hidden[number * plane : (number + 1) * plane]) for number in range(4)]

    for number in range(4):
        active_out[:, number * width : (number + 1) * width] = planes[number].astype(bf16)
    active_out.send()

    def lifted(parity):
        parts = []
        for image in range(images):
            at = (parity * images + image) * columns
            parts.append(above[at : at + columns])
            start = image * per_image
            parts.append(planes[2 + parity][start : start + per_image - columns])
        return stack_rows(parts)

    by_row = [(lifted(0), lifted(1)), (planes[0], planes[1]), (planes[2], planes[3])]
    moved = jnp.zeros((plane, width), f32)
    for tap_row in range(3):
        even, odd = by_row[tap_row]
        for tap_column, window in enumerate((shifted(odd, 1, columns), even, odd)):
            tap = 3 * tap_row + tap_column
            window = window.astype(bf16)
            moved = moved + dot(window, weight[tap])
    moved_out[...] = moved
    moved_out.send()
    mask = mask_of(info, plane, plane, images)
    pixels = images_of(info, images) * per_image
    put_pair(pair_out, *local_moments(moved, mask, pixels))
    edge_out[...] = stack_rows(
        [moved[image * per_image : image * per_image + columns] for image in range(images)]
    )


def expand(geometry, info, hidden, pairs, counts, gain, shift, weight, others, active_out, hidden_out, moments_out, state_out):
    images, rows, columns = geometry
    plane = images * rows * columns
    per_image = rows * columns
    width = hidden.shape[1]
    average, inverse, total = gathered_moments(pairs, counts[...] * (per_image / (4 * per_image)), width // 128)
    moments_out[0:1] = average
    moments_out[1:2] = inverse
    moments_out[2:3] = jnp.broadcast_to(total, (1, width))
    moments_out[3:8] = jnp.zeros((5, width), f32)
    moments_out.send()
    active = silu((hidden[...] - average) * inverse * gain[...] + shift[...]).astype(bf16)
    active_out[...] = active
    active_out.send()
    wide = dot(active, weight[...])
    hidden_out[...] = wide
    hidden_out.send()
    mask = mask_of(info, plane, plane, images)
    pixels = images_of(info, images) * per_image
    summed, spread = local_moments(wide, mask, pixels)
    for image in range(images):
        state_out[image : image + 1] = total_of(wide[image * per_image : (image + 1) * per_image])
    state_out[images : images + 1] = summed
    state_out[images + 1 : images + 2] = spread
    if others is None:
        state_out[images + 2 : images + 4] = jnp.zeros((2, wide.shape[1]), f32)
    else:
        state_out[images + 2 : images + 4] = others[0:2]
    state_out[images + 4 : images + 5] = jnp.full((1, wide.shape[1]), pixels, f32)
    if state_out.shape[0] > images + 5:
        state_out[images + 5 :] = jnp.zeros((state_out.shape[0] - images - 5, wide.shape[1]), f32)


def expand_packing(geometry, early, has_others, info, *refs):
    *refs, pack_out = refs
    maps, refs = refs[:early], list(refs[early:])
    others = refs.pop(6) if has_others else None
    expand(geometry, info, *refs[:6], others, *refs[6:])
    at = 0
    for one in (*maps, refs[6].held):
        part = one[...]
        pack_out[:, at : at + part.shape[1]] = part
        at += part.shape[1]


def groups_of(states, images, at):
    return [
        (state[images + 4 : images + 5], state[at : at + 1], state[at + 1 : at + 2]) for state in states
    ]


def merge_states(images, adders, *refs):
    *states, out = refs
    image_sums = states[0][0:images]
    for adder in adders:
        image_sums = image_sums + states[adder][0:images]
    out[0:images] = image_sums
    total, summed, spread = merge(groups_of(states, images, images))
    out[images : images + 1] = summed
    out[images + 1 : images + 2] = spread
    _, summed, spread = merge(groups_of(states, images, images + 2))
    out[images + 2 : images + 3] = summed
    out[images + 3 : images + 4] = spread
    out[images + 4 : images + 5] = total
    if out.shape[0] > images + 5:
        out[images + 5 :] = states[0][images + 5 :]


def excited(image_sums, area, average, inverse, gain, shift, squeeze, excite):
    image_means = (image_sums / area - average) * inverse
    pooled = image_means * gain + shift
    reduced = exact_dot(pooled, squeeze)
    squeezed = silu(reduced)
    gate = jax.nn.sigmoid(exact_dot(squeezed, excite))
    return image_means, pooled, reduced, squeezed, gate


def wide_spread(values, per_image):
    return stack_rows(
        [
            jnp.broadcast_to(values[image : image + 1], (per_image, values.shape[1]))
            for image in range(values.shape[0])
        ]
    )


def finish_state(states, images, at):
    total, summed, spread = merge(groups_of(states, images, at))
    average = summed / total
    return average, lax.rsqrt(spread / total + epsilon), total


def put_gates(gates_out, reduced_out, image_means, pooled, gate, reduced, squeezed):
    images = gate.shape[0]
    gates_out[0:images] = image_means
    gates_out[images : 2 * images] = pooled
    gates_out[2 * images : 3 * images] = gate
    reduced_out[0:images] = reduced
    reduced_out[images : 2 * images] = squeezed


def reduce_second(
    geometry,
    peers,
    area,
    info,
    hidden,
    shortcut,
    gain,
    shift,
    gain_p,
    shift_p,
    squeeze,
    excite,
    weight,
    *rest,
):
    images, rows, columns = geometry
    plane = images * rows * columns
    per_image = rows * columns
    states = rest[:peers]
    moments_out, gates_out, reduced_out, summed_out, block_out, moved_out, pair_out, first_out, last_out = rest[peers:]
    average, inverse, total = finish_state(states, images, images)
    average_p, inverse_p, _ = finish_state(states, images, images + 2)
    for row, value in enumerate((average, inverse, total, average_p, inverse_p)):
        moments_out[row : row + 1] = value
    moments_out[5:8] = jnp.zeros((3, average.shape[1]), f32)
    image_means, pooled, reduced, squeezed, gate = excited(
        states[0][0:images], area, average, inverse, gain[...], shift[...], squeeze[...], excite[...]
    )
    put_gates(gates_out, reduced_out, image_means, pooled, gate, reduced, squeezed)
    branch = (hidden[...] - average) * inverse * gain[...] + shift[...]
    summed = (
        branch * wide_spread(gate, per_image)
        + (shortcut[...] - average_p) * inverse_p * gain_p[...]
        + shift_p[...]
    )
    summed_out[...] = summed
    for one in (moments_out, gates_out, reduced_out, summed_out):
        one.send()
    block = silu(summed).astype(bf16)
    block_out[...] = block
    block_out.send()
    moved = dot(block, weight[...])
    moved_out[...] = moved
    moved_out.send()
    mask = mask_of(info, plane, plane, images)
    pixels = images_of(info, images) * per_image
    put_pair(pair_out, *local_moments(moved, mask, pixels))
    put_edges(first_out, last_out, moved, images, per_image, columns)


def put_edges(first_out, last_out, values, images, per_image, columns):
    first_out[...] = stack_rows(
        [values[image * per_image : image * per_image + columns] for image in range(images)]
    )
    last_out[...] = stack_rows(
        [values[(image + 1) * per_image - columns : (image + 1) * per_image] for image in range(images)]
    )


def extended(values, above, below, images, per_image, columns):
    parts = []
    for image in range(images):
        parts.append(above[image * columns : (image + 1) * columns])
        parts.append(values[image * per_image : (image + 1) * per_image])
        parts.append(below[image * columns : (image + 1) * columns])
    return stack_rows(parts)


def window_of(values, lift, images, per_image, columns):
    span = per_image + 2 * columns
    return stack_rows(
        [
            values[image * span + lift * columns : image * span + lift * columns + per_image]
            for image in range(images)
        ]
    )


def spatial_second(
    geometry,
    last,
    info,
    hidden,
    above,
    below,
    pairs,
    counts,
    gain,
    shift,
    weight,
    active_out,
    moved_out,
    moments_out,
    pair_out,
    first_out,
    last_out,
):
    images, rows, columns = geometry
    plane = images * rows * columns
    per_image = rows * columns
    width = hidden.shape[1]
    average, inverse, total = gathered_moments(pairs, counts[...] * 0.25, width // 128)
    moments_out[0:1] = average
    moments_out[1:2] = inverse
    moments_out[2:3] = jnp.broadcast_to(total, (1, width))
    moments_out[3:8] = jnp.zeros((5, width), f32)

    def active(values):
        return silu((values - average) * inverse * gain[...] + shift[...])

    top = active(above[...]) * jnp.where(info[1] > 0, 1.0, 0.0)
    bottom = active(below[...]) * jnp.where(info[1] < last, 1.0, 0.0)
    middle = active(hidden[...])
    active_out[...] = middle.astype(bf16)
    active_out.send()
    moments_out.send()
    middle = extended(middle, top, bottom, images, per_image, columns)
    by_column = (shifted(middle, 1, columns), middle, shifted(middle, -1, columns))
    moved = jnp.zeros((plane, width), f32)
    for tap_column in range(3):
        for tap_row in range(3):
            tap = 3 * tap_row + tap_column
            window = window_of(by_column[tap_column], tap_row, images, per_image, columns).astype(bf16)
            moved = moved + dot(window, weight[tap])
    moved_out[...] = moved
    moved_out.send()
    mask = mask_of(info, plane, plane, images)
    pixels = images_of(info, images) * per_image
    put_pair(pair_out, *local_moments(moved, mask, pixels))
    put_edges(first_out, last_out, moved, images, per_image, columns)


def finish_second(
    geometry,
    peers,
    area,
    info,
    hidden,
    block,
    out_grad,
    gain,
    shift,
    squeeze,
    excite,
    *rest,
):
    images, rows, columns = geometry
    plane = images * rows * columns
    per_image = rows * columns
    states = rest[:peers]
    moments_out, gates_out, reduced_out, mixed_out, grad_out, state_out = rest[peers:]
    average, inverse, total = finish_state(states, images, images)
    for row, value in enumerate((average, inverse, total)):
        moments_out[row : row + 1] = value
    moments_out[3:8] = jnp.zeros((5, average.shape[1]), f32)
    image_means, pooled, reduced, squeezed, gate = excited(
        states[0][0:images], area, average, inverse, gain[...], shift[...], squeeze[...], excite[...]
    )
    put_gates(gates_out, reduced_out, image_means, pooled, gate, reduced, squeezed)
    normed = (hidden[...] - average) * inverse
    summed = (normed * gain[...] + shift[...]) * wide_spread(gate, per_image) + block[...].astype(f32)
    mask = mask_of(info, plane, plane, images)
    logistic = jax.nn.sigmoid(summed)
    mixed_out[...] = (summed * logistic * mask).astype(bf16)
    for one in (moments_out, gates_out, reduced_out, mixed_out):
        one.send()
    grad = out_grad[...].astype(f32) * mask * (logistic * (1.0 + summed * (1.0 - logistic)))
    grad_out[...] = grad
    grad_out.send()
    put_image_sums(state_out, grad, normed, images, per_image)


def put_image_sums(state_out, grad, normed, images, per_image):
    crossed = grad * normed
    for image in range(images):
        part = slice(image * per_image, (image + 1) * per_image)
        state_out[image : image + 1] = total_of(grad[part])
        state_out[images + image : images + image + 1] = total_of(crossed[part])


def excite_back(
    images,
    area,
    has_others,
    info,
    gain,
    shift,
    gates,
    reduced,
    squeeze,
    excite,
    mine,
    core_other,
    y_other,
    both_other,
    sums_out,
    pooled_grad_out,
    gate_grad_out,
    reduced_grad_out,
):
    state = (mine[...] + core_other[...]) + (y_other[...] + both_other[...])
    plain = state[0:images]
    crossed = state[images : 2 * images]
    image_means = gates[0:images]
    gate = gates[2 * images : 3 * images]
    gate_grad = gain[...] * crossed + shift[...] * plain
    before_gate = gate_grad * gate * (1.0 - gate)
    squeezed_grad = exact_dot(before_gate, excite[...], 1)
    reduced_grad = squeezed_grad * slope(reduced[0:images])
    pooled_grad = exact_dot(reduced_grad, squeeze[...], 1)
    pooled_grad_out[...] = pooled_grad / area
    gate_grad_out[...] = before_gate
    reduced_grad_out[...] = reduced_grad
    mask = (iota_rows(images) < info[0]).astype(f32)
    sums_out[0:1] = total_of(mask * (plain * gate + pooled_grad))
    sums_out[1:2] = total_of(mask * (crossed * gate + pooled_grad * image_means))
    if has_others:
        sums_out[2:3] = total_of(mask * plain)
        sums_out[3:4] = state[2 * images : 2 * images + 1]


def expand_back(
    geometry,
    peers,
    cut,
    info,
    grad,
    hidden,
    moments,
    gates,
    pooled_grad,
    gain,
    weight,
    middle,
    middle_moments,
    middle_gain,
    middle_shift,
    *rest,
):
    images, rows, columns = geometry
    plane = images * rows * columns
    per_image = rows * columns
    sums = rest[0][...]
    for other in rest[1:peers]:
        sums = sums + other[...]
    sums_out, mine_out, *rest = rest[peers:]
    theirs_out = rest.pop(0) if cut else None
    middle_grad_out, pair_out, first_out, last_out = rest
    sums_out[...] = sums
    mask = mask_of(info, plane, plane, images)
    average, inverse, total = moments[0:1], moments[1:2], moments[2:3]
    normed = (hidden[...] - average) * inverse
    upstream = grad[...] * wide_spread(gates[2 * images : 3 * images], per_image) + wide_spread(
        pooled_grad[...], per_image
    )
    low = norm_back(upstream, normed, inverse, gain[...], total, sums[0:1], sums[1:2], mask)
    if cut:
        put_halves(mine_out, theirs_out, low, cut, info)
    low = low.astype(bf16)
    if not cut:
        mine_out[...] = low
        mine_out.send()
    average, inverse = middle_moments[0:1], middle_moments[1:2]
    normed = (middle[...] - average) * inverse
    middle_grad = dot(low, weight[...], 1, 1) * slope(normed * middle_gain[...] + middle_shift[...])
    middle_grad_out[...] = middle_grad
    middle_grad_out.send()
    masked = middle_grad * mask
    put_pair(pair_out, total_of(masked), total_of(masked * normed))
    put_edges(first_out, last_out, middle_grad, images, per_image, columns)


def spatial_second_back(
    geometry,
    last,
    info,
    grad,
    grad_above,
    grad_below,
    hidden,
    above,
    below,
    moments,
    gain,
    pairs,
    weight,
    earlier,
    earlier_moments,
    earlier_gain,
    earlier_shift,
    sums_out,
    mine_out,
    theirs_out,
    earlier_grad_out,
    pair_out,
):
    images, rows, columns = geometry
    plane = images * rows * columns
    per_image = rows * columns
    width = hidden.shape[1]
    shift_part, gain_part = gathered_sums(pairs, width // 128)
    sums_out[0:1] = shift_part
    sums_out[1:2] = gain_part
    sums_out[2:8] = jnp.zeros((6, width), f32)
    mask = mask_of(info, plane, plane, images)
    edge_mask = mask_of(info, images * columns, images * columns, images)
    average, inverse, total = moments[0:1], moments[1:2], moments[2:3]

    def lowered(upstream, values, rows_mask):
        normed = (values - average) * inverse
        return norm_back(upstream, normed, inverse, gain[...], total, shift_part, gain_part, rows_mask)

    middle = lowered(grad[...], hidden[...], mask)
    put_halves(mine_out, theirs_out, middle, width, info)
    top = lowered(grad_above[...], above[...], edge_mask * jnp.where(info[1] > 0, 1.0, 0.0))
    bottom = lowered(grad_below[...], below[...], edge_mask * jnp.where(info[1] < last, 1.0, 0.0))
    middle = extended(middle, top, bottom, images, per_image, columns)
    by_column = (shifted(middle, -1, columns), middle, shifted(middle, 1, columns))
    moved = jnp.zeros((plane, width), f32)
    for tap_column in range(3):
        for tap_row in range(3):
            window = window_of(by_column[tap_column], 2 - tap_row, images, per_image, columns)
            moved = moved + dot(window.astype(bf16), weight[3 * tap_row + tap_column], 1, 1)
    normed = (earlier[...] - earlier_moments[0:1]) * earlier_moments[1:2]
    earlier_grad = moved * slope(normed * earlier_gain[...] + earlier_shift[...])
    earlier_grad_out[...] = earlier_grad
    earlier_grad_out.send()
    masked = earlier_grad * mask
    put_pair(pair_out, total_of(masked), total_of(masked * normed))


def reduce_second_back(
    geometry,
    info,
    grad,
    hidden,
    moments,
    gain,
    pairs,
    weight,
    carried,
    summed,
    wide_hidden,
    shortcut,
    wide_moments,
    sums_out,
    mine_out,
    theirs_out,
    summed_grad_out,
    state_out,
):
    images, rows, columns = geometry
    plane = images * rows * columns
    per_image = rows * columns
    width = hidden.shape[1]
    shift_part, gain_part = gathered_sums(pairs, width // 128)
    sums_out[0:1] = shift_part
    sums_out[1:2] = gain_part
    sums_out[2:8] = jnp.zeros((6, width), f32)
    mask = mask_of(info, plane, plane, images)
    normed = (hidden[...] - moments[0:1]) * moments[1:2]
    low = norm_back(
        grad[...], normed, moments[1:2], gain[...], moments[2:3], shift_part, gain_part, mask
    )
    put_halves(mine_out, theirs_out, low, width, info)
    low = low.astype(bf16)
    summed_grad = (carried[...] + dot(low, weight[...], 1, 1)) * slope(summed[...])
    summed_grad_out[...] = summed_grad
    summed_grad_out.send()
    normed = (wide_hidden[...] - wide_moments[0:1]) * wide_moments[1:2]
    put_image_sums(state_out, summed_grad, normed, images, per_image)
    other = (shortcut[...] - wide_moments[3:4]) * wide_moments[4:5]
    state_out[2 * images : 2 * images + 1] = total_of(summed_grad * mask * other)
    rest = state_out.shape[0] - 2 * images - 1
    state_out[2 * images + 1 :] = jnp.zeros((rest, summed_grad.shape[1]), f32)


def put_quarters(outs, maps, info):
    quarter = 2 * info[2] + jnp.right_shift(info[1], 1)
    for number, out in enumerate(outs):
        at = 0
        for one in maps:
            width = one.shape[1] // 4
            first = pl.multiple_of((quarter ^ number) * width, width)
            out[:, at : at + width] = one[:, pl.ds(first, width)]
            at += width
        out.send()


def shortcut_back(geometry, peers, info, grad, shortcut, moments, gain, weight, *rest):
    images, rows, columns = geometry
    plane = images * rows * columns
    sums = rest[0][...]
    for other in rest[1:peers]:
        sums = sums + other[...]
    low_out, image_out = rest[peers:]
    mask = mask_of(info, plane, plane, images)
    normed = (shortcut[...] - moments[3:4]) * moments[4:5]
    low = norm_back(
        grad[...], normed, moments[4:5], gain[...], moments[2:3], sums[2:3], sums[3:4], mask
    )
    low = low.astype(bf16)
    low_out[...] = low
    low_out.send()
    image_out[...] = dot(low, weight[...], 1, 1)


def spatial_first_back(
    geometry,
    last,
    info,
    grad,
    grad_below,
    hidden,
    below,
    moments,
    gain,
    pairs,
    weight,
    earlier,
    earlier_moments,
    earlier_gain,
    earlier_shift,
    sums_out,
    low_out,
    earlier_grad_out,
    pair_out,
):
    images, rows, columns = geometry
    plane = images * rows * columns
    per_image = rows * columns
    width = hidden.shape[1]
    shift_part, gain_part = gathered_sums(pairs, width // 128)
    sums_out[0:1] = shift_part
    sums_out[1:2] = gain_part
    sums_out[2:8] = jnp.zeros((6, width), f32)
    mask = mask_of(info, plane, plane, images)
    edge_mask = mask_of(info, images * columns, images * columns, images)
    average, inverse, total = moments[0:1], moments[1:2], moments[2:3]

    def lowered(upstream, values, rows_mask):
        normed = (values - average) * inverse
        return norm_back(upstream, normed, inverse, gain[...], total, shift_part, gain_part, rows_mask)

    middle = lowered(grad[...], hidden[...], mask)
    bottom = lowered(grad_below[...], below[...], edge_mask * jnp.where(info[1] < last, 1.0, 0.0))
    parts = []
    for image in range(images):
        parts.append(middle[image * per_image + columns : (image + 1) * per_image])
        parts.append(bottom[image * columns : (image + 1) * columns])
    lower = stack_rows(parts)
    here = middle.astype(bf16)
    low_out[...] = here
    low_out.send()
    here_right = shifted(middle, -1, columns).astype(bf16)
    next_right = shifted(lower, -1, columns).astype(bf16)
    lower = lower.astype(bf16)

    def back(window, tap_row, tap_column):
        return dot(window, weight[3 * tap_row + tap_column], 1, 1)

    planes = [
        back(here, 1, 1),
        back(here, 1, 2) + back(here_right, 1, 0),
        back(here, 2, 1) + back(lower, 0, 1),
        back(here, 2, 2) + back(here_right, 2, 0) + back(lower, 0, 2) + back(next_right, 0, 0),
    ]
    shift_sum = jnp.zeros((1, width), f32)
    gain_sum = jnp.zeros((1, width), f32)
    for number in range(4):
        at = slice(number * plane, (number + 1) * plane)
        normed = (earlier[at] - earlier_moments[0:1]) * earlier_moments[1:2]
        earlier_grad = planes[number] * slope(normed * earlier_gain[...] + earlier_shift[...])
        earlier_grad_out[at] = earlier_grad
        masked = earlier_grad * mask
        shift_sum = shift_sum + total_of(masked)
        gain_sum = gain_sum + total_of(masked * normed)
    put_pair(pair_out, shift_sum, gain_sum)


def reduce_first_back(
    geometry,
    info,
    grad,
    hidden,
    moments,
    gain,
    pairs,
    weight,
    image_part,
    sums_2,
    sums_3,
    sums_4,
    sums_5,
    sums_6,
    *rest,
):
    *lows, gain_grad_out, shift_grad_out, low_out, image_out = rest
    if lows:
        maps, quarters_out = lows[:-4], lows[-4:]
        for one in maps:
            one.wait()
        put_quarters(quarters_out, maps, info)
    images, rows, columns = geometry
    plane = images * rows * columns
    width = hidden.shape[1]
    shift_part, gain_part = gathered_sums(pairs, width // 128)
    at = 0
    for shift_row, gain_row in (
        (shift_part, gain_part),
        (sums_2[0:1], sums_2[1:2]),
        (sums_3[0:1], sums_3[1:2]),
        (sums_3[2:3], sums_3[3:4]),
        (sums_4[0:1], sums_4[1:2]),
        (sums_5[0:1], sums_5[1:2]),
        (sums_6[0:1], sums_6[1:2]),
    ):
        shift_grad_out[:, at : at + shift_row.shape[1]] = shift_row
        gain_grad_out[:, at : at + shift_row.shape[1]] = gain_row
        at += shift_row.shape[1]
    mask = mask_of(info, 4 * plane, plane, images)
    normed = (hidden[...] - moments[0:1]) * moments[1:2]
    low = norm_back(
        grad[...], normed, moments[1:2], gain[...], moments[2:3], shift_part, gain_part, mask
    ).astype(bf16)
    low_out[...] = low
    low_out.send()
    gain_grad_out.send()
    shift_grad_out.send()
    image_grad = dot(low, weight[...], 1, 1)
    image_grad = stack_rows([image_grad[:plane] + image_part[...], image_grad[plane:]]).astype(bf16)
    order = plane_order(4 * plane, images, rows, columns)
    image_out[...] = dot(order, image_grad, 0, 0).astype(bf16)


def unit(size):
    rows = lax.broadcasted_iota(jnp.int32, (size, size), 0)
    columns = lax.broadcasted_iota(jnp.int32, (size, size), 1)
    return (rows == columns).astype(bf16)


def turned(values, one):
    return dot(one, values, 1, 1).astype(bf16)


def outer_rows(inner, outer, out, base=0):
    width = out.shape[1]
    pieces = outer.shape[1] // width
    count = inner.shape[1]
    if pieces == 1:
        step = min(512, count)
        one = unit(step)
        for start in range(0, count, step):
            part = turned(inner[:, start : start + step], one)
            out[base + start : base + start + step] = dot(part, outer).astype(bf16)
        return
    step = 512 // pieces
    row = lax.broadcasted_iota(jnp.int32, (step * pieces, step), 0)
    column = lax.broadcasted_iota(jnp.int32, (step * pieces, step), 1)
    spreads = [(row == column * pieces + piece).astype(bf16) for piece in range(pieces)]
    stacked = stack_rows([outer[:, piece * width : (piece + 1) * width] for piece in range(pieces)])
    for start in range(0, count, step):
        part = inner[:, start : start + step]
        widened = [dot(spread, part, 1, 1).astype(bf16) for spread in spreads]
        result = dot(jnp.concatenate(widened, 1), stacked)
        out[base + start * pieces : base + (start + step) * pieces] = result.astype(bf16)


def weight_rows(inner, outer, out):
    outer_rows(inner[...], outer[...], out)


def two_parts(values):
    first = values.astype(bf16).astype(f32)
    return first, values - first


def left_parts(values):
    first, second = two_parts(values)
    return stack_rows([first, second, first]).astype(bf16)


def right_parts(values):
    first, second = two_parts(values)
    return stack_rows([first, first, second]).astype(bf16)


def gate_rows(images, share, pooled, reduced, gate_grad, reduced_grad, out, base=0):
    width = out.shape[1]
    squeezed = reduced[images : 2 * images]
    right = right_parts(reduced_grad[...] * share)
    units = reduced_grad.shape[1]
    rows = pooled.shape[2]
    for piece in range(pooled.shape[0]):
        part = dot(left_parts(pooled[piece]), right, 0, 0)
        out[base : base + rows, piece * units : (piece + 1) * units] = part.astype(bf16)
    wide_pieces = gate_grad.shape[1] // width
    row = lax.broadcasted_iota(jnp.int32, (units, units * wide_pieces), 0)
    column = lax.broadcasted_iota(jnp.int32, (units, units * wide_pieces), 1)
    left = left_parts(squeezed)
    right = right_parts(gate_grad[...] * share)
    result = jnp.zeros((units * wide_pieces, width), f32)
    for piece in range(wide_pieces):
        widened = dot(left, (column == row * wide_pieces + piece).astype(bf16)).astype(bf16)
        result = result + dot(widened, right[:, piece * width : (piece + 1) * width], 0, 0)
    out[base + rows : base + rows + units * wide_pieces] = result.astype(bf16)


def spatial_alone(geometry, info, active, above, below, outer, out):
    images, rows, columns = geometry
    per_image = rows * columns
    width = active.shape[1]

    def edge(values, at):
        parts = [values[image * per_image + at : image * per_image + at + columns] for image in range(images)]
        return stack_rows(parts).astype(f32)

    top = edge(above, per_image - columns) * jnp.where(info[1] > 0, 1.0, 0.0)
    bottom = edge(below, 0) * jnp.where(info[1] < info[4], 1.0, 0.0)
    middle = extended(active[...].astype(f32), top, bottom, images, per_image, columns)
    by_column = (shifted(middle, 1, columns), middle, shifted(middle, -1, columns))
    one = unit(width)
    for tap in range(9):
        window = window_of(by_column[tap % 3], tap // 3, images, per_image, columns).astype(bf16)
        out[tap * width : (tap + 1) * width] = dot(turned(window, one), outer[...]).astype(bf16)


def first_alone(geometry, info, active, above, outer, out):
    images, rows, columns = geometry
    per_image = rows * columns
    width = active.shape[1] // 4
    inside = jnp.where(info[1] > 0, 1.0, 0.0)
    one = unit(width)
    for tap in range(9):
        tap_row, tap_column = tap // 3, tap % 3
        number = (0 if tap_row == 1 else 2) + (0 if tap_column == 1 else 1)
        at = slice(number * width, (number + 1) * width)
        window = active[:, at].astype(f32)
        if tap_row == 0:
            parts = []
            for image in range(images):
                start = image * per_image
                parts.append(above[start + per_image - columns : start + per_image, at].astype(f32) * inside)
                parts.append(window[start : start + per_image - columns])
            window = stack_rows(parts)
        if tap_column == 0:
            window = shifted(window, 1, columns)
        out[tap * width : (tap + 1) * width] = dot(turned(window.astype(bf16), one), outer[...]).astype(bf16)


class Band:
    def __init__(self, rows, half, lines, xs):
        self.rows, self.half, self.lines, self.xs = rows, half, lines, xs

    def shapes(self):
        lines = len(self.lines)
        left = ((lines, len(self.xs), self.rows, self.half), bf16)
        right = ((lines, 2, self.rows, self.half), bf16)
        return [left, left, right, right]


def spot_of(info):
    return info[2], jnp.right_shift(info[1], 1), jnp.bitwise_and(info[1], 1)


def send_piece(band, spot, piece, source, place, refs, semaphores, used):
    x, y, core = spot
    line, x_of, y_of, core_of = piece >> 3, (piece >> 2) & 1, (piece >> 1) & 1, piece & 1
    if line not in band.lines or x_of not in band.xs:
        return []
    slot = band.lines.index(line)
    copies = []
    for half in range(2):
        mine = (y == y_of) if half == 0 else (x == x_of)
        inner = band.xs.index(x_of) if half == 0 else y_of
        columns = pl.ds(band.half * half, band.half)
        for kept in (True, False):
            target = refs[2 * half + (0 if kept else 1)].at[slot, inner, place]
            copy = pltpu.make_async_copy(source.at[:, columns], target, semaphores.at[used[0]])
            used[0] += 1
            wanted = mine if kept else jnp.logical_not(mine)
            if core is not None:
                wanted = jnp.logical_and(core == core_of, wanted)
            copies.append((wanted, copy))
    return copies


def send_rows(band, spot, source, base, first, last, refs, semaphores, used):
    copies = []
    for piece in range(first // band.rows, (last - 1) // band.rows + 1):
        start = max(first, piece * band.rows)
        stop = min(last, (piece + 1) * band.rows)
        held = source.at[pl.ds(base + start - first, stop - start)]
        place = pl.ds(start - piece * band.rows, stop - start)
        copies += send_piece(band, spot, piece, held, place, refs, semaphores, used)
    return copies


def conduct(copies, action):
    for wanted, copy in copies:

        def act(copy=copy):
            getattr(copy, action)()

        pl.when(wanted)(act)


def paired(own, other):
    return stack_rows([own[...], other[...]])


def merged_rows(values):
    return values[...].reshape(-1, values.shape[-1])


def half_of(values, width, info):
    first, second = [], []
    for start in range(0, values.shape[1], width):
        first.append(values[:, start : start + width // 2])
        second.append(values[:, start + width // 2 : start + width])
    low = jnp.right_shift(info[1], 1) == 0
    return jnp.where(low, jnp.concatenate(first, 1), jnp.concatenate(second, 1))


def place_rows(slice_rows, core, source, first, last, target, semaphores, used):
    copies = []
    for piece in range(first // slice_rows, (last - 1) // slice_rows + 1):
        start = max(first, piece * slice_rows)
        stop = min(last, (piece + 1) * slice_rows)
        held = source.at[pl.ds(start - first, stop - start)]
        place = pl.ds(start - piece * slice_rows, stop - start)
        target_rows = target.at[piece >> 2, (piece >> 1) & 1, place]
        copies.append(
            (core == (piece & 1), pltpu.make_async_copy(held, target_rows, semaphores.at[used[0]]))
        )
        used[0] += 1
    return copies


def plane_rows(values):
    return values[...].reshape(-1, values.shape[-1])


def line_place(info, line):
    return jnp.bitwise_and(info[3], 1) == (line & 1)


def either_copy(stays, source, kept, sent, semaphores, used):
    copies = []
    for wanted, target in ((stays, kept), (jnp.logical_not(stays), sent)):
        copies.append((wanted, pltpu.make_async_copy(source, target, semaphores.at[used[0]])))
        used[0] += 1
    return copies


def early_rows(starts, slice_rows, info, *rest):
    (
        active,
        planes,
        lows,
        pooled,
        reduced,
        reduced_other,
        gate_grad,
        reduced_grad,
        gate_grad_other,
        reduced_grad_other,
        kept,
        sent,
        gate_held,
        slices_held,
        semaphores,
    ) = rest
    core = jnp.bitwise_and(info[1], 1)
    quarter = 2 * info[2] + jnp.right_shift(info[1], 1)
    rows, width = slices_held.shape[1:]
    units = reduced.shape[1]
    images = reduced.shape[0] // 2
    pooled.wait(), gate_grad.wait(), gate_grad_other.wait()
    right = right_parts(paired(reduced_grad, reduced_grad_other))
    share = pooled.shape[0] // 4
    for number in range(share):
        part = dot(left_parts(pooled[quarter * share + number]), right, 0, 0)
        gate_held[0:units, number * units : (number + 1) * units] = part.astype(bf16)
    columns = pl.ds(pl.multiple_of(quarter * width, width), width)
    gate_held[units : 2 * units] = dot(
        left_parts(stack_rows([reduced[images:], reduced_other[images:]])),
        right_parts(stack_rows([gate_grad[:, columns], gate_grad_other[:, columns]])),
        0,
        0,
    ).astype(bf16)
    lowest = starts[0] // slice_rows
    count = slices_held.shape[0]
    numbers = range(count)
    found = {number: [] for number in numbers}
    skipped = -(starts[0] - lowest * slice_rows) % 16

    def pick(first, last, channels):
        near = [
            number
            for number in numbers
            if (lowest + 2 * number + 2) * slice_rows > first
            and (lowest + 2 * number) * slice_rows - skipped < last
        ]
        row = lax.broadcasted_iota(jnp.int32, (rows, channels), 0)
        column = lax.broadcasted_iota(jnp.int32, (rows, channels), 1)
        chosen = []
        for number in near:
            begin = (lowest + 2 * number + core) * slice_rows - first
            limit = slice_rows
            if number == 0:
                moved = jnp.where(core == 0, skipped, 0)
                begin = begin - moved
                limit = limit + moved
            wanted = jnp.logical_and(column == row + begin, row < limit)
            chosen.append(wanted.astype(f32))
        return near, stack_rows(chosen).astype(bf16)

    def add(near, result):
        for at, number in enumerate(near):
            found[number].append(result[at * rows : (at + 1) * rows])

    near, chosen = pick(starts[1], starts[2], 2 * units)
    add(near, dot(chosen, gate_held[...]))
    for first, last, inner, at in ((starts[0], starts[1], active, 0), (starts[2], starts[3], planes, 1)):
        near, chosen = pick(first, last, inner.shape[-1])
        left = dot(chosen, plane_rows(inner), 1, 1).astype(bf16)
        outer = lows[:, :, at * width : (at + 1) * width].reshape(-1, width)
        add(near, dot(left, outer))
    used = [0]
    copies = []
    for number in numbers:
        slices_held[number] = sum(found[number][1:], found[number][0]).astype(bf16)
        piece = lowest + 2 * number
        line, spot = piece >> 3, (piece >> 1) & 3
        slot = spot if line >= 2 else 4
        added = either_copy(
            line_place(info, line), slices_held.at[number], kept.at[slot], sent.at[slot], semaphores, used
        )
        conduct(added, "start")
        copies += added
    conduct(copies, "wait")


def late_rows(geometry, start, slice_rows, info, active, low, kept, sent, held, semaphores):
    images, _, columns = geometry
    core = jnp.bitwise_and(info[1], 1)
    width = active.shape[-1] // 4
    span = active.shape[1] // images
    rim = jnp.zeros((columns, width), bf16)

    def whole_images(values, columns_of):
        return [
            [values[first + number, image * span : (image + 1) * span, columns_of] for number in range(4)]
            for first in range(0, active.shape[0], 4)
            for image in range(images)
        ]

    def plane_of(number):
        return whole_images(active, slice(number * width, (number + 1) * width))

    def level(image_list):
        return stack_rows([part for parts in image_list for part in parts])

    def lifted(values, height):
        parts = []
        for at in range(0, values.shape[0], height):
            parts += [rim, values[at : at + height - columns]]
        return stack_rows(parts)

    outer = level(whole_images(low, slice(0, low.shape[-1])))
    turned_low = turned(outer, unit(outer.shape[1]))
    one = unit(width)
    height = 4 * span
    by_row = []
    for parity in (1, 0, 1):
        even, odd = level(plane_of(2 * parity)), level(plane_of(2 * parity + 1))
        by_row.append((shifted(odd.astype(f32), 1, columns).astype(bf16), even, odd))
    by_row[0] = tuple(lifted(values, height) for values in by_row[0])
    used = [0]
    copies = []
    for tap in range(9):
        product = dot(turned_low, by_row[tap // 3][tap % 3]).astype(bf16)
        held[tap * width : (tap + 1) * width] = turned(product, one)
        first = start + tap * width
        last = first + width
        for piece in range(first // slice_rows, (last - 1) // slice_rows + 1):
            begin, stop = max(first, piece * slice_rows), min(last, (piece + 1) * slice_rows)
            line, spot = piece >> 3, (piece >> 1) & 3
            place = pl.ds(begin - piece * slice_rows, stop - begin)
            added = either_copy(
                line_place(info, line),
                held.at[pl.ds(begin - start, stop - begin)],
                kept.at[spot, place],
                sent.at[spot, place],
                semaphores,
                used,
            )
            added = [(jnp.logical_and(core == (piece & 1), wanted), copy) for wanted, copy in added]
            conduct(added, "start")
            copies += added
    conduct(copies, "wait")


def pair_sums(info, kept, came, *outs):
    outs[0][...] = (kept[0:4].astype(f32) + came[0:4].astype(f32)).astype(bf16)
    outs[0].send()
    if len(outs) == 2:
        outs[1][...] = (kept[4].astype(f32) + came[4].astype(f32)).astype(bf16)


def owner_sums(info, kept, came, *rest):
    *others, first, second, third, fourth = rest
    quarter = 2 * info[2] + jnp.right_shift(info[1], 1)
    kept.wait(), came.wait()
    for number, out in enumerate((first, second, third, fourth)):
        total = kept[quarter ^ number].astype(f32) + came[quarter ^ number].astype(f32)
        if others:
            lower = others[0][...].astype(f32) + others[1][...].astype(f32)
            total = jnp.where(info[3] >= 2, total, lower)
        out[...] = total.astype(bf16)
        out.send()


def gate_slices(images, start, slice_rows, info, pooled, reduced, gate_grad, reduced_grad, target, held, half_held, semaphores):
    core = jnp.bitwise_and(info[1], 1)
    gate_rows(images, 1.0, pooled, reduced, gate_grad, reduced_grad, held)
    half_held[...] = half_of(held[...].astype(f32), held.shape[1], info).astype(bf16)
    last = start + held.shape[0]
    copies = place_rows(slice_rows, core, half_held, start, last, target, semaphores, [0])
    conduct(copies, "start")
    conduct(copies, "wait")


def whole_rows_of(start, slice_rows, info, active, low, target, held, semaphores):
    core = jnp.bitwise_and(info[1], 1)
    outer_rows(merged_rows(active), merged_rows(low), held)
    last = start + held.shape[0]
    copies = place_rows(slice_rows, core, held, start, last, target, semaphores, [0])
    conduct(copies, "start")
    conduct(copies, "wait")


def image_rows(values, image, images):
    span = values.shape[1] // images
    return [values[number, image * span : (image + 1) * span] for number in range(values.shape[0])]


def whole_spatial_rows(geometry, start, slice_rows, info, active, low, target, held, semaphores):
    images, _, columns = geometry
    core = jnp.bitwise_and(info[1], 1)
    used = [0]
    copies = []
    width = active.shape[-1]
    rim = jnp.zeros((columns, width), f32)
    outer, maps = [], []
    for image in range(images):
        outer += image_rows(low, image, images)
        parts = [part.astype(f32) for part in image_rows(active, image, images)]
        maps.append(stack_rows([rim] + parts + [rim]))
    outer = stack_rows(outer)
    span = maps[0].shape[0]
    every = stack_rows(maps)
    by_column = (shifted(every, 1, columns), every, shifted(every, -1, columns))
    by_column = [part.astype(bf16) for part in by_column]
    one = unit(width)
    for tap in range(9):
        tap_row, tap_column = tap // 3, tap % 3
        window = stack_rows(
            [
                by_column[tap_column][
                    image * span + tap_row * columns : (image + 1) * span - (2 - tap_row) * columns
                ]
                for image in range(images)
            ]
        )
        held[tap * width : (tap + 1) * width] = dot(turned(window, one), outer).astype(bf16)
        first = start + tap * width
        added = place_rows(
            slice_rows,
            core,
            held.at[pl.ds(tap * width, width)],
            first,
            first + width,
            target,
            semaphores,
            used,
        )
        conduct(added, "start")
        copies.extend(added)
    conduct(copies, "wait")


def reduce_rows(band, info, planes, planes_other, low, low_other, *rest):
    *targets, held, semaphores = rest
    spot = spot_of(info)
    outer_rows(paired(planes, planes_other), paired(low, low_other), held)
    copies = send_rows(band, spot, held, 0, 0, held.shape[0], targets, semaphores, [0])
    conduct(copies, "start")
    conduct(copies, "wait")


def second_halves(band, info, left, left_came, right, right_came, *outs):
    x, y = info[2], jnp.right_shift(info[1], 1)

    def total(first, second, slot, inner):
        return first[slot, inner].astype(f32) + second[slot, inner].astype(f32)

    outs = list(outs)
    split = len(band.xs) == 2
    left_outs = [outs.pop(0) for _ in range(2 if split else 1)]
    right_outs = outs
    left.wait(), left_came.wait(), right.wait(), right_came.wait()
    for slot in range(len(band.lines)):
        if split:
            left_outs[0][slot] = total(left, left_came, slot, x).astype(bf16)
            left_outs[1][slot] = total(left, left_came, slot, 1 - x).astype(bf16)
        else:
            left_outs[0][slot] = total(left, left_came, slot, 0).astype(bf16)
        right_outs[0][slot] = total(right, right_came, slot, y).astype(bf16)
        right_outs[1][slot] = total(right, right_came, slot, 1 - y).astype(bf16)


def line_halves(band, info, left, left_came, right, right_came, *outs):
    low = jnp.bitwise_and(info[3], 1)
    half = band.half

    def put(out, at, slot):
        out[at, :, 0:half] = (left[slot].astype(f32) + left_came[slot].astype(f32)).astype(bf16)
        out[at, :, half:] = (right[slot].astype(f32) + right_came[slot].astype(f32)).astype(bf16)

    left.wait(), left_came.wait(), right.wait(), right_came.wait()
    if len(band.lines) == 1:
        put(outs[0], 0, 0)
        return
    for at in range(len(band.lines) // 2):
        put(outs[0], at, 2 * at + low)
        put(outs[1], at, 2 * at + 1 - low)


def line_sum(band, info, own, came, *outs):
    if len(band.lines) < 4:
        outs[0][...] = (own[0].astype(f32) + came[0].astype(f32)).astype(bf16)
        return
    top = jnp.right_shift(info[3], 1)
    own.wait(), came.wait()
    for out, slot in zip(outs, (top, 1 - top)):
        out[...] = (own[slot].astype(f32) + came[slot].astype(f32)).astype(bf16)


class Loaded:
    def __init__(self, source, held, semaphore):
        self.held = held
        self.shape = held.shape
        self.copy = pltpu.make_async_copy(source, held, semaphore)
        self.copy.start()
        self.arrived = False

    def wait(self):
        if not self.arrived:
            self.copy.wait()
            self.arrived = True

    def __getitem__(self, index):
        self.wait()
        return self.held[index]


class Gathered:
    def __init__(self, sources, held, semaphores, places):
        self.held = held
        self.shape = held.shape
        self.copies = []
        for number, (source, place) in enumerate(zip(sources, places)):
            copy = pltpu.make_async_copy(source, held.at[place], semaphores.at[number])
            copy.start()
            self.copies.append(copy)

    def wait(self):
        for copy in self.copies:
            copy.wait()
        self.copies = []

    def __getitem__(self, index):
        self.wait()
        return self.held[index]


class PlanePair:
    def __init__(self, own, other, first=0, last=None):
        self.own, self.other = list(own), list(other)
        self.first, self.last = first, own[0].shape[1] if last is None else last

    def part(self, first, last):
        return PlanePair(self.own, self.other, first, last)


class Kept:
    def __init__(self, held, target, semaphore):
        self.held = held
        self.shape = held.shape
        self.copy = pltpu.make_async_copy(held, target, semaphore)
        self.sent = False

    def __setitem__(self, index, value):
        assert not self.sent
        self.held[index] = value

    def send(self):
        if not self.sent:
            self.copy.start()
            self.sent = True


def extent(shape, index):
    sizes = []
    for size, part in zip(shape, index):
        start, stop, _ = part.indices(size)
        sizes.append(stop - start)
    return tuple(sizes) + tuple(shape[len(index) :])


def bounded(ref, index):
    parts = []
    for size, part in zip(ref.shape, index):
        start, stop, _ = part.indices(size)
        parts.append(pl.ds(start, stop - start))
    return ref.at[tuple(parts)]


def run_rows(kernel, shapes, buffers, held, copies, *args, limit=64, after=(), cost=7):
    views = []
    for arg in args[1:]:
        if isinstance(arg, (list, PlanePair)):
            views.append((arg, None))
        else:
            views.append(arg if isinstance(arg, tuple) else (arg, ()))
    arrays = [args[0]]
    loaded_shapes, load_semaphores_of = [], []
    for source, index in views:
        if isinstance(source, PlanePair):
            arrays += source.own + source.other
            blocks = (8, source.own[0].shape[0], source.last - source.first)
            loaded_shapes.append(pltpu.VMEM(blocks, source.own[0].dtype))
            load_semaphores_of.append(8)
        elif index is None:
            arrays += source
            loaded_shapes.append(pltpu.VMEM((len(source),) + source[0].shape, source[0].dtype))
            load_semaphores_of.append(len(source))
        else:
            arrays.append(source)
            loaded_shapes.append(pltpu.VMEM(extent(source.shape, index), source.dtype))
            load_semaphores_of.append(1)
    loads = len(views)
    given_count = len(arrays)
    shapes = [jax.ShapeDtypeStruct(*one) for one in shapes]
    aliases = {}
    if buffers is not None:
        aliases = {len(arrays) + number: number for number in range(len(buffers))}
        arrays += list(buffers)
    arrays += list(after)
    inputs = len(arrays)

    def body(*refs):
        info, given = refs[0], refs[1:given_count]
        targets = refs[inputs : inputs + len(shapes)]
        rest = refs[inputs + len(shapes) :]
        load_semaphores = rest[loads]
        loaded, at, first = [], 0, 0
        for number in range(loads):
            argument, index = views[number]
            span = load_semaphores_of[number]
            semaphores = load_semaphores.at[pl.ds(first, span)]
            first += span
            if isinstance(argument, PlanePair):
                core = jnp.bitwise_and(info[1], 1)
                quarter = 2 * info[2] + jnp.right_shift(info[1], 1)
                columns = pl.ds(argument.first, argument.last - argument.first)
                sources = [one.at[:, columns] for one in given[at : at + span]]
                places = [2 * (quarter ^ number) + core for number in range(4)]
                places += [2 * (quarter ^ number) + 1 - core for number in range(4)]
                loaded.append(Gathered(sources, rest[number], semaphores, places))
                at += span
                continue
            if index is None:
                places = [info[1], info[1] ^ 2, info[1] ^ 1, info[1] ^ 3]
                loaded.append(Gathered(given[at : at + span], rest[number], semaphores, places))
                at += span
                continue
            source = given[at]
            if index:
                source = bounded(source, index)
            loaded.append(Loaded(source, rest[number], semaphores.at[0]))
            at += 1
        kernel(info, *loaded, *targets, *rest[loads + 1 :])
        for one in loaded:
            one.wait()

    anywhere = pl.BlockSpec(memory_space=pl.ANY)
    return pl.pallas_call(
        body,
        out_shape=shapes,
        in_specs=[pl.BlockSpec(memory_space=pltpu.SMEM)] + [anywhere] * (inputs - 1),
        out_specs=[anywhere] * len(shapes),
        scratch_shapes=loaded_shapes
        + [pltpu.SemaphoreType.DMA((sum(load_semaphores_of),))]
        + [pltpu.VMEM(shape, bf16) for shape in held]
        + [pltpu.SemaphoreType.DMA((copies,))],
        input_output_aliases=aliases,
        compiler_params=pltpu.CompilerParams(vmem_limit_bytes=limit << 20),
        cost_estimate=pl.CostEstimate(
            flops=cost * 10**9, bytes_accessed=cost * 3 * 10**6, transcendentals=0
        ),
    )(*arrays)


def run(kernel, outs, *args, scalars=1, limit=64, into=None, after=(), cost=7):
    views = [arg if isinstance(arg, tuple) else (arg, ()) for arg in args[scalars:]]
    arrays = list(args[:scalars]) + [array for array, _ in views]
    held = [pltpu.VMEM(extent(array.shape, index), array.dtype) for array, index in views]
    kept = [pltpu.VMEM(shape, dtype) for shape, dtype in outs]
    shapes = [jax.ShapeDtypeStruct(shape, dtype) for shape, dtype in outs]
    aliases = {}
    first_row = 0
    if into is not None:
        buffer, full, first_row = into
        shapes = [jax.ShapeDtypeStruct(full, outs[0][1])]
        if buffer is not None:
            aliases = {len(arrays): 0}
            arrays.append(buffer)
    single = len(shapes) == 1
    arrays += list(after)
    inputs, loads, results = len(arrays), len(views), len(outs)

    def body(*refs):
        given, targets = refs[:inputs], refs[inputs : inputs + results]
        rest = refs[inputs + results :]
        loaded_refs, kept_refs = rest[:loads], rest[loads : loads + results]
        load_semaphores, keep_semaphores = rest[loads + results :]
        order = sorted(range(loads), key=lambda number: held[number].shape and _size(held[number]))
        loaded = [None] * loads
        for number in order:
            source = given[scalars + number]
            index = views[number][1]
            if index:
                source = bounded(source, index)
            loaded[number] = Loaded(source, loaded_refs[number], load_semaphores.at[number])
        stored = []
        for number in range(results):
            target = targets[number]
            if into is not None:
                target = target.at[pl.ds(first_row, outs[0][0][0])]
            stored.append(Kept(kept_refs[number], target, keep_semaphores.at[number]))
        kernel(*given[:scalars], *loaded, *stored)
        for one in stored:
            one.send()
        for one in loaded:
            one.wait()
        for one in stored:
            one.copy.wait()

    anywhere = pl.BlockSpec(memory_space=pl.ANY)
    return pl.pallas_call(
        body,
        out_shape=shapes[0] if single else shapes,
        in_specs=[pl.BlockSpec(memory_space=pltpu.SMEM)] * scalars + [anywhere] * (inputs - scalars),
        out_specs=anywhere if single else [anywhere] * len(shapes),
        scratch_shapes=held
        + kept
        + [pltpu.SemaphoreType.DMA((max(loads, 1),)), pltpu.SemaphoreType.DMA((results,))],
        input_output_aliases=aliases,
        compiler_params=pltpu.CompilerParams(vmem_limit_bytes=limit << 20),
        cost_estimate=pl.CostEstimate(
            flops=cost * 10**9, bytes_accessed=cost * 3 * 10**6, transcendentals=0
        ),
    )(*arrays)


def following(arrays, others):
    def body(*refs):
        pass

    anywhere = pl.BlockSpec(memory_space=pl.ANY)
    return pl.pallas_call(
        body,
        out_shape=[jax.ShapeDtypeStruct(array.shape, array.dtype) for array in arrays],
        in_specs=[anywhere] * (len(arrays) + len(others)),
        out_specs=[anywhere] * len(arrays),
        input_output_aliases={number: number for number in range(len(arrays))},
    )(*arrays, *others)


def _size(ref):
    total = jnp.dtype(ref.dtype).itemsize
    for one in ref.shape:
        total *= one
    return total


def exchanged(payload):
    return lax.all_to_all(payload, everywhere, 0, 0, tiled=True)


def swapped(shard, wide_bits, narrow_bits):
    wide, narrow = lax.axis_size("wide"), lax.axis_size("narrow")
    if not wide_bits:
        return lax.ppermute(shard, "narrow", [(i, i ^ narrow_bits) for i in range(narrow)])
    if not narrow_bits:
        return lax.ppermute(shard, "wide", [(i, i ^ wide_bits) for i in range(wide)])
    pairs = [
        (w * narrow + n, (w ^ wide_bits) * narrow + (n ^ narrow_bits))
        for w in range(wide)
        for n in range(narrow)
    ]
    return lax.ppermute(shard, everywhere, pairs)


def handed(shard, by):
    peers = lax.axis_size("narrow")
    pairs = [(i, i + by) for i in range(peers) if 0 <= i + by < peers]
    return lax.ppermute(shard, "narrow", pairs)


def later_stages():
    peers = lax.axis_size("wide")
    steps, bit = [], 2
    while bit < peers:
        if 2 * bit < peers:
            steps.append((bit, 2 * bit, 3 * bit))
            bit *= 4
        else:
            steps.append((bit,))
            bit *= 2
    return steps


def merged_state(images, state):
    def combined(state, others, adders):
        return run(
            functools.partial(merge_states, images, adders),
            [(state.shape, f32)],
            state,
            *others,
            scalars=0,
        )

    state = combined(state, [swapped(state, 0, 1)], (1,))
    others = [swapped(state, 0, 2), swapped(state, 1, 0), swapped(state, 1, 2)]
    state = combined(state, others, (1,))
    stages = later_stages()
    for step in stages[:-1]:
        state = combined(state, [swapped(state, bits, 0) for bits in step], ())
    return [state] + [swapped(state, bits, 0) for bits in stages[-1]]


def wide_parts(sums):
    sums = sums + swapped(sums, 1, 0)
    stages = later_stages()
    for step in stages[:-1]:
        sums = sum([swapped(sums, bits, 0) for bits in step], sums)
    return [sums] + [swapped(sums, bits, 0) for bits in stages[-1]]


def swapped_once(shard, axis, bits, sender, only=None):
    peers = lax.axis_size(axis)
    pairs = [(i, i ^ bits) for i in range(peers) if bool(i & bits) == sender]
    if only is not None:
        pairs = [pair for pair in pairs if pair[1] in only]
    return lax.ppermute(shard, axis, pairs)


class Transfer:
    def __init__(self, band, info, arrays):
        self.band, self.info = band, info
        self.split = len(band.xs) == 2
        self.left, left_sent, self.right, right_sent = arrays
        self.left_came, self.right_came = swapped(left_sent, 0, 2), self.along_x(right_sent)

    def along_x(self, shard):
        return swapped(shard, 1, 0) if self.split else swapped_once(shard, "wide", 1, True)

    def second(self, after=()):
        band = self.band
        flat = ((len(band.lines), band.rows, band.half), bf16)
        outs = run(
            functools.partial(second_halves, band),
            [flat] * (4 if self.split else 3),
            self.info,
            self.left,
            self.left_came,
            self.right,
            self.right_came,
            after=after,
        )
        self.left, left_sent = outs[0], outs[1 if self.split else 0]
        self.right, right_sent = outs[-2], outs[-1]
        self.left_came, self.right_came = self.along_x(left_sent), swapped(right_sent, 0, 2)
        return (outs[0],)

    def third(self, after=()):
        band = self.band
        count = max(len(band.lines) // 2, 1)
        shape = ((count, band.rows, 2 * band.half), bf16)
        outs = run(
            functools.partial(line_halves, band),
            [shape] * min(len(band.lines), 2),
            self.info,
            self.left,
            self.left_came,
            self.right,
            self.right_came,
            after=after,
        )
        if len(band.lines) > 1:
            self.own, self.came = outs[0], swapped(outs[1], 2, 0)
        else:
            self.own, self.came = outs, swapped_once(outs, "wide", 2, True)
        return (self.own,)

    def fourth(self, after=()):
        band = self.band
        shape = ((band.rows, 2 * band.half), bf16)
        outs = run(
            functools.partial(line_sum, band),
            [shape] * (2 if len(band.lines) == 4 else 1),
            self.info,
            self.own,
            self.came,
            after=after,
        )
        if len(band.lines) == 4:
            self.own, self.came = outs[0], swapped(outs[1], 4, 0)
        else:
            only = [2 * line + x for line in band.lines for x in band.xs]
            self.own, self.came = outs, swapped_once(outs, "wide", 4, band.lines[0] < 2, only)
        return (self.own,)

    def result(self):
        return self.own.astype(f32) + self.came.astype(f32)


class PlaneTransfer:
    def __init__(self, info, kept, sent, upward):
        self.info, self.kept, self.upward = info, kept, upward
        self.came = swapped(sent, 2, 0)
        self.extra = ()

    def third(self, after=()):
        slots = self.kept.shape[0]
        shapes = [((4,) + self.kept.shape[1:], bf16)]
        if slots > 4:
            shapes.append((self.kept.shape[1:], bf16))
        outs = run(pair_sums, shapes, self.info, self.kept, self.came, after=after)
        if slots > 4:
            self.extra = (outs[1], swapped_once(outs[1], "wide", 4, self.upward, [2, 3]))
            outs = outs[0]
        self.kept, self.came = outs, swapped_once(outs, "wide", 4, not self.upward)
        return (outs,)

    def fourth(self, after=()):
        shapes = [(self.kept.shape[1:], bf16)] * 4
        outs = run(owner_sums, shapes, self.info, self.kept, self.came, *self.extra, after=after)
        self.parts = [outs[0], swapped(outs[1], 0, 2), swapped(outs[2], 1, 0), swapped(outs[3], 1, 2)]
        return (outs[0],)

    def result(self):
        quarter = 2 * self.info[2] + jnp.right_shift(self.info[1], 1)
        columns = [lax.select_n(quarter ^ number, *self.parts) for number in range(4)]
        return jnp.concatenate(columns, 1).astype(f32)


def swept(mine, info):
    low = info[1] < 2
    kept = jnp.where(low, mine[0], mine[1])
    came = swapped(jnp.where(low, mine[1], mine[0]), 0, 2)
    halves = [jnp.where(low, kept, came), jnp.where(low, came, kept)]
    return jnp.concatenate(halves, 1).astype(f32)


def scattered(rows, devices):
    done = lax.psum_scatter(rows, everywhere, scatter_dimension=0, tiled=True)
    return done.astype(f32).reshape(-1)


def on_device(
    images,
    first_reduce,
    first_spatial,
    first_expand,
    first_squeeze,
    first_excite,
    first_project,
    second_reduce,
    second_spatial,
    second_expand,
    second_squeeze,
    second_excite,
    norm_gains,
    norm_shifts,
    image_counts,
    out_grad,
):
    wide, narrow = lax.axis_size("wide"), lax.axis_size("narrow")
    assert narrow == 4
    devices = wide * narrow
    count, rows_in, cols_in, channels = images.shape
    rows, columns = rows_in // 2, cols_in // 2
    geometry = (count, rows, columns)
    plane = count * rows * columns
    edge = count * columns
    area = rows * columns * narrow
    last = narrow - 1
    mid = first_reduce.shape[1]
    out = first_expand.shape[1]
    chunks = mid // 128
    place = lax.axis_index("wide").astype(jnp.int32)
    info = jnp.stack(
        [
            image_counts[0],
            lax.axis_index("narrow").astype(jnp.int32),
            jnp.bitwise_and(place, 1),
            jnp.right_shift(place, 1),
            jnp.full((), narrow - 1, jnp.int32),
        ]
    )
    widths = [mid, mid, out, out, mid, mid, out]
    gains, shifts, at = [], [], 0
    for width in widths:
        part = (slice(0, 1), slice(at, at + width))
        gains.append((norm_gains[None], part))
        shifts.append((norm_shifts[None], part))
        at += width
    pair = ((devices, 2 * chunks, 128), f32)
    small = ((8, mid), f32)
    large = ((8, out), f32)
    edge_map = ((edge, mid), f32)
    taps = (9, mid, mid)
    spatial_one = first_spatial.reshape(taps)
    spatial_two = second_spatial.reshape(taps)
    bind = functools.partial

    planes, h1, pairs, edges = run(
        bind(reduce_first, geometry),
        [
            ((4 * plane, channels), bf16),
            ((4 * plane, mid), f32),
            ((devices, 2 * chunks + 8, 128), f32),
            ((2 * edge, mid), f32),
        ],
        info,
        images.reshape(4 * plane, channels),
        first_reduce,
    )
    halo = handed(edges, 1)
    pairs = exchanged(pairs)
    squeeze_rows = 2 * out * second_squeeze.shape[1] // mid
    first_rows = [0, channels, channels + 9 * mid]
    first_rows.append(first_rows[2] + out)
    first_rows.append(first_rows[3] + squeeze_rows)
    whole_rows = first_rows[4] + channels * out // mid
    second_rows = [0, out, out + 9 * mid, 2 * out + 9 * mid]
    second_shape = (second_rows[3] + squeeze_rows, mid)
    slice_rows = whole_rows // devices
    second_slice = second_shape[0] // devices
    by_hand = wide == 8 and slice_rows % 16 == 0 and second_slice % 16 == 0
    planes_other = swapped(planes, 0, 1)
    hp, moments_p = run(
        bind(project_first, geometry), [((plane, out), f32), large], info, planes, first_project
    )
    a1, h2, moments_1, counts, pairs, edges = run(
        bind(spatial_first, geometry),
        [
            ((plane, 4 * mid), bf16),
            ((plane, mid), f32),
            small,
            ((devices, 128), f32),
            pair,
            ((edge, mid), f32),
        ],
        info,
        h1,
        halo,
        pairs,
        gains[0],
        shifts[0],
        spatial_one,
    )
    h2_below = handed(edges, -1)
    pairs = exchanged(pairs)
    xs = (planes, (slice(0, plane),))
    a2, h3, moments_2, state, pack = run(
        bind(expand_packing, geometry, 2, True),
        [
            ((plane, mid), bf16),
            ((plane, out), f32),
            small,
            large,
            ((plane, 5 * mid + channels), bf16),
        ],
        info,
        a1,
        xs,
        h2,
        pairs,
        counts,
        gains[1],
        shifts[1],
        first_expand,
        moments_p,
        after=(h2_below,),
    )
    if by_hand:
        groups = [[first + number for number in range(8)] for first in range(0, devices, 8)]
        pack = lax.all_gather(pack, everywhere, axis_index_groups=groups)
        at = [0, 4 * mid, 4 * mid + channels, 5 * mid + channels]
        a1_plane, xs_plane, a2_plane = [
            (pack, (slice(0, 8), slice(0, plane), slice(at[number], at[number + 1])))
            for number in range(3)
        ]

    def spread(parts, after):
        came = [swapped(parts[1], 0, 2), swapped(parts[2], 1, 0), swapped(parts[3], 1, 2)]
        own = [parts[0], *following(came, after)]
        return PlanePair(own, [swapped(one, 0, 1) for one in own])

    states = merged_state(count, state)
    moments_3, gates_1, reduced_1, r1, o1, k1, pairs, firsts, lasts = run(
        bind(reduce_second, geometry, len(states), area),
        [
            large,
            ((3 * count, out), f32),
            ((2 * count, first_squeeze.shape[1]), f32),
            ((plane, out), f32),
            ((plane, out), bf16),
            ((plane, mid), f32),
            pair,
            edge_map,
            edge_map,
        ],
        info,
        h3,
        hp,
        gains[2],
        shifts[2],
        gains[3],
        shifts[3],
        first_squeeze,
        first_excite,
        second_reduce,
        *states,
        after=(planes_other,) if by_hand else (),
    )
    k1_above, k1_below = handed(lasts, 1), handed(firsts, -1)
    pairs = exchanged(pairs)
    a3, k2, moments_4, pairs, firsts, lasts = run(
        bind(spatial_second, geometry, last),
        [((plane, mid), bf16), ((plane, mid), f32), small, pair, edge_map, edge_map],
        info,
        k1,
        k1_above,
        k1_below,
        pairs,
        counts,
        gains[4],
        shifts[4],
        spatial_two,
    )
    k2_above, k2_below = handed(lasts, 1), handed(firsts, -1)
    pairs = exchanged(pairs)

    pack_widths = [out, mid, mid]
    a4, k3, moments_5, state, pack = run(
        bind(expand_packing, geometry, 2, False),
        [
            ((plane, mid), bf16),
            ((plane, out), f32),
            small,
            large,
            ((plane, sum(pack_widths)), bf16),
        ],
        info,
        o1,
        a3,
        k2,
        pairs,
        counts,
        gains[5],
        shifts[5],
        second_expand,
        after=(k2_above, k2_below),
    )
    pack = lax.all_gather(pack, "narrow")
    packed, at = [], 0
    for width in pack_widths:
        packed.append((pack, (slice(0, narrow), slice(0, plane), slice(at, at + width))))
        at += width
    o1_all, a3_all, a4_all = packed

    def gathered_halves(mine, theirs):
        came = swapped(theirs, 0, 2)
        return [mine, came, swapped(mine, 0, 1), swapped(came, 0, 1)]

    def joined(mine, theirs, width):
        low = info[1] < 2
        first, second = jnp.where(low, mine, theirs), jnp.where(low, theirs, mine)
        parts = [one.reshape(plane, -1, width // 2) for one in (first, second)]
        return jnp.concatenate(parts, 2).reshape(plane, -1)

    states = merged_state(count, state)
    if by_hand:
        units = first_squeeze.shape[1]
        pooled = gates_1[count : 2 * count]
        pooled = jnp.concatenate([pooled, swapped(pooled, 1, 0)], 0)
        pooled = pooled.reshape(2 * count, -1, out // units).transpose(2, 0, 1)
        reduced_other = swapped(reduced_1, 1, 0)
    moments_6, gates_2, reduced_2, mixed, dr2, state = run(
        bind(finish_second, geometry, len(states), area),
        [
            large,
            ((3 * count, out), f32),
            ((2 * count, second_squeeze.shape[1]), f32),
            ((plane, out), bf16),
            ((plane, out), f32),
            ((2 * count, out), f32),
        ],
        info,
        k3,
        o1,
        out_grad.reshape(plane, out),
        gains[6],
        shifts[6],
        second_squeeze,
        second_excite,
        *states,
        after=(a1_plane[0], pooled, reduced_other) if by_hand else (),
    )

    def excitation_back(state, has_others, number, gates, reduced, squeeze, excite):
        pooled = gates[count : 2 * count].reshape(count, -1, mid // squeeze.shape[1])
        pooled = pooled.transpose(2, 0, 1)
        sums, pooled_grad, gate_grad, reduced_grad = run(
            bind(excite_back, count, area, has_others),
            [
                ((4 if has_others else 2, out), f32),
                ((count, out), f32),
                ((count, out), f32),
                ((count, squeeze.shape[1]), f32),
            ],
            info,
            gains[number],
            shifts[number],
            gates,
            reduced,
            squeeze,
            excite,
            state,
            swapped(state, 0, 1),
            swapped(state, 0, 2),
            swapped(state, 0, 3),
            after=() if has_others else (pooled,),
        )
        return wide_parts(sums), pooled_grad, (pooled, reduced, gate_grad, reduced_grad)

    parts, pooled_grad, saved_two = excitation_back(
        state, False, 6, gates_2, reduced_2, second_squeeze, second_excite
    )
    half_out, half_mid = ((plane, out // 2), bf16), ((plane, mid // 2), bf16)
    back_outs = [((2, out), f32), half_out, half_out, ((plane, mid), f32), pair, edge_map, edge_map]
    sums_6, dk3_mine, dk3_theirs, du5, pairs, firsts, lasts = run(
        bind(expand_back, geometry, len(parts), mid),
        back_outs,
        info,
        dr2,
        k3,
        moments_6,
        gates_2,
        pooled_grad,
        gains[6],
        second_expand,
        k2,
        moments_5,
        gains[5],
        shifts[5],
        *parts,
    )
    du5_above, du5_below = handed(lasts, 1), handed(firsts, -1)
    pairs = exchanged(pairs)
    share = 1.0 / narrow
    if by_hand:
        second_shapes = [((wide, 2, second_slice, mid // 2), bf16)]
        second_sent = run_rows(
            bind(gate_slices, count, second_rows[3], second_slice),
            second_shapes,
            None,
            [(squeeze_rows, mid), (squeeze_rows, mid // 2)],
            16,
            info,
            *saved_two,
            cost=1,
        )
        tie = second_sent[:1]
    else:
        tie = ()
        second_flat = run(
            weight_rows,
            [((out, mid), bf16)],
            a4,
            joined(dk3_mine, dk3_theirs, mid),
            scalars=0,
            into=(None, second_shape, second_rows[2]),
        )
        second_flat = run(
            bind(gate_rows, count, share),
            [((squeeze_rows, mid), bf16)],
            *saved_two,
            scalars=0,
            into=(second_flat, second_shape, second_rows[3]),
        )
    sums_5, dk2_mine, dk2_theirs, du4, pairs = run(
        bind(spatial_second_back, geometry, last),
        [small, half_mid, half_mid, ((plane, mid), f32), pair],
        info,
        du5,
        du5_above,
        du5_below,
        k2,
        k2_above,
        k2_below,
        moments_5,
        gains[5],
        pairs,
        spatial_two,
        k1,
        moments_4,
        gains[4],
        shifts[4],
    )
    pairs = exchanged(pairs)
    if by_hand:
        second_sent = run_rows(
            bind(whole_rows_of, second_rows[2], second_slice),
            second_shapes,
            second_sent,
            [(out, mid // 2)],
            16,
            info,
            a4_all,
            gathered_halves(dk3_mine, dk3_theirs),
        )
        tie = second_sent
    else:
        tie = ()
    sums_4, dk1_mine, dk1_theirs, dr1, state = run(
        bind(reduce_second_back, geometry),
        [small, half_mid, half_mid, ((plane, out), f32), large],
        info,
        du4,
        k1,
        moments_4,
        gains[4],
        pairs,
        second_reduce,
        dr2,
        r1,
        h3,
        hp,
        moments_3,
        after=tuple(second_sent) if by_hand else (),
    )
    parts, pooled_grad, saved_one = excitation_back(
        state, True, 2, gates_1, reduced_1, first_squeeze, first_excite
    )
    if by_hand:
        second_sent = run_rows(
            bind(whole_spatial_rows, geometry, second_rows[1], second_slice),
            second_shapes,
            second_sent,
            [(9 * mid, mid // 2)],
            9 * 3,
            info,
            a3_all,
            gathered_halves(dk2_mine, dk2_theirs),
            after=(pooled_grad,),
        )
        tie = second_sent[:1]
    else:
        second_flat = run(
            bind(spatial_alone, geometry),
            [((9 * mid, mid), bf16)],
            info,
            a3,
            handed(a3, 1),
            handed(a3, -1),
            joined(dk2_mine, dk2_theirs, mid),
            into=(second_flat, second_shape, second_rows[1]),
        )
    if by_hand:
        second_sent = run_rows(
            bind(whole_rows_of, 0, second_slice),
            second_shapes,
            second_sent,
            [(out, mid // 2)],
            16,
            info,
            o1_all,
            gathered_halves(dk1_mine, dk1_theirs),
            after=parts[:1],
        )
        second_halves_summed = lax.psum_scatter(
            second_sent[0], "wide", scatter_dimension=0, tiled=False
        )
        tie = second_sent
    else:
        second_flat = run(
            weight_rows,
            [((out, mid), bf16)],
            o1,
            joined(dk1_mine, dk1_theirs, mid),
            scalars=0,
            into=(second_flat, second_shape, second_rows[0]),
        )
        second_done = scattered(second_flat, devices)
    sums_3, dh3, du2, pairs, firsts, _ = run(
        bind(expand_back, geometry, len(parts), 0),
        [((4, out), f32), ((plane, out), bf16), ((plane, mid), f32), pair, edge_map, edge_map],
        info,
        dr1,
        h3,
        moments_3,
        gates_1,
        pooled_grad,
        gains[2],
        first_expand,
        h2,
        moments_2,
        gains[1],
        shifts[1],
        *parts,
        after=tuple(second_sent) if by_hand else (),
    )
    du2_below = handed(firsts, -1)
    pairs = exchanged(pairs)
    dhp, image_part = run(
        bind(shortcut_back, geometry, len(parts)),
        [((plane, out), bf16), ((plane, channels), f32)],
        info,
        dr1,
        hp,
        moments_3,
        gains[3],
        first_project,
        *parts,
        after=(du2,),
    )
    if by_hand:
        pieces = out // mid
        wide_slice = slice_rows // pieces
        held_rows = -(-wide_slice // 16) * 16
        corner = Band(slice_rows, mid // 2, [0], [0])
        wide_rows = [one // pieces for one in first_rows[2:] + [whole_rows]]
        lowest = wide_rows[0] // wide_slice
        shared = wide_rows[0] - lowest * wide_slice
        skipped = -shared % 16
        assert channels <= 4 * slice_rows and lowest == devices // 2 - 2
        assert wide_slice + skipped <= held_rows
        tie = (image_part,)
    else:
        tie = ()
        first_shape = (whole_rows, mid)
        first_flat = run(
            weight_rows,
            [((out, mid), bf16)],
            a2,
            dh3,
            scalars=0,
            into=(None, first_shape, first_rows[2]),
        )
        first_flat = run(
            bind(gate_rows, count, share),
            [((squeeze_rows, mid), bf16)],
            *saved_one,
            scalars=0,
            into=(first_flat, first_shape, first_rows[3]),
        )
        first_flat = run(
            weight_rows,
            [((channels * out // mid, mid), bf16)],
            (planes, (slice(0, plane),)),
            dhp,
            scalars=0,
            into=(first_flat, first_shape, first_rows[4]),
        )
    sums_2, dh2, du1, pairs = run(
        bind(spatial_first_back, geometry, last),
        [small, ((plane, mid), bf16), ((4 * plane, mid), f32), pair],
        info,
        du2,
        du2_below,
        h2,
        h2_below,
        moments_2,
        gains[1],
        pairs,
        spatial_one,
        h1,
        moments_1,
        gains[0],
        shifts[0],
        after=tie,
    )
    pairs = exchanged(pairs)
    if by_hand:
        tie = ()
    else:
        first_flat = run(
            bind(first_alone, geometry),
            [((9 * mid, mid), bf16)],
            info,
            a1,
            handed(a1, 1),
            dh2,
            into=(first_flat, first_shape, first_rows[1]),
        )
    channel_row = ((1, norm_gains.shape[0]), f32)
    quarters = [((plane, out // 2 + mid // 4), bf16)] * 4 if by_hand else []
    *quarters, gain_grad, shift_grad, dh1, image_grad = run(
        bind(reduce_first_back, geometry),
        quarters
        + [channel_row, channel_row, ((4 * plane, mid), bf16), ((4 * plane, channels), bf16)],
        info,
        du1,
        h1,
        moments_1,
        gains[0],
        pairs,
        first_reduce,
        image_part,
        sums_2,
        sums_3,
        sums_4,
        sums_5,
        sums_6,
        *((dh3, dhp, dh2) if by_hand else ()),
        after=tie,
    )
    if by_hand:
        units = first_squeeze.shape[1]
        tie = (image_grad,)
        corner_sent = run_rows(
            bind(reduce_rows, corner),
            corner.shapes(),
            None,
            [(channels, mid)],
            16,
            info,
            planes,
            planes_other,
            dh1,
            swapped(dh1, 0, 1),
            after=tie,
            cost=7,
        )
        final = Transfer(corner, info, corner_sent)
        tie = (corner_sent[0],)
        lows_plane = spread(quarters, tie)
        slots = ((5, held_rows, out // 4), bf16)
        upper_sent = run_rows(
            bind(early_rows, wide_rows, wide_slice),
            [slots, slots],
            None,
            [(2 * units, out // 4), ((devices - lowest) // 2, held_rows, out // 4)],
            devices - lowest,
            info,
            a2_plane,
            xs_plane,
            lows_plane.part(0, out // 2),
            pooled,
            reduced_1,
            reduced_other,
            *saved_one[2:],
            swapped(saved_one[2], 1, 0),
            swapped(saved_one[3], 1, 0),
            after=tie,
            cost=7,
        )
        early = PlaneTransfer(info, *upper_sent, True)
        tie = (upper_sent[0],)
        slots = ((4, slice_rows, mid // 4), bf16)
        lower_sent = run_rows(
            bind(late_rows, geometry, first_rows[1], slice_rows),
            [slots, slots],
            None,
            [(9 * mid, mid // 4)],
            9 * 3 * 2,
            info,
            a1_plane,
            lows_plane.part(out // 2, out // 2 + mid // 4),
            after=tie,
            cost=7,
        )
        late = PlaneTransfer(info, *lower_sent, False)
        tie = (lower_sent[0],)
        tie = tie + (second_halves_summed,)
        second_done = swept(second_halves_summed, info)
        tie = final.second(tie)
        tie = early.third(tie)
        tie = final.third(tie)
        tie = late.third(tie)
        tie = final.fourth(tie)
        tie = early.fourth(tie)
        late.fourth(tie + (second_done, *early.parts[1:]))
        upper_done, lower_done, corner_done = early.result(), late.result(), final.result()
        piece = place * narrow + info[1]
        row = piece * slice_rows + lax.iota(jnp.int32, slice_rows)
        lower_done = jnp.where(row[:, None] < channels, corner_done, lower_done)
        mixed_rows = jnp.concatenate(
            [
                lower_done[: shared * pieces].reshape(shared, out),
                upper_done[shared + skipped : wide_slice + skipped],
            ],
            0,
        )
        first_done = jnp.where(
            piece < lowest,
            lower_done.reshape(-1),
            jnp.where(piece == lowest, mixed_rows, upper_done[:wide_slice]).reshape(-1),
        )
        second_done = second_done.reshape(-1)
    else:
        first_flat = run(
            weight_rows,
            [((channels, mid), bf16)],
            planes,
            dh1,
            scalars=0,
            into=(first_flat, first_shape, 0),
        )
        first_done = scattered(first_flat, devices)
    return (
        mixed.reshape(out_grad.shape),
        image_grad.reshape(images.shape),
        first_done,
        second_done,
        gain_grad.reshape(-1),
        shift_grad.reshape(-1),
    )


def solution(mesh):
    in_specs = (
        (P("wide", "narrow", None, None),) + (P(),) * 13 + (P("wide"), P("wide", "narrow", None, None))
    )
    out_specs = (
        P("wide", "narrow", None, None),
        P("wide", "narrow", None, None),
        P(everywhere),
        P(everywhere),
        P(),
        P(),
    )
    return jax.shard_map(
        on_device, mesh=mesh, in_specs=in_specs, out_specs=out_specs, check_vma=False
    )
```
